32 devices in a mesh: dp: 8 (over y, x, core), side: 4 (over z).
Axes of the slice: x: 2, y: 2, z: 4, core: 2. Of those that a mesh axis runs over, the one named last changes fastest.
Arguments:
- hidden_in: bfloat16 [32, 512, 768], P(('dp', 'side')), may hold values from -6 to 6
- side_state: bfloat16 [32, 512, 96], P(('dp', 'side')), may hold values from -6 to 6
- lengths: int32 [32], P('dp'), may hold values from 16 to 512, as said below
- assign: int32 [32], P('dp'), may hold values from 0 to 3, as said below
- buckets: int32 [1023], replicated, may hold values from 0 to 31
- backbone_gain_attn: float32 [768], replicated, may hold values from 0.25 to 1.75
- backbone_query: bfloat16 [768, 768], replicated, may hold values from -0.109375 to 0.109375
- backbone_key: bfloat16 [768, 768], replicated, may hold values from -0.109375 to 0.109375
- backbone_value: bfloat16 [768, 768], replicated, may hold values from -0.21875 to 0.21875
- backbone_project: bfloat16 [768, 768], replicated, may hold values from -1.25 to 1.25
- backbone_rel: float32 [32, 12], replicated, may hold values from -4 to 4
- backbone_gain_ff: float32 [768], replicated, may hold values from 0.25 to 1.75
- backbone_ff_in: bfloat16 [768, 3072], replicated, may hold values from -0.21875 to 0.21875
- backbone_ff_out: bfloat16 [3072, 768], replicated, may hold values from -0.15625 to 0.15625
- down_weight: bfloat16 [768, 96], replicated, may hold values from -0.21875 to 0.21875
- gate_logit: float32 [96], replicated, may hold values from -6 to 6
- side_gain_attn: float32 [96], replicated, may hold values from 0.25 to 1.75
- side_query: bfloat16 [96, 96], replicated, may hold values from -0.4375 to 0.4375
- side_key: bfloat16 [96, 96], replicated, may hold values from -0.4375 to 0.4375
- side_value: bfloat16 [96, 96], replicated, may hold values from -0.625 to 0.625
- side_project: bfloat16 [96, 96], replicated, may hold values from -3.5 to 3.5
- side_rel: float32 [32, 12], replicated, may hold values from -4 to 4
- side_gain_ff: float32 [96], replicated, may hold values from 0.25 to 1.75
- side_ff_in: bfloat16 [96, 384], replicated, may hold values from -0.625 to 0.625
- side_ff_out: bfloat16 [384, 96], replicated, may hold values from -0.4375 to 0.4375
- cotangent: bfloat16 [32, 512, 96], P(('dp', 'side')), may hold values from -6 to 6
Outputs:
- side_out: bfloat16 [32, 512, 96], P(('dp', 'side'))
- grad_state: float32 [32, 512, 96], P(('dp', 'side'))
- grad_down: float32 [768, 96], replicated
- grad_gate: float32 [96], replicated
- grad_gain_attn: float32 [96], replicated
- grad_query: float32 [96, 96], replicated
- grad_key: float32 [96, 96], replicated
- grad_value: float32 [96, 96], replicated
- grad_project: float32 [96, 96], replicated
- grad_rel: float32 [32, 12], replicated
- grad_gain_ff: float32 [96], replicated
- grad_ff_in: float32 [96, 384], replicated
- grad_ff_out: float32 [384, 96], replicated
The draws below stay inside these ranges and needn't reach their ends.
Inputs may be any that keep to these rules, and one draw needn't show every extreme that they name: `lengths`: each sequence has at least 16 real tokens; one sequence has exactly 512. Within each group of 4 sequences of one index of dp, assign is a permutation of the group's sequences (numbered in side order, the side device of sequence n being n). Every backbone device of the group holds at most 1 sequence of any one side device, and exactly 1 of some.
All inputs are finite; a program needn't handle non-finite values.
Results may differ from the reference program's by a relative error of at most 0.028.
Values may be sent and summed in bfloat16 or wider, within the bound.
No kernel may reach another device: no remote copies, remote signals or barrier semaphores. Data moves between devices by JAX's collectives and lax.ppermute only.
A program may use at most 192 MiB of HBM per device.

```python
import jax
import jax.numpy as jnp
from jax import lax

D = 768
H = 12
HD = 64
FF = 3072
NB = 32
DS = 96
SH = 12
SHD = 8
FS = 384
L = 512
ROWS_DEV = 1
GROUP_ROWS = 4
ROWS = 32


def draw_lengths(key, part):
    key_one, key_two, key_three, key_four = jax.random.split(key, 4)
    first_part = jax.random.randint(key_one, (ROWS,), 1, L + 1)
    second_part = jax.random.randint(key_two, (ROWS,), 1, L + 1)
    device_factor = jnp.repeat(jax.random.randint(key_three, (ROWS // ROWS_DEV,), 1, 5), ROWS_DEV)
    spread_out = first_part * second_part // L * device_factor // 2
    bounded = jnp.clip(spread_out, 16, L)
    longest = jax.random.randint(key_four, (), 0, ROWS)
    return jnp.where(jnp.arange(ROWS) == longest, L, bounded).astype(jnp.int32)


def draw_assign(key, part):
    side_count = GROUP_ROWS // ROWS_DEV
    group_count = ROWS // GROUP_ROWS
    key_one, key_two = jax.random.split(key)
    offsets = jax.vmap(lambda single: jax.random.permutation(single, side_count))(jax.random.split(key_one, group_count))
    orders = jax.vmap(lambda single: jax.random.permutation(single, ROWS_DEV))(jax.random.split(key_two, group_count * side_count))
    orders = orders.reshape(group_count, side_count, ROWS_DEV)
    sources = jnp.arange(side_count)[None, :, None]
    slot_index = jnp.arange(ROWS_DEV)
    targets = (sources + offsets[:, slot_index % side_count][:, None, :]) % side_count
    group_index = jnp.arange(group_count)[:, None, None]
    local_rows = orders[group_index, targets, slot_index[None, None, :]]
    return (targets * ROWS_DEV + local_rows).reshape(ROWS).astype(jnp.int32)


def with_ends(drawn, key, least, top_value):
    extent = drawn.shape
    place = [jax.random.randint(jax.random.fold_in(key, axis), (), 0, extent[axis]) for axis in range(len(extent))]
    drawn = drawn.at[tuple(place)].set(least)
    longest = extent.index(max(extent))
    place[longest] = (place[longest] + 1) % extent[longest]
    return drawn.at[tuple(place)].set(top_value)


def levels(key, dims, cuts, smallest, largest):
    level = 1.0
    for dim, blocks in cuts:
        steps = jax.random.uniform(jax.random.fold_in(jax.random.fold_in(key, 6), dim), (blocks,), jnp.float32, smallest / len(cuts), largest / len(cuts))
        level = level * jnp.repeat(jnp.exp(steps), dims[dim] // blocks).reshape((-1,) + (1,) * (len(dims) - 1 - dim))
    return level


def noise(rng, shape, width, reach, cuts=(), kind=jnp.bfloat16):
    result = width * jax.random.normal(rng, shape, jnp.float32)
    if cuts:
        result = result * levels(rng, shape, cuts, -0.22, 0.18)
    return jnp.clip(result, -reach, reach).astype(kind)


def setup_inputs(seed: int = 0) -> dict:
    streams_of = jax.random.split(jax.random.key(seed), 27)
    hidden_in = noise(streams_of[0], (ROWS, L, D), 1.0, 6.0, ((0, 32),))
    side_state = noise(streams_of[1], (ROWS, L, DS), 1.0, 6.0, ((0, 32),))
    lengths = draw_lengths(jax.random.fold_in(streams_of[26], 71), 0)
    assign = draw_assign(jax.random.fold_in(streams_of[26], 71), 0)
    buckets = with_ends(jax.random.randint(streams_of[4], (2 * L - 1,), 0, NB), jax.random.fold_in(streams_of[4], 1), 0, NB - 1).astype(jnp.int32)
    backbone_gain_attn = jnp.clip(1.0 + 0.15 * jax.random.normal(streams_of[5], (D,), jnp.float32), 0.25, 1.75)
    backbone_query = noise(streams_of[6], (D, D), (4 * D) ** -0.5, 0.109375)
    backbone_key = noise(streams_of[7], (D, D), (4 * D) ** -0.5, 0.109375)
    backbone_value = noise(streams_of[8], (D, D), D ** -0.5, 0.21875)
    backbone_project = noise(streams_of[9], (D, D), (D // 32) ** -0.5, 1.25)
    backbone_rel = noise(streams_of[10], (NB, H), 1.0, 4.0, (), jnp.float32)
    backbone_gain_ff = jnp.clip(1.0 + 0.15 * jax.random.normal(streams_of[11], (D,), jnp.float32), 0.25, 1.75)
    backbone_ff_in = noise(streams_of[12], (D, FF), D ** -0.5, 0.21875)
    backbone_ff_out = noise(streams_of[13], (FF, D), (FF // 2) ** -0.5, 0.15625)
    down_weight = noise(streams_of[14], (D, DS), D ** -0.5, 0.21875)
    gate_logit = noise(streams_of[15], (DS,), 1.5, 6.0, (), jnp.float32)
    side_gain_attn = jnp.clip(1.0 + 0.15 * jax.random.normal(streams_of[16], (DS,), jnp.float32), 0.25, 1.75)
    side_query = noise(streams_of[17], (DS, DS), (2 * DS) ** -0.5, 0.4375)
    side_key = noise(streams_of[18], (DS, DS), (2 * DS) ** -0.5, 0.4375)
    side_value = noise(streams_of[19], (DS, DS), DS ** -0.5, 0.625)
    side_project = noise(streams_of[20], (DS, DS), (DS // 32) ** -0.5, 3.5)
    side_rel = noise(streams_of[21], (NB, SH), 1.0, 4.0, (), jnp.float32)
    side_gain_ff = jnp.clip(1.0 + 0.15 * jax.random.normal(streams_of[22], (DS,), jnp.float32), 0.25, 1.75)
    side_ff_in = noise(streams_of[23], (DS, FS), DS ** -0.5, 0.625)
    side_ff_out = noise(streams_of[24], (FS, DS), (FS // 2) ** -0.5, 0.4375)
    cotangent = noise(streams_of[25], (ROWS, L, DS), 1.0, 6.0, ((0, 32),))
    return {"hidden_in": hidden_in, "side_state": side_state, "lengths": lengths, "assign": assign, "buckets": buckets, "backbone_gain_attn": backbone_gain_attn, "backbone_query": backbone_query, "backbone_key": backbone_key, "backbone_value": backbone_value, "backbone_project": backbone_project, "backbone_rel": backbone_rel, "backbone_gain_ff": backbone_gain_ff, "backbone_ff_in": backbone_ff_in, "backbone_ff_out": backbone_ff_out, "down_weight": down_weight, "gate_logit": gate_logit, "side_gain_attn": side_gain_attn, "side_query": side_query, "side_key": side_key, "side_value": side_value, "side_project": side_project, "side_rel": side_rel, "side_gain_ff": side_gain_ff, "side_ff_in": side_ff_in, "side_ff_out": side_ff_out, "cotangent": cotangent}


epsilon = 1e-06
masked_score = -1000000000.0

@jax.custom_vjp
def low(v):
    return lax.optimization_barrier(v.astype(jnp.bfloat16)).astype(jnp.float32)

@jax.custom_vjp
def low_back(v):
    return v

def low_keep(v):
    return (low(v), None)

def low_pass(kept, grad):
    return (grad,)

def back_keep(v):
    return (v, None)

def back_low(kept, grad):
    return (low(grad),)
low.defvjp(low_keep, low_pass)
low_back.defvjp(back_keep, back_low)

def product(left_side, right_side):
    return jnp.dot(left_side, right_side, precision=lax.Precision.HIGHEST, preferred_element_type=jnp.float32)

def normalize(rows, gain):
    return rows * lax.rsqrt(lax.optimization_barrier(jnp.mean(rows * rows, axis=-1, keepdims=True)) + epsilon) * gain

def smooth_unit(values):
    return jax.nn.gelu(values, approximate=False)

def position_bias(buckets, table):
    onehot = (buckets[:, None] == jnp.arange(NB, dtype=jnp.int32)[None, :]).astype(jnp.float32)
    per_offset = product(onehot, table)
    places = jnp.arange(L, dtype=jnp.int32)
    offset = places[None, :] - places[:, None] + L - 1
    return jnp.transpose(per_offset[offset], (2, 0, 1))

def visible_keys(length):
    return jnp.arange(L, dtype=jnp.int32)[None, None, :] < length

def backbone_row(row_in, length, bias, weights):
    gain_attn, weight_query, weight_key, weight_value, weight_project, gain_ff, weight_in, weight_out = weights
    normed = low(normalize(row_in, gain_attn))
    queries = low(product(normed, weight_query)).reshape(L, H, HD)
    keys_all = low(product(normed, weight_key)).reshape(L, H, HD)
    values_all = low(product(normed, weight_value)).reshape(L, H, HD)
    scores = jnp.einsum('qhd,khd->hqk', queries, keys_all, precision=lax.Precision.HIGHEST) + bias
    probability = low(jax.nn.softmax(jnp.where(visible_keys(length), scores, masked_score), axis=-1))
    context = low(jnp.einsum('hqk,khd->qhd', probability, values_all, precision=lax.Precision.HIGHEST).reshape(L, D))
    stream = row_in + product(context, weight_project)
    inner = low(smooth_unit(product(low(normalize(stream, gain_ff)), weight_in)))
    return low(stream + product(inner, weight_out))

def side_row(tap_row, state_row, length, bias, params):
    gate_logit, gain_attn, weight_query, weight_key, weight_value, weight_project, gain_ff, weight_in, weight_out = params
    gate_value = jax.nn.sigmoid(gate_logit)
    mixed = gate_value * tap_row + (1.0 - gate_value) * state_row
    normed = low(normalize(mixed, gain_attn))
    queries = low_back(low(product(normed, weight_query))).reshape(L, SH, SHD)
    keys_all = low_back(low(product(normed, weight_key))).reshape(L, SH, SHD)
    values_all = low_back(low(product(normed, weight_value))).reshape(L, SH, SHD)
    scores = low_back(jnp.einsum('qhd,khd->hqk', queries, keys_all, precision=lax.Precision.HIGHEST) + bias)
    probability = low(jax.nn.softmax(jnp.where(visible_keys(length), scores, masked_score), axis=-1))
    context = low_back(low(jnp.einsum('hqk,khd->qhd', probability, values_all, precision=lax.Precision.HIGHEST).reshape(L, DS)))
    residual = mixed + low_back(product(context, weight_project))
    pre_act = low_back(product(low(normalize(residual, gain_ff)), weight_in))
    inner = low(smooth_unit(pre_act))
    return residual + low_back(product(inner, weight_out))

def reference(hidden_in, side_state, lengths, assign, buckets, backbone_gain_attn, backbone_query, backbone_key, backbone_value, backbone_project, backbone_rel, backbone_gain_ff, backbone_ff_in, backbone_ff_out, down_weight, gate_logit, side_gain_attn, side_query, side_key, side_value, side_project, side_rel, side_gain_ff, side_ff_in, side_ff_out, cotangent):
    slot_group = jnp.arange(ROWS, dtype=jnp.int32) // GROUP_ROWS
    natural = slot_group * GROUP_ROWS + assign.astype(jnp.int32)
    slot_length = lengths[natural]
    backbone_weights = tuple((member.astype(jnp.float32) for member in (backbone_gain_attn, backbone_query, backbone_key, backbone_value, backbone_project, backbone_gain_ff, backbone_ff_in, backbone_ff_out)))
    backbone_table = backbone_rel.astype(jnp.float32)

    def forward(primals):
        weight_down = primals[0]
        table = primals[7]
        state = primals[11]
        params = (primals[1], primals[2], primals[3], primals[4], primals[5], primals[6], primals[8], primals[9], primals[10])
        backbone_bias = position_bias(buckets, backbone_table)

        def backbone_step(items):
            return backbone_row(items[0].astype(jnp.float32), items[1], backbone_bias, backbone_weights)
        hidden = lax.map(jax.checkpoint(backbone_step), (hidden_in, slot_length))

        def tap_step(hidden_row):
            return low_back(low(product(hidden_row, weight_down)))
        taps = lax.map(jax.checkpoint(tap_step), hidden)
        tap_rows = jnp.zeros((ROWS, L, DS), jnp.float32).at[natural].set(taps)
        bias = position_bias(buckets, table)

        def side_step(items):
            return side_row(items[0], items[1], items[2], bias, params)
        return lax.map(jax.checkpoint(side_step), (tap_rows, state, lengths))
    primals = tuple((member.astype(jnp.float32) for member in (down_weight, gate_logit, side_gain_attn, side_query, side_key, side_value, side_project, side_rel, side_gain_ff, side_ff_in, side_ff_out, side_state)))
    output, pullback = jax.vjp(forward, primals)
    grads = pullback(cotangent.astype(jnp.float32))[0]
    return (output.astype(jnp.bfloat16), grads[11], grads[0], grads[1], grads[2], grads[3], grads[4], grads[5], grads[6], grads[7], grads[8], grads[9], grads[10])
```

```python
import functools
import math

import jax
import jax.numpy as jnp
from jax import lax
from jax.experimental import pallas as pl
from jax.experimental.pallas import tpu as pltpu
from jax.sharding import PartitionSpec as P

D = 768
H = 12
HD = 64
FF = 3072
NB = 32
DS = 96
SH = 12
SHD = 8
FS = 384
L = 512
W = 128
TILE = 128

EPS = 1e-06
MASKED = -1e9
LIMIT = 60.0
F32 = jnp.float32
BF16 = jnp.bfloat16
VMEM_BYTES = 44 * 1024 * 1024


def dot(a, b, dims=((1,), (0,)), precision=None):
    return lax.dot_general(
        a, b, (dims, ((), ())), precision=precision, preferred_element_type=F32
    )


def dot_nt(a, b):
    return dot(a, b, ((1,), (1,)))


def dot_tn(a, b):
    return dot(a, b, ((0,), (0,)))


def normal_cdf(v):
    return 0.5 * (1.0 + lax.erf(v * (1.0 / math.sqrt(2.0))))


def offset_table(buckets, rel):
    rows = lax.broadcasted_iota(jnp.int32, (NB, 2 * L), 0)
    onehot = (rows == buckets).astype(F32)
    return dot(rel, onehot, precision=lax.Precision.HIGHEST)


def toeplitz(row):
    wide = jnp.broadcast_to(row, (TILE, 2 * L))
    return pltpu.roll(wide, 2 * L - (TILE - 1), 1, stride=1, stride_axis=0)


def bias_block(bias_ref, head, block):
    start = (L // TILE - 1 - block) * TILE
    return bias_ref[head, :, start : start + L]


def lane_group(shape, size):
    return lax.broadcasted_iota(jnp.int32, shape, len(shape) - 1) // size


def bounded(q, k, table, size, heads):
    rows = lax.broadcasted_iota(jnp.int32, (q.shape[1], W), 0) // size
    cols = lax.broadcasted_iota(jnp.int32, (q.shape[1], W), 1)
    pick = ((rows == cols) & (rows < heads)).astype(BF16)
    qf, kf = q.astype(F32), k.astype(F32)
    qn = jnp.max(dot((qf * qf).astype(BF16), pick), axis=0, keepdims=True)
    kn = jnp.max(dot((kf * kf).astype(BF16), pick), axis=0, keepdims=True)
    top = jnp.max(jnp.sqrt(qn) * jnp.sqrt(kn)) * 1.02
    return top + jnp.max(jnp.abs(table)) < LIMIT


def start_all(pairs, sems):
    copies = [pltpu.make_async_copy(src, dst, sems.at[n]) for n, (src, dst) in enumerate(pairs)]
    for copy in copies:
        copy.start()
    return copies


def backbone_kernel(
    lengths_ref, assign_ref, rel_hbm, bucket_hbm, x_hbm, gain1_hbm, wq_hbm, wk_hbm, wv_hbm, wo_hbm, gain2_hbm, w1_hbm,
    w2_hbm, wd_hbm,
    hidden_ref, taps_ref,
    rel, buckets, x_ref, gain1_ref, wq, wk, wv, wo, gain2_ref, w1, w2, wd, sems,
    normed, q_s, k_s, vx, ctx, bias, stream, inner,
):
    pairs = (
        (rel_hbm, rel), (bucket_hbm, buckets.at[0]), (x_hbm, x_ref), (gain1_hbm, gain1_ref.at[0]),
        (wq_hbm, wq), (wk_hbm, wk), (wv_hbm, wv), (wo_hbm, wo), (gain2_hbm, gain2_ref.at[0]),
        (w1_hbm, w1), (w2_hbm, w2), (wd_hbm, wd),
    )
    copies = start_all(pairs, sems)
    length = lengths_ref[assign_ref[lax.axis_index("side")]]

    copies[0].wait()
    copies[1].wait()
    table = offset_table(buckets[...], rel[...])
    for head in range(H):
        bias[head] = toeplitz(table[head : head + 1])
    copies[2].wait()
    copies[3].wait()
    x = x_ref[...].astype(F32)
    scale = lax.rsqrt(jnp.mean(x * x, axis=1, keepdims=True) + EPS)
    normed[...] = (x * scale * gain1_ref[...]).astype(BF16)
    copies[4].wait()
    q_s[...] = dot(normed[...], wq[...]).astype(BF16)
    copies[5].wait()
    k_s[...] = dot(normed[...], wk[...]).astype(BF16)
    copies[6].wait()
    live_row = lax.broadcasted_iota(jnp.int32, (L, 1), 0) < length
    value = dot(normed[...], wv[...])
    value = jnp.where(live_row, value, 0.0).astype(BF16)
    ones = jnp.where(live_row, 1.0, 0.0).astype(BF16)
    for pair in range(H // 2):
        vx[pair, :, :W] = value[:, pair * W : (pair + 1) * W]
        vx[pair, :, W:] = jnp.broadcast_to(ones, (L, W))
    low_half = lax.broadcasted_iota(jnp.int32, (L, W), 1) < HD
    low_row = lax.broadcasted_iota(jnp.int32, (TILE, W), 1) < HD
    live = lax.broadcasted_iota(jnp.int32, (1, L), 1) < length

    def attend(pair, stable):
        lanes = pl.ds(pl.multiple_of(pair * W, W), W)
        keys = k_s[:, lanes]
        for block in range(L // TILE):
            rows = slice(block * TILE, (block + 1) * TILE)
            query = q_s[rows, lanes]
            results = []
            for half in range(2):
                mine = low_row if half == 0 else jnp.logical_not(low_row)
                scores = dot_nt(jnp.where(mine, query, jnp.zeros_like(query)), keys)
                scores = scores + bias_block(bias, pair * 2 + half, block)
                if stable:
                    scores = jnp.where(live, scores, MASKED)
                    scores = scores - jnp.max(scores, axis=1, keepdims=True)
                results.append(dot(jnp.exp(scores).astype(BF16), vx[pair]))
            top = jnp.where(low_row, results[0][:, :W], results[1][:, :W])
            total = jnp.where(low_row, results[0][:, W:], results[1][:, W:])
            ctx[rows, lanes] = (top / total).astype(BF16)

    safe = bounded(q_s[...], k_s[...], table, HD, H)

    @pl.when(safe)
    def _():
        @pl.loop(0, H // 2)
        def _(pair):
            attend(pair, False)

    @pl.when(jnp.logical_not(safe))
    def _():
        @pl.loop(0, H // 2)
        def _(pair):
            attend(pair, True)

    copies[7].wait()
    copies[8].wait()
    flow = x_ref[...].astype(F32) + dot(ctx[...], wo[...])
    stream[...] = flow
    scale = lax.rsqrt(jnp.mean(flow * flow, axis=1, keepdims=True) + EPS)
    normed[...] = (flow * scale * gain2_ref[...]).astype(BF16)
    copies[9].wait()
    step = 256

    @pl.loop(0, FF // step)
    def _(n):
        cols = pl.ds(pl.multiple_of(n * step, step), step)
        pre = dot(normed[...], w1[:, cols])
        inner[:, cols] = (pre * normal_cdf(pre)).astype(BF16)

    copies[10].wait()
    for n in range(D // 256):
        cols = slice(n * 256, (n + 1) * 256)
        hidden_ref[:, cols] = (stream[:, cols] + dot(inner[...], w2[:, cols])).astype(BF16)
    copies[11].wait()
    taps_ref[...] = dot_nt(hidden_ref[...], wd[...]).astype(BF16)


def backbone(*args):
    smem = pl.BlockSpec(memory_space=pltpu.SMEM)
    vmem = pl.BlockSpec(memory_space=pltpu.VMEM)
    hbm = pl.BlockSpec(memory_space=pl.ANY)
    return pl.pallas_call(
        backbone_kernel,
        out_shape=(
            jax.ShapeDtypeStruct((L, D), BF16),
            jax.ShapeDtypeStruct((L, DS), BF16),
        ),
        in_specs=[smem, smem] + [hbm] * 12,
        out_specs=(vmem, vmem),
        scratch_shapes=[
            pltpu.VMEM((H, NB), F32),
            pltpu.VMEM((1, 2 * L), jnp.int32),
            pltpu.VMEM((L, D), BF16),
            pltpu.VMEM((1, D), F32),
            pltpu.VMEM((D, D), BF16),
            pltpu.VMEM((D, D), BF16),
            pltpu.VMEM((D, D), BF16),
            pltpu.VMEM((D, D), BF16),
            pltpu.VMEM((1, D), F32),
            pltpu.VMEM((D, FF), BF16),
            pltpu.VMEM((FF, D), BF16),
            pltpu.VMEM((DS, D), BF16),
            pltpu.SemaphoreType.DMA((12,)),
            pltpu.VMEM((L, D), BF16),
            pltpu.VMEM((L, D), BF16),
            pltpu.VMEM((L, D), BF16),
            pltpu.VMEM((H // 2, L, 2 * W), BF16),
            pltpu.VMEM((L, D), BF16),
            pltpu.VMEM((H, TILE, 2 * L), F32),
            pltpu.VMEM((L, D), F32),
            pltpu.VMEM((L, FF), BF16),
        ],
        compiler_params=pltpu.CompilerParams(vmem_limit_bytes=60 * 1024 * 1024),
        cost_estimate=pl.CostEstimate(
            flops=9_000_000_000, bytes_accessed=17_000_000, transcendentals=5_000_000
        ),
        name="backbone",
    )(*args)


DOWN0, QKV0, SMALL0, PROJ0, FFIN0, FFOUT0 = 0, 576, 864, 896, 992, 1280
PACK = 1568
HALF = PACK // 2


def side_kernel(
    count, lengths_ref, assign_ref, taps_ref, *rest
):
    moved_hbm = rest[:count]
    (
        bucket_hbm, rel_hbm, gate_hbm, gain1_hbm, gain2_hbm, wq_hbm, wk_hbm, wv_hbm, wo_hbm, w1_hbm, w2_hbm, hidden_hbm,
        out_ref, gstate_ref, keep_ref, send_ref,
        buckets, rel, gate_ref, gain1_ref, gain2_ref, wq_ref, wk_ref, wv_ref, wo_ref, w1_ref, w2_ref, hidden,
        moved, sems, wpad, bias, probs, q_s, k_s, v_s, top_s, sum_s, dcx, qt_s, dct_s, dq_s, dkt, dvt,
        diag, dtab, pack,
    ) = rest[count:]
    rank = lax.axis_index("side")
    seq = assign_ref[rank]
    pairs = (
        (bucket_hbm, buckets.at[0]), (rel_hbm, rel), (gate_hbm, gate_ref.at[0]), (gain1_hbm, gain1_ref.at[0]),
        (gain2_hbm, gain2_ref.at[0]), (wq_hbm, wq_ref), (wk_hbm, wk_ref), (wv_hbm, wv_ref), (wo_hbm, wo_ref),
        (w1_hbm, w1_ref), (w2_hbm, w2_ref), (hidden_hbm, hidden),
    )
    copies = start_all(pairs, sems)
    for step in range(count):

        @pl.when(lax.rem(rank + count - seq, count) == step)
        def _():
            pltpu.make_async_copy(moved_hbm[step], moved, sems.at[12]).start()

    for copy in copies[:-1]:
        copy.wait()
    length = lengths_ref[seq]
    wpad[...] = jnp.zeros_like(wpad)
    wpad[0, :, :DS] = wq_ref[...]
    wpad[1, :, :DS] = wk_ref[...]
    wpad[2, :, :DS] = wv_ref[...]
    wpad[3, :, :DS] = wo_ref[...].astype(F32).T.astype(BF16)
    table = offset_table(buckets[...], rel[...])
    for head in range(SH):
        bias[head] = toeplitz(table[head : head + 1])

    gate = jax.nn.sigmoid(gate_ref[...])
    gain1, gain2 = gain1_ref[...], gain2_ref[...]
    pltpu.make_async_copy(moved_hbm[0], moved, sems.at[12]).wait()
    tap = taps_ref[...].astype(F32)
    old = moved[0].astype(F32).T
    mixed = gate * tap + (1.0 - gate) * old
    scale1 = lax.rsqrt(jnp.mean(mixed * mixed, axis=1, keepdims=True) + EPS)
    unit1 = mixed * scale1
    normed1 = (unit1 * gain1).astype(BF16)
    lane = lax.broadcasted_iota(jnp.int32, (L, W), 1)
    live_row = lax.broadcasted_iota(jnp.int32, (L, W), 0) < length
    query = dot(normed1, wpad[0]).astype(BF16)
    key = dot(normed1, wpad[1]).astype(BF16)
    value = dot(normed1, wpad[2]).astype(BF16)
    one = jnp.ones((L, W), BF16)
    mask_key = jnp.where(live_row, 0.0, MASKED)
    q_s[...] = jnp.where(lane == DS, 1.0, query.astype(F32)).astype(BF16)
    k_s[...] = jnp.where(lane == DS, mask_key, key.astype(F32)).astype(BF16)
    v_s[:, :W] = value
    v_s[:, W:] = one
    safe = bounded(query, key, table, SHD, SH)
    head_of = lax.broadcasted_iota(jnp.int32, (TILE, W), 1) // SHD
    marker = lax.broadcasted_iota(jnp.int32, (TILE, W), 1) == DS
    zero_tile = jnp.zeros((TILE, W), BF16)
    blocks = [slice(b * TILE, (b + 1) * TILE) for b in range(L // TILE)]

    def attend(head, stable):
        mine = head_of == head
        for block, rows in enumerate(blocks):
            q_h = jnp.where(mine | marker, q_s[rows], zero_tile)
            scores = dot_nt(q_h, k_s[...]) + bias_block(bias, head, block)
            if stable:
                scores = scores - jnp.max(scores, axis=1, keepdims=True)
            weight = jnp.exp(scores).astype(BF16)
            probs[head, rows] = weight
            both = dot(weight, v_s[...])
            top_s[rows] = jnp.where(mine, both[:, :W], top_s[rows])
            sum_s[rows] = jnp.where(mine, both[:, W:], sum_s[rows])

    sum_s[...] = jnp.ones_like(sum_s)
    top_s[...] = jnp.zeros_like(top_s)

    @pl.when(safe)
    def _():
        @pl.loop(0, SH)
        def _(head):
            attend(head, False)

    @pl.when(jnp.logical_not(safe))
    def _():
        @pl.loop(0, SH)
        def _(head):
            attend(head, True)

    inverse = 1.0 / sum_s[...]
    context = top_s[...] * inverse
    context16 = context[:, :DS].astype(BF16)
    residual = mixed + dot(context16, wo_ref[...])
    scale2 = lax.rsqrt(jnp.mean(residual * residual, axis=1, keepdims=True) + EPS)
    unit2 = residual * scale2
    normed2 = (unit2 * gain2).astype(BF16)
    pre = dot(normed2, w1_ref[...])
    cdf = normal_cdf(pre)
    inner = (pre * cdf).astype(BF16)
    out_ref[...] = (residual + dot_nt(inner, w2_ref[...])).T.astype(BF16)

    cotangent = moved[1].astype(F32).T.astype(BF16)
    slope = cdf + pre * (jnp.exp(-0.5 * pre * pre) * (1.0 / math.sqrt(2.0 * math.pi)))
    d_pre = (dot(cotangent, w2_ref[...]) * slope).astype(BF16)
    g_ffout = dot_tn(cotangent, inner)
    g_ffin = dot_tn(normed2, d_pre)
    for n in range(FS // W):
        pack[FFIN0 + n * DS : FFIN0 + (n + 1) * DS] = g_ffin[:, n * W : (n + 1) * W]
        pack[FFOUT0 + n * DS : FFOUT0 + (n + 1) * DS] = g_ffout[:, n * W : (n + 1) * W]
    dy = dot_nt(d_pre, w1_ref[...])
    g_gain2 = jnp.sum(dy * unit2, axis=0, keepdims=True)
    dyg = dy * gain2
    d_resid = cotangent.astype(F32) + scale2 * (
        dyg - unit2 * jnp.mean(dyg * unit2, axis=1, keepdims=True)
    )
    d_attn = d_resid.astype(BF16)
    pack[PROJ0 : PROJ0 + DS] = jnp.zeros((DS, W), F32)
    pack[PROJ0 : PROJ0 + DS, :DS] = dot_tn(context16, d_attn)
    d_context = dot(d_attn, wpad[3]).astype(BF16)
    d_scaled = (d_context.astype(F32) * inverse).astype(BF16)
    product = d_scaled.astype(F32) * context
    r_head = lax.broadcasted_iota(jnp.int32, (W, W), 0) // SHD
    c_head = lax.broadcasted_iota(jnp.int32, (W, W), 1) // SHD
    same = (r_head == c_head).astype(F32)
    delta = dot(product, same, precision=lax.Precision.HIGHEST) * -0.25
    delta_hi = delta.astype(BF16).astype(F32)
    dcx[:, :W] = d_scaled
    dcx[:, W:] = jnp.where(lane % 2 == 0, delta_hi, delta - delta_hi).astype(BF16)
    d_scaled_t = d_scaled.astype(F32).T
    query_t = query.astype(F32).T
    for head in range(SH):
        rows = slice(head * SHD, (head + 1) * SHD)
        qt_s[head] = query_t[rows].astype(BF16)
        dct_s[head] = d_scaled_t[rows].astype(BF16)
    dq_s[...] = jnp.zeros_like(dq_s)
    dkt[...] = jnp.zeros_like(dkt)
    dvt[...] = jnp.zeros_like(dvt)
    dtab[...] = jnp.zeros_like(dtab)

    @pl.loop(0, SH)
    def _(head):
        diag[...] = jnp.zeros_like(diag)
        mine = head_of == head
        both_mine = jnp.concatenate([mine, mine], axis=1)
        tiles = []
        for block, rows in enumerate(blocks):
            lhs = jnp.where(both_mine, dcx[rows], jnp.zeros((TILE, 2 * W), BF16))
            d_scores = probs[head, rows].astype(F32) * dot_nt(lhs, v_s[...])
            start = (L // TILE - 1 - block) * TILE
            diag[:, start : start + L] += d_scores
            d16 = d_scores.astype(BF16)
            tiles.append(d16)
            dq_s[rows] = jnp.where(mine, dot(d16, k_s[...]), dq_s[rows])
        d_all = jnp.concatenate(tiles, axis=0)
        rows8 = pl.ds(pl.multiple_of(head * SHD, SHD), SHD)
        dkt[rows8] = dot(qt_s[head], d_all)
        dvt[rows8] = dot(dct_s[head], probs[head])
        cur = diag[...]
        half = TILE // 2
        while half >= 8:
            cur = pltpu.roll(cur[:half], half, 1) + cur[half:]
            half //= 2
        for shift in (4, 2, 1):
            cur = pltpu.roll(cur, shift, 1) + pltpu.roll(cur, 8 - shift, 0)
        dtab[pl.ds(head, 1)] = cur[:1]

    dq = dq_s[...].astype(BF16)
    dk = dkt[...].T.astype(BF16)
    dv = dvt[...].T.astype(BF16)
    for n, grad in enumerate((dq, dk, dv)):
        pack[QKV0 + n * DS : QKV0 + (n + 1) * DS] = dot_tn(normed1, grad)
    d_normed = dot_nt(dq, wpad[0]) + dot_nt(dk, wpad[1]) + dot_nt(dv, wpad[2])
    dyg = d_normed * gain1
    d_mixed = d_resid + scale1 * (dyg - unit1 * jnp.mean(dyg * unit1, axis=1, keepdims=True))
    gstate_ref[...] = ((1.0 - gate) * d_mixed).T.astype(BF16)
    d_tap = (gate * d_mixed).astype(BF16)
    copies[11].wait()
    down_t = dot_tn(d_tap, hidden[...])
    for n in range(D // W):
        pack[DOWN0 + n * DS : DOWN0 + (n + 1) * DS] = down_t[:, n * W : (n + 1) * W]
    rows = lax.broadcasted_iota(jnp.int32, (NB, 2 * L), 0)
    onehot = (rows == buckets[...]).astype(F32)
    totals = dot(dtab[...], onehot, ((1,), (1,)), lax.Precision.HIGHEST)
    pack[SMALL0 : SMALL0 + NB] = jnp.zeros((NB, W), F32)
    pack[SMALL0 : SMALL0 + 16, :NB] = totals
    g_gate = gate * (1.0 - gate) * jnp.sum(d_mixed * (tap - old), axis=0, keepdims=True)
    g_gain1 = jnp.sum(d_normed * unit1, axis=0, keepdims=True)
    pack[SMALL0 + 16 : SMALL0 + 17, :DS] = g_gate
    pack[SMALL0 + 17 : SMALL0 + 18, :DS] = g_gain1
    pack[SMALL0 + 18 : SMALL0 + 19, :DS] = g_gain2
    core = lax.rem(lax.axis_index("dp"), 2)
    keep_ref[...] = pack[pl.ds(pl.multiple_of(core * HALF, HALF), HALF)].astype(BF16)
    send_ref[...] = pack[pl.ds(pl.multiple_of((1 - core) * HALF, HALF), HALF)].astype(BF16)


def side_block(lengths, assign, taps, moved, *args):
    smem = pl.BlockSpec(memory_space=pltpu.SMEM)
    vmem = pl.BlockSpec(memory_space=pltpu.VMEM)
    hbm = pl.BlockSpec(memory_space=pl.ANY)
    count = len(moved)
    return pl.pallas_call(
        functools.partial(side_kernel, count),
        out_shape=(
            jax.ShapeDtypeStruct((DS, L), BF16),
            jax.ShapeDtypeStruct((DS, L), BF16),
            jax.ShapeDtypeStruct((HALF, W), BF16),
            jax.ShapeDtypeStruct((HALF, W), BF16),
        ),
        in_specs=[smem, smem, vmem] + [hbm] * (count + len(args)),
        out_specs=(vmem,) * 4,
        scratch_shapes=[
            pltpu.VMEM((1, 2 * L), jnp.int32),
            pltpu.VMEM((SH, NB), F32),
            pltpu.VMEM((1, DS), F32),
            pltpu.VMEM((1, DS), F32),
            pltpu.VMEM((1, DS), F32),
            pltpu.VMEM((DS, DS), BF16),
            pltpu.VMEM((DS, DS), BF16),
            pltpu.VMEM((DS, DS), BF16),
            pltpu.VMEM((DS, DS), BF16),
            pltpu.VMEM((DS, FS), BF16),
            pltpu.VMEM((DS, FS), BF16),
            pltpu.VMEM((L, D), BF16),
            pltpu.VMEM((2, DS, L), BF16),
            pltpu.SemaphoreType.DMA((13,)),
            pltpu.VMEM((4, DS, W), BF16),
            pltpu.VMEM((SH, TILE, 2 * L), F32),
            pltpu.VMEM((SH, L, L), BF16),
            pltpu.VMEM((L, W), BF16),
            pltpu.VMEM((L, W), BF16),
            pltpu.VMEM((L, 2 * W), BF16),
            pltpu.VMEM((L, W), F32),
            pltpu.VMEM((L, W), F32),
            pltpu.VMEM((L, 2 * W), BF16),
            pltpu.VMEM((SH, SHD, L), BF16),
            pltpu.VMEM((SH, SHD, L), BF16),
            pltpu.VMEM((L, W), F32),
            pltpu.VMEM((W, L), F32),
            pltpu.VMEM((W, L), F32),
            pltpu.VMEM((TILE, 2 * L), F32),
            pltpu.VMEM((16, 2 * L), F32),
            pltpu.VMEM((PACK, W), F32),
        ],
        compiler_params=pltpu.CompilerParams(vmem_limit_bytes=VMEM_BYTES),
        cost_estimate=pl.CostEstimate(
            flops=9_000_000_000, bytes_accessed=4_000_000, transcendentals=5_000_000
        ),
        name="side_block",
    )(lengths, assign, taps, *moved, *args)


def finish_kernel(count, assign_ref, mine_hbm, other_hbm, *rest):
    outs, gstates = rest[:count], rest[count : 2 * count]
    results = rest[2 * count : 2 * count + 13]
    half, out, gstate16, *parts, sems = rest[2 * count + 13 :]
    rank = lax.axis_index("side")
    core = lax.rem(lax.axis_index("dp"), 2)
    first = pltpu.make_async_copy(mine_hbm, half.at[core], sems.at[0])
    second = pltpu.make_async_copy(other_hbm, half.at[1 - core], sems.at[1])
    first.start()
    second.start()
    slot = jnp.int32(0)
    for n in range(count):
        slot = jnp.where(assign_ref[n] == rank, n, slot)
    for step in range(count):

        @pl.when(lax.rem(rank + count - slot, count) == step)
        def _():
            pltpu.make_async_copy(gstates[step], gstate16, sems.at[2]).start()
            pltpu.make_async_copy(outs[step], out, sems.at[3]).start()

    gstate, down, gate, gain1, gq, gk, gv, go, rel, gain2, g1, g2 = parts
    pltpu.make_async_copy(gstates[0], gstate16, sems.at[2]).wait()
    pltpu.make_async_copy(outs[0], out, sems.at[3]).wait()
    gstate[...] = gstate16[...].astype(F32)
    first.wait()
    second.wait()

    def take(start, stop):
        pieces = []
        for side in range(2):
            low, high = max(start, side * HALF), min(stop, (side + 1) * HALF)
            if low < high:
                pieces.append(half[side, low - side * HALF : high - side * HALF].astype(F32))
        return pieces[0] if len(pieces) == 1 else jnp.concatenate(pieces, axis=0)

    for n in range(D // W):
        down[:, n * W : (n + 1) * W] = take(DOWN0 + n * DS, DOWN0 + (n + 1) * DS)
    for n, ref in enumerate((gq, gk, gv)):
        ref[...] = take(QKV0 + n * DS, QKV0 + (n + 1) * DS)[:, :DS]
    small = take(SMALL0, SMALL0 + NB)
    rel[...] = small[:SH, :NB]
    gate[...] = small[16:17, :DS]
    gain1[...] = small[17:18, :DS]
    gain2[...] = small[18:19, :DS]
    go[...] = take(PROJ0, PROJ0 + DS)[:, :DS]
    for n in range(FS // W):
        g1[:, n * W : (n + 1) * W] = take(FFIN0 + n * DS, FFIN0 + (n + 1) * DS)
        g2[:, n * W : (n + 1) * W] = take(FFOUT0 + n * DS, FFOUT0 + (n + 1) * DS)
    pairs = [
        (ref.at[0] if ref.shape[0] == 1 else ref, result)
        for ref, result in zip([out, *parts], results, strict=True)
    ]
    for copy in start_all(pairs, sems):
        copy.wait()


def finish(assign, mine, other, outs, gstates):
    smem = pl.BlockSpec(memory_space=pltpu.SMEM)
    hbm = pl.BlockSpec(memory_space=pl.ANY)
    count = len(outs)
    parts = [
        (DS, L), (DS, D), (1, DS), (1, DS), (DS, DS), (DS, DS), (DS, DS), (DS, DS), (SH, NB), (1, DS), (DS, FS), (DS, FS),
    ]
    shapes = [jax.ShapeDtypeStruct(p[1:] if p[0] == 1 else p, F32) for p in parts]
    return pl.pallas_call(
        functools.partial(finish_kernel, count),
        out_shape=(jax.ShapeDtypeStruct((DS, L), BF16), *shapes),
        in_specs=[smem] + [hbm] * (2 + 2 * count),
        out_specs=(hbm,) * 13,
        scratch_shapes=[
            pltpu.VMEM((2, HALF, W), BF16),
            pltpu.VMEM((DS, L), BF16),
            pltpu.VMEM((DS, L), BF16),
            *[pltpu.VMEM(p, F32) for p in parts],
            pltpu.SemaphoreType.DMA((13,)),
        ],
        compiler_params=pltpu.CompilerParams(vmem_limit_bytes=16 * 1024 * 1024),
        name="finish",
    )(assign, mine, other, *outs, *gstates)


def swap(value, axis, bit):
    size = lax.axis_size(axis)
    return lax.ppermute(value, axis, [(i, i ^ bit) for i in range(size)])


def rotations(value):
    size = lax.axis_size("side")
    return [value] + [
        lax.ppermute(value, "side", [(i, (i + k) % size) for i in range(size)])
        for k in range(1, size)
    ]


def add(one, two):
    return (one.astype(F32) + two.astype(F32)).astype(BF16)


def total(keep, send):
    mine = add(keep, swap(send, "dp", 1))
    for axis, first in (("dp", 2), ("side", 1)):
        bit = first
        while bit < lax.axis_size(axis):
            mine = add(mine, swap(mine, axis, bit))
            bit *= 2
    return mine, swap(mine, "dp", 1)


def shards(
    hidden_in, side_state, lengths, assign, buckets,
    backbone_gain_attn, backbone_query, backbone_key, backbone_value, backbone_project, backbone_rel,
    backbone_gain_ff, backbone_ff_in, backbone_ff_out, down_weight, gate_logit,
    side_gain_attn, side_query, side_key, side_value, side_project, side_rel,
    side_gain_ff, side_ff_in, side_ff_out, cotangent,
):
    moved = rotations(jnp.stack([side_state[0].T, cotangent[0].T]))
    wide = jnp.pad(buckets, (0, 1))
    hidden, taps = backbone(
        lengths, assign, backbone_rel.T, wide, hidden_in[0], backbone_gain_attn,
        backbone_query, backbone_key, backbone_value, backbone_project, backbone_gain_ff,
        backbone_ff_in, backbone_ff_out, down_weight.T,
    )
    out, gstate, keep, send = side_block(
        lengths, assign, taps, moved, wide, side_rel.T, gate_logit, side_gain_attn, side_gain_ff,
        side_query, side_key, side_value, side_project, side_ff_in, side_ff_out.T, hidden,
    )
    outs, gstates = rotations(out), rotations(gstate)
    mine, other = total(keep, send)
    res = finish(assign, mine, other, outs, gstates)
    out, gstate, down, gate, gain1, gq, gk, gv, go, rel, gain2, g1, g2 = res
    return (
        out.T[None], gstate.T[None], down.T, gate, gain1, gq, gk, gv, go, rel.T, gain2, g1, g2.T,
    )


def solution(mesh):
    rows = P(("dp", "side"), None, None)
    return jax.shard_map(
        shards,
        mesh=mesh,
        in_specs=(rows, rows, P("dp"), P("dp")) + (P(),) * 21 + (rows,),
        out_specs=(rows, rows) + (P(),) * 11,
        check_vma=False,
    )
```

```python
import functools
import math

import jax
import jax.numpy as jnp
from jax import lax
from jax.experimental import pallas as pl
from jax.experimental.pallas import tpu as pltpu
from jax.sharding import PartitionSpec as P

D = 768
H = 12
HD = 64
FF = 3072
NB = 32
DS = 96
SH = 12
SHD = 8
FS = 384
L = 512
W = 128
OFFSETS = 2 * L - 1
TILE = 128

EPS = 1e-06
MASKED = -1e9
LIMIT = 60.0
F32 = jnp.float32
BF16 = jnp.bfloat16
VMEM_BYTES = 44 * 1024 * 1024
UNROLL = 6
UNROLL_BACK = 6
PAIRS = 6


def dot(a, b, dims=((1,), (0,)), precision=None):
    return lax.dot_general(
        a, b, (dims, ((), ())), precision=precision, preferred_element_type=F32
    )


def dot_nt(a, b):
    return dot(a, b, ((1,), (1,)))


def dot_tn(a, b):
    return dot(a, b, ((0,), (0,)))


def normal_cdf(v):
    return 0.5 * (1.0 + lax.erf(v * (1.0 / math.sqrt(2.0))))


def offset_table(buckets, rel):
    rows = lax.broadcasted_iota(jnp.int32, (NB, OFFSETS), 0)
    onehot = (rows == buckets).astype(F32)
    table = dot(rel, onehot, precision=lax.Precision.HIGHEST)
    return jnp.concatenate([table, jnp.zeros((rel.shape[0], 1), F32)], axis=1)


def toeplitz(row):
    wide = jnp.broadcast_to(row, (TILE, 2 * L))
    return pltpu.roll(wide, 2 * L - (TILE - 1), 1, stride=1, stride_axis=0)


def bounded(q, k, table, size, heads):
    rows = lax.broadcasted_iota(jnp.int32, (q.shape[1], W), 0) // size
    cols = lax.broadcasted_iota(jnp.int32, (q.shape[1], W), 1)
    pick = ((rows == cols) & (rows < heads)).astype(BF16)
    qf, kf = q.astype(F32), k.astype(F32)
    qn = jnp.max(dot((qf * qf).astype(BF16), pick), axis=0, keepdims=True)
    kn = jnp.max(dot((kf * kf).astype(BF16), pick), axis=0, keepdims=True)
    top = jnp.max(jnp.sqrt(qn) * jnp.sqrt(kn)) * 1.02
    return top + jnp.max(jnp.abs(table)) < LIMIT


def start_all(pairs, sems):
    copies = [pltpu.make_async_copy(src, dst, sems.at[n]) for n, (src, dst) in enumerate(pairs)]
    for copy in copies:
        copy.start()
    return copies


def backbone_kernel(
    lengths_ref, assign_ref, rel_hbm, bucket_hbm, x_hbm, gain1_hbm, wq_hbm, wk_hbm, wv_hbm, wo_hbm, gain2_hbm, w1_hbm,
    w2_hbm, wd_hbm,
    hidden_ref, taps_ref,
    rel, buckets, x_ref, gain1_ref, wq, wk, wv, wo, gain2_ref, w1, w2, wd, sems,
    normed, q_s, k_s, vx, ctx, table, stream, inner,
):
    pairs = (
        (x_hbm, x_ref), (gain1_hbm, gain1_ref.at[0]), (rel_hbm, rel), (bucket_hbm, buckets.at[0]),
        (wq_hbm, wq), (wk_hbm, wk), (wv_hbm, wv), (wo_hbm, wo), (gain2_hbm, gain2_ref.at[0]),
        (w1_hbm, w1), (w2_hbm, w2), (wd_hbm, wd),
    )
    copies = [pltpu.make_async_copy(src, dst, sems.at[n]) for n, (src, dst) in enumerate(pairs)]
    for n in (0, 1, 4):
        copies[n].start()
    length = lengths_ref[assign_ref[lax.axis_index("side")]]
    copies[0].wait()
    copies[1].wait()
    for n in (5, 6, 2, 3):
        copies[n].start()
    x = x_ref[...].astype(F32)
    scale = lax.rsqrt(jnp.mean(x * x, axis=1, keepdims=True) + EPS)
    normed[...] = (x * scale * gain1_ref[...]).astype(BF16)
    copies[4].wait()
    copies[7].start()
    q_s[...] = dot(normed[...], wq[...]).astype(BF16)
    copies[5].wait()
    k_s[...] = dot(normed[...], wk[...]).astype(BF16)
    copies[6].wait()
    for n in (8, 9, 10, 11):
        copies[n].start()
    live_row = lax.broadcasted_iota(jnp.int32, (L, 1), 0) < length
    value = dot(normed[...], wv[...])
    value = jnp.where(live_row, value, 0.0).astype(BF16)
    ones = jnp.where(live_row, 1.0, 0.0).astype(BF16)
    for pair in range(H // 2):
        vx[pair, :, :W] = value[:, pair * W : (pair + 1) * W]
        vx[pair, :, W:] = jnp.broadcast_to(ones, (L, W))
    low_half = lax.broadcasted_iota(jnp.int32, (L, W), 1) < HD
    low_row = lax.broadcasted_iota(jnp.int32, (TILE, W), 1) < HD
    live = lax.broadcasted_iota(jnp.int32, (1, L), 1) < length

    def attend(pair, stable):
        lanes = pl.ds(pl.multiple_of(pair * W, W), W)
        keys = k_s[:, lanes]
        tiles = [toeplitz(table[pl.ds(pair * 2 + half, 1)]) for half in range(2)]
        for block in range(L // TILE):
            rows = slice(block * TILE, (block + 1) * TILE)
            start = (L // TILE - 1 - block) * TILE
            query = q_s[rows, lanes]
            results = []
            for half in range(2):
                mine = low_row if half == 0 else jnp.logical_not(low_row)
                scores = dot_nt(jnp.where(mine, query, jnp.zeros_like(query)), keys)
                scores = scores + tiles[half][:, start : start + L]
                if stable:
                    scores = jnp.where(live, scores, MASKED)
                    scores = scores - jnp.max(scores, axis=1, keepdims=True)
                results.append(dot(jnp.exp(scores).astype(BF16), vx[pair]))
            top = jnp.where(low_row, results[0][:, :W], results[1][:, :W])
            total = jnp.where(low_row, results[0][:, W:], results[1][:, W:])
            ctx[rows, lanes] = (top / total).astype(BF16)

    copies[2].wait()
    copies[3].wait()
    table[...] = jnp.zeros_like(table)
    table[:H] = offset_table(buckets[...], rel[...])
    safe = bounded(q_s[...], k_s[...], table[...], HD, H)

    @pl.when(safe)
    def _():
        @pl.loop(0, H // 2, step=PAIRS)
        def _(first):
            for n in range(PAIRS):
                attend(first + n, False)

    @pl.when(jnp.logical_not(safe))
    def _():
        @pl.loop(0, H // 2)
        def _(pair):
            attend(pair, True)

    copies[7].wait()
    copies[8].wait()
    flow = x_ref[...].astype(F32) + dot(ctx[...], wo[...])
    stream[...] = flow
    scale = lax.rsqrt(jnp.mean(flow * flow, axis=1, keepdims=True) + EPS)
    normed[...] = (flow * scale * gain2_ref[...]).astype(BF16)
    copies[9].wait()
    copies[10].wait()
    for r in range(L // 256):
        part = slice(r * 256, (r + 1) * 256)
        for n in range(FF // 3072):
            cols = slice(n * 3072, (n + 1) * 3072)
            pre = dot(normed[part], w1[:, cols])
            inner[part, cols] = (pre * normal_cdf(pre)).astype(BF16)
        hidden_ref[part] = (stream[part] + dot(inner[part], w2[...])).astype(BF16)
    copies[11].wait()
    taps_ref[...] = dot_nt(wd[...], hidden_ref[...]).astype(BF16)


def backbone(*args):
    smem = pl.BlockSpec(memory_space=pltpu.SMEM)
    vmem = pl.BlockSpec(memory_space=pltpu.VMEM)
    hbm = pl.BlockSpec(memory_space=pl.ANY)
    fixed = pl.BlockSpec(memory_space=pltpu.HBM)
    return pl.pallas_call(
        backbone_kernel,
        out_shape=(
            jax.ShapeDtypeStruct((L, D), BF16),
            jax.ShapeDtypeStruct((DS, L), BF16),
        ),
        in_specs=[smem, smem] + [fixed] * 12,
        out_specs=(vmem, vmem),
        scratch_shapes=[
            pltpu.VMEM((H, NB), F32),
            pltpu.VMEM((1, OFFSETS), jnp.int32),
            pltpu.VMEM((L, D), BF16),
            pltpu.VMEM((1, D), F32),
            pltpu.VMEM((D, D), BF16),
            pltpu.VMEM((D, D), BF16),
            pltpu.VMEM((D, D), BF16),
            pltpu.VMEM((D, D), BF16),
            pltpu.VMEM((1, D), F32),
            pltpu.VMEM((D, FF), BF16),
            pltpu.VMEM((FF, D), BF16),
            pltpu.VMEM((DS, D), BF16),
            pltpu.SemaphoreType.DMA((12,)),
            pltpu.VMEM((L, D), BF16),
            pltpu.VMEM((L, D), BF16),
            pltpu.VMEM((L, D), BF16),
            pltpu.VMEM((H // 2, L, 2 * W), BF16),
            pltpu.VMEM((L, D), BF16),
            pltpu.VMEM((16, 2 * L), F32),
            pltpu.VMEM((L, D), F32),
            pltpu.VMEM((L, FF), BF16),
        ],
        compiler_params=pltpu.CompilerParams(vmem_limit_bytes=60 * 1024 * 1024),
        cost_estimate=pl.CostEstimate(
            flops=9_000_000_000, bytes_accessed=17_000_000, transcendentals=5_000_000
        ),
        name="backbone",
    )(*args)


DOWN0, QKV0, PROJ0, FFIN0, FFOUT0 = 0, 576, 864, 960, 1248
PACK = 1536
PART = PACK // 4


def place():
    index = lax.axis_index("dp")
    return lax.rem(index, 2), lax.rem(lax.div(index, 2), 2)


def column_norm(rows):
    return lax.rsqrt(jnp.mean(rows * rows, axis=0, keepdims=True) + EPS)


def norm_back(grad, unit, scale):
    return scale * (grad - unit * jnp.mean(grad * unit, axis=0, keepdims=True))


def head_sums(rows):
    return jnp.sum(rows.reshape(SH, SHD, L), axis=1)


def fill_heads(ref, rows, extra):
    for head in range(SH):
        mine = rows[head * SHD : (head + 1) * SHD]
        other = extra[head] if isinstance(extra, list) else extra
        ref[head] = jnp.concatenate([mine, other], axis=0).astype(BF16)


def side_kernel(count, lengths_ref, assign_ref, *rest):
    moved_hbm, rest = rest[:count], rest[count:]
    (
        taps_hbm, gate_hbm, gain1_hbm, gain2_hbm, wq_hbm, wk_hbm, wv_hbm, bucket_hbm, rel_hbm, wo_hbm, w1_hbm, w2_hbm,
        back_ref, tap_ref, rest_ref,
        taps, vectors, wq, wk, wv, buckets, rel, wo, w1, w2,
        moved, sems, table, probs, qt, kt, vt, dt, ctx, sums, dq, dk, dv, dall, diag, dtab,
    ) = rest
    rank = lax.axis_index("side")
    seq = assign_ref[rank]
    for step in range(count):

        @pl.when(lax.rem(rank + count - seq, count) == step)
        def _():
            pltpu.make_async_copy(moved_hbm[step], moved, sems.at[12]).start()

    pairs = (
        (taps_hbm, taps), (gate_hbm, vectors.at[0]), (gain1_hbm, vectors.at[1]), (gain2_hbm, vectors.at[2]),
        (wq_hbm, wq), (wk_hbm, wk), (wv_hbm, wv), (bucket_hbm, buckets.at[0]), (rel_hbm, rel), (wo_hbm, wo),
        (w1_hbm, w1), (w2_hbm, w2),
    )
    vectors[...] = jnp.zeros_like(vectors)
    copies = start_all(pairs, sems)
    length = lengths_ref[seq]
    row8 = lax.broadcasted_iota(jnp.int32, (SHD, L), 0)
    lane8 = lax.broadcasted_iota(jnp.int32, (SHD, L), 1)
    for copy in copies[:9]:
        copy.wait()
    table[...] = jnp.zeros_like(table)
    table[:SH] = offset_table(buckets[...], rel[...])
    eye = lax.broadcasted_iota(jnp.int32, (DS, DS), 0) == lax.broadcasted_iota(
        jnp.int32, (DS, DS), 1
    )
    columns = dot(eye.astype(F32), vectors[...], ((1,), (1,)), lax.Precision.HIGHEST)
    gate = jax.nn.sigmoid(columns[:, 0:1])
    gain1, gain2 = columns[:, 1:2], columns[:, 2:3]
    pltpu.make_async_copy(moved_hbm[0], moved, sems.at[12]).wait()
    tap = taps[...].astype(F32)
    old = moved[0].astype(F32)
    mixed = gate * tap + (1.0 - gate) * old
    scale1 = column_norm(mixed)
    unit1 = mixed * scale1
    normed1 = (unit1 * gain1).astype(BF16)
    query = dot_tn(wq[...], normed1).astype(BF16).astype(F32)
    key = dot_tn(wk[...], normed1).astype(BF16).astype(F32)
    value = dot_tn(wv[...], normed1)
    fill_heads(qt, query, jnp.where(row8 == 0, 1.0, 0.0))
    fill_heads(kt, key, jnp.where((row8 == 0) & (lane8 >= length), MASKED, 0.0))
    fill_heads(vt, value, jnp.where(row8 < 2, 1.0, 0.0))
    top = jnp.max(head_sums(query * query), axis=1) * jnp.max(head_sums(key * key), axis=1)
    safe = jnp.sqrt(jnp.max(top)) + jnp.max(jnp.abs(table[...])) < LIMIT
    blocks = [slice(b * TILE, (b + 1) * TILE) for b in range(L // TILE)]

    def rows8(head):
        return pl.ds(pl.multiple_of(head * SHD, SHD), SHD)

    def attend(head, stable):
        tile = toeplitz(table[pl.ds(head, 1)])
        for block, rows in enumerate(blocks):
            start = (L // TILE - 1 - block) * TILE
            scores = dot_tn(qt[head, :, rows], kt[head]) + tile[:, start : start + L]
            if stable:
                scores = scores - jnp.max(scores, axis=1, keepdims=True)
            probs[head, rows] = jnp.exp(scores).astype(BF16)
        both = dot_nt(vt[head], probs[head])
        ctx[rows8(head)] = both[:SHD]
        sums[rows8(head)] = jnp.broadcast_to(both[SHD : SHD + 1], (SHD, L))

    @pl.when(safe)
    def _():
        @pl.loop(0, SH, step=UNROLL)
        def _(first):
            for n in range(UNROLL):
                attend(first + n, False)

    @pl.when(jnp.logical_not(safe))
    def _():
        @pl.loop(0, SH)
        def _(head):
            attend(head, True)

    for copy in copies[9:12]:
        copy.wait()
    inverse = 1.0 / sums[...]
    context = ctx[...] * inverse
    context16 = context.astype(BF16)
    residual = mixed + dot_tn(wo[...], context16)
    scale2 = column_norm(residual)
    unit2 = residual * scale2
    normed2 = (unit2 * gain2).astype(BF16)
    pre = dot_tn(w1[...], normed2)
    cdf = normal_cdf(pre)
    inner = (pre * cdf).astype(BF16)
    back_ref[0] = (residual + dot(w2[...], inner)).astype(BF16)

    cotangent = moved[1]
    slope = cdf + pre * (jnp.exp(-0.5 * pre * pre) * (1.0 / math.sqrt(2.0 * math.pi)))
    d_pre = (dot_tn(w2[...], cotangent) * slope).astype(BF16)
    g_ffout = dot_nt(cotangent, inner)
    g_ffin = dot_nt(normed2, d_pre)
    for n in range(FS // W):
        for first, grad in ((FFIN0, g_ffin), (FFOUT0, g_ffout)):
            start = first - QKV0 + n * DS
            rest_ref[start : start + DS] = grad[:, n * W : (n + 1) * W].astype(BF16)
    dy = dot(w1[...], d_pre)
    g_gain2 = jnp.sum(dy * unit2, axis=1, keepdims=True)
    d_resid = cotangent.astype(F32) + norm_back(dy * gain2, unit2, scale2)
    d_attn = d_resid.astype(BF16)
    pad = jnp.zeros((W - DS, L), BF16)
    g_project = dot_nt(context16, jnp.concatenate([d_attn, pad], axis=0))
    d_context = dot(wo[...], d_attn).astype(BF16)
    d_scaled = (d_context.astype(F32) * inverse).astype(BF16).astype(F32)
    delta = head_sums(d_scaled * context)
    delta_hi = delta.astype(BF16).astype(F32)
    extra = []
    for head in range(SH):
        high, low = delta_hi[head : head + 1], (delta - delta_hi)[head : head + 1]
        extra.append(jnp.where(row8 == 0, -high, jnp.where(row8 == 1, -low, 0.0)))
    fill_heads(dt, d_scaled, extra)
    dtab[...] = jnp.zeros_like(dtab)

    def attend_back(head, spot):
        for block, rows in enumerate(blocks):
            grads = dot_tn(dt[head, :, rows], vt[head])
            dall[spot, rows] = (probs[head, rows].astype(F32) * grads).astype(BF16)
        dk[rows8(head)] = dot(qt[head], dall[spot])[:SHD]
        dv[rows8(head)] = dot(dt[head], probs[head])[:SHD]
        dq[rows8(head)] = dot_nt(kt[head], dall[spot])[:SHD]
        tiles = []
        for offset in range(2 * (L // TILE) - 1):
            total_tile = None
            for block, rows in enumerate(blocks):
                n = offset + block - (L // TILE - 1)
                if 0 <= n < L // TILE:
                    piece = dall[spot, rows, n * TILE : (n + 1) * TILE].astype(F32)
                    total_tile = piece if total_tile is None else total_tile + piece
            diag[spot, :, offset * TILE : (offset + 1) * TILE] = total_tile
        diag[spot, :, 2 * L - TILE :] = jnp.zeros((TILE, TILE), F32)
        back = 7 - lax.broadcasted_iota(jnp.int32, (8, 2 * L), 0)
        groups = [
            jnp.take_along_axis(diag[spot, g * 8 : g * 8 + 8], back, axis=0)
            for g in reversed(range(TILE // 8))
        ]
        rolled = pltpu.roll(jnp.concatenate(groups, axis=0), 0, 1, stride=1, stride_axis=0)
        dtab[pl.ds(head, 1)] = jnp.sum(rolled, axis=0, keepdims=True)

    @pl.loop(0, SH, step=UNROLL_BACK)
    def _(first):
        for n in range(UNROLL_BACK):
            attend_back(first + n, n)


    spots = lax.broadcasted_iota(jnp.int32, (W, OFFSETS), 0) - DS
    onehot = (spots == buckets[...]).astype(F32)
    g_rel = dot(dtab[:, :OFFSETS], onehot, ((1,), (1,)), lax.Precision.HIGHEST)
    grads = [ref[...].astype(BF16) for ref in (dq, dk, dv)]
    for n, grad in enumerate(grads):
        full = dot_nt(normed1, jnp.concatenate([grad, pad], axis=0))
        if n == 0:
            full = full + jnp.concatenate([g_rel, jnp.zeros((DS - 16, W), F32)], axis=0)
        rest_ref[n * DS : (n + 1) * DS] = full.astype(BF16)
    d_normed = dot(wq[...], grads[0]) + dot(wk[...], grads[1]) + dot(wv[...], grads[2])
    d_mixed = d_resid + norm_back(d_normed * gain1, unit1, scale1)
    back_ref[1] = ((1.0 - gate) * d_mixed).astype(BF16)
    tap_ref[...] = (gate * d_mixed).astype(BF16)
    g_gate = gate * (1.0 - gate) * jnp.sum(d_mixed * (tap - old), axis=1, keepdims=True)
    g_gain1 = jnp.sum(d_normed * unit1, axis=1, keepdims=True)
    lane = lax.broadcasted_iota(jnp.int32, (DS, W), 1)
    for n, grad in enumerate((g_gate, g_gain1, g_gain2)):
        g_project = jnp.where(lane == DS + n, grad, g_project)
    rest_ref[PROJ0 - QKV0 : PROJ0 - QKV0 + DS] = g_project.astype(BF16)


def pack_kernel(tap_ref, rest_ref, hidden_ref, keep_ref, send_ref, pack):
    down = dot(tap_ref[...], hidden_ref[...])
    for n in range(D // W):
        pack[n * DS : (n + 1) * DS] = down[:, n * W : (n + 1) * W].astype(BF16)
    pack[QKV0:] = rest_ref[...]
    core, across = place()
    for n in range(2):
        for ref, half in ((keep_ref, core), (send_ref, 1 - core)):
            start = (half * 2 + (across if n == 0 else 1 - across)) * PART
            ref[n] = pack[pl.ds(pl.multiple_of(start, PART), PART)]


def pack_grads(tap, rest, hidden):
    vmem = pl.BlockSpec(memory_space=pltpu.VMEM)
    return pl.pallas_call(
        pack_kernel,
        out_shape=(jax.ShapeDtypeStruct((2, PART, W), BF16),) * 2,
        in_specs=[vmem] * 3,
        out_specs=(vmem,) * 2,
        scratch_shapes=[pltpu.VMEM((PACK, W), BF16)],
        compiler_params=pltpu.CompilerParams(vmem_limit_bytes=8 * 1024 * 1024),
        cost_estimate=pl.CostEstimate(
            flops=80_000_000, bytes_accessed=2_000_000, transcendentals=0
        ),
        name="pack_grads",
    )(tap, rest, hidden)


def side_block(lengths, assign, moved, *args):
    smem = pl.BlockSpec(memory_space=pltpu.SMEM)
    vmem = pl.BlockSpec(memory_space=pltpu.VMEM)
    hbm = pl.BlockSpec(memory_space=pl.ANY)
    count = len(moved)
    return pl.pallas_call(
        functools.partial(side_kernel, count),
        out_shape=(
            jax.ShapeDtypeStruct((2, DS, L), BF16),
            jax.ShapeDtypeStruct((DS, L), BF16),
            jax.ShapeDtypeStruct((PACK - QKV0, W), BF16),
        ),
        in_specs=[smem, smem] + [hbm] * (count + len(args)),
        out_specs=(vmem,) * 3,
        scratch_shapes=[
            pltpu.VMEM((DS, L), BF16),
            pltpu.VMEM((8, DS), F32),
            pltpu.VMEM((DS, DS), BF16),
            pltpu.VMEM((DS, DS), BF16),
            pltpu.VMEM((DS, DS), BF16),
            pltpu.VMEM((1, OFFSETS), jnp.int32),
            pltpu.VMEM((SH, NB), F32),
            pltpu.VMEM((DS, DS), BF16),
            pltpu.VMEM((DS, FS), BF16),
            pltpu.VMEM((DS, FS), BF16),
            pltpu.VMEM((2, DS, L), BF16),
            pltpu.SemaphoreType.DMA((13,)),
            pltpu.VMEM((16, 2 * L), F32),
            pltpu.VMEM((SH, L, L), BF16),
            pltpu.VMEM((SH, 2 * SHD, L), BF16),
            pltpu.VMEM((SH, 2 * SHD, L), BF16),
            pltpu.VMEM((SH, 2 * SHD, L), BF16),
            pltpu.VMEM((SH, 2 * SHD, L), BF16),
            pltpu.VMEM((DS, L), F32),
            pltpu.VMEM((DS, L), F32),
            pltpu.VMEM((DS, L), F32),
            pltpu.VMEM((DS, L), F32),
            pltpu.VMEM((DS, L), F32),
            pltpu.VMEM((UNROLL_BACK, L, L), BF16),
            pltpu.VMEM((UNROLL_BACK, TILE, 2 * L), F32),
            pltpu.VMEM((16, 2 * L), F32),
        ],
        compiler_params=pltpu.CompilerParams(vmem_limit_bytes=VMEM_BYTES),
        cost_estimate=pl.CostEstimate(
            flops=9_000_000_000, bytes_accessed=4_000_000, transcendentals=5_000_000
        ),
        name="side_block",
    )(lengths, assign, *moved, *args)


def finish_kernel(count, assign_ref, *rest):
    quarters, rest = rest[:4], rest[4:]
    backs, results = rest[:count], rest[count : count + 13]
    part, out, *parts, sems = rest[count + 13 :]
    rank = lax.axis_index("side")
    core, across = place()
    spots = [
        2 * half + quarter for half in (core, 1 - core) for quarter in (across, 1 - across)
    ]
    masks = [0]
    for n in reversed(range(16)):
        if 1 << n < count:
            masks += [mask ^ (1 << n) for mask in masks]
    slot = jnp.int32(0)
    for n in range(count):
        slot = jnp.where(assign_ref[n] == rank, n, slot)
    gstate, down, gate, gain1, gq, gk, gv, go, rel, gain2, g1, g2 = parts
    for step in range(count):

        @pl.when((rank ^ slot) == masks[step])
        def _():
            out[...] = backs[step][0]
            gstate[...] = backs[step][1].astype(F32)

    targets = [out, *parts]
    pairs = [
        (ref.at[0] if ref.shape[0] == 1 else ref, result)
        for ref, result in zip(targets, results, strict=True)
    ]
    copies = [pltpu.make_async_copy(src, dst, sems.at[n]) for n, (src, dst) in enumerate(pairs)]
    copies[0].start()
    copies[1].start()
    for ref, spot in zip(quarters, spots, strict=True):
        part[spot] = ref[...]

    def take(start, stop):
        pieces = []
        for n in range(4):
            low, high = max(start, n * PART), min(stop, (n + 1) * PART)
            if low < high:
                pieces.append(part[n, low - n * PART : high - n * PART].astype(F32))
        return pieces[0] if len(pieces) == 1 else jnp.concatenate(pieces, axis=0)

    for n in range(D // W):
        down[:, n * W : (n + 1) * W] = take(DOWN0 + n * DS, DOWN0 + (n + 1) * DS)
    for n, ref in enumerate((gq, gk, gv)):
        ref[...] = take(QKV0 + n * DS, QKV0 + (n + 1) * DS)[:, :DS]
    rel[...] = take(QKV0, QKV0 + 16)[:SH, DS : DS + NB]
    project = take(PROJ0, PROJ0 + DS)
    go[...] = project[:, :DS]
    turned = project.T
    gate[...] = turned[DS : DS + 1]
    gain1[...] = turned[DS + 1 : DS + 2]
    gain2[...] = turned[DS + 2 : DS + 3]
    for n in range(FS // W):
        g1[:, n * W : (n + 1) * W] = take(FFIN0 + n * DS, FFIN0 + (n + 1) * DS)
        g2[:, n * W : (n + 1) * W] = take(FFOUT0 + n * DS, FFOUT0 + (n + 1) * DS)
    for copy in copies[2:]:
        copy.start()
    for copy in copies:
        copy.wait()


def finish(assign, quarters, backs):
    smem = pl.BlockSpec(memory_space=pltpu.SMEM)
    vmem = pl.BlockSpec(memory_space=pltpu.VMEM)
    hbm = pl.BlockSpec(memory_space=pl.ANY)
    fixed = pl.BlockSpec(memory_space=pltpu.HBM)
    count = len(backs)
    parts = [
        (DS, L), (DS, D), (1, DS), (1, DS), (DS, DS), (DS, DS), (DS, DS), (DS, DS), (SH, NB), (1, DS), (DS, FS), (DS, FS),
    ]
    shapes = [jax.ShapeDtypeStruct(p[1:] if p[0] == 1 else p, F32) for p in parts]
    return pl.pallas_call(
        functools.partial(finish_kernel, count),
        out_shape=(jax.ShapeDtypeStruct((DS, L), BF16), *shapes),
        in_specs=[smem] + [vmem] * (4 + count),
        out_specs=(hbm,) * 13,
        scratch_shapes=[
            pltpu.VMEM((4, PART, W), BF16),
            pltpu.VMEM((DS, L), BF16),
            *[pltpu.VMEM(p, F32) for p in parts],
            pltpu.SemaphoreType.DMA((13,)),
        ],
        compiler_params=pltpu.CompilerParams(vmem_limit_bytes=16 * 1024 * 1024),
        name="finish",
    )(assign, *quarters, *backs)


def swap(value, axis, bit):
    size = lax.axis_size(axis)
    return lax.ppermute(value, axis, [(i, i ^ bit) for i in range(size)])


def rotations(value):
    size = lax.axis_size("side")
    return [value] + [
        lax.ppermute(value, "side", [(i, (i + k) % size) for i in range(size)])
        for k in range(1, size)
    ]


def add(one, two):
    return (one.astype(F32) + two.astype(F32)).astype(BF16)


def bits(axis, first=0):
    return [1 << n for n in range(first, 16) if 1 << n < lax.axis_size(axis)]


def spread(blocks, bit):
    return blocks + [swap(block, "side", bit) for block in blocks]


def total(keep, send, back):
    levels = bits("side")[::-1]
    backs = spread([back], levels[0])
    got = swap(send, "dp", 1)
    mine = add(keep[0], got[0])
    across = swap(add(keep[1], got[1]), "dp", 2)
    mine = add(mine, across)
    mine = add(mine, swap(mine, "side", 1))
    mine, *backs = lax.optimization_barrier((mine, *backs))
    for bit in levels[1:]:
        backs = spread(backs, bit)
    for bit in bits("dp", 2):
        mine = add(mine, swap(mine, "dp", bit))
    for bit in bits("side", 1):
        mine = add(mine, swap(mine, "side", bit))
    across = swap(mine, "dp", 2)
    return (mine, across, swap(mine, "dp", 1), swap(across, "dp", 1)), backs


def shards(
    hidden_in, side_state, lengths, assign, buckets,
    backbone_gain_attn, backbone_query, backbone_key, backbone_value, backbone_project, backbone_rel,
    backbone_gain_ff, backbone_ff_in, backbone_ff_out, down_weight, gate_logit,
    side_gain_attn, side_query, side_key, side_value, side_project, side_rel,
    side_gain_ff, side_ff_in, side_ff_out, cotangent,
):
    moved = rotations(jnp.stack([side_state[0].T, cotangent[0].T]))
    hidden, taps = backbone(
        lengths, assign, backbone_rel.T, buckets, hidden_in[0], backbone_gain_attn,
        backbone_query, backbone_key, backbone_value, backbone_project, backbone_gain_ff,
        backbone_ff_in, backbone_ff_out, down_weight.T,
    )
    back, tap, rest = side_block(
        lengths, assign, moved, taps, gate_logit, side_gain_attn, side_gain_ff,
        side_query, side_key, side_value, buckets, side_rel.T, side_project, side_ff_in, side_ff_out.T,
    )
    keep, send = pack_grads(tap, rest, hidden)
    quarters, backs = total(keep, send, back)
    res = finish(assign, quarters, backs)
    out, gstate, down, gate, gain1, gq, gk, gv, go, rel, gain2, g1, g2 = res
    return (
        out.T[None], gstate.T[None], down.T, gate, gain1, gq, gk, gv, go, rel.T, gain2, g1, g2.T,
    )


def solution(mesh):
    rows = P(("dp", "side"), None, None)
    return jax.shard_map(
        shards,
        mesh=mesh,
        in_specs=(rows, rows, P("dp"), P("dp")) + (P(),) * 21 + (rows,),
        out_specs=(rows, rows) + (P(),) * 11,
        check_vma=False,
    )
```

```python
import functools
import math

import jax
import jax.numpy as jnp
from jax import lax
from jax.experimental import pallas as pl
from jax.experimental.pallas import tpu as pltpu
from jax.sharding import PartitionSpec as P

D = 768
H = 12
HD = 64
FF = 3072
NB = 32
DS = 96
SH = 12
SHD = 8
FS = 384
L = 512
W = 128
OFFSETS = 2 * L - 1
TILE = 128

EPS = 1e-06
MASKED = -1e9
LIMIT = 60.0
F32 = jnp.float32
BF16 = jnp.bfloat16
VMEM_BYTES = 44 * 1024 * 1024
UNROLL = 6
UNROLL_BACK = 6
PAIRS = 6


def dot(a, b, dims=((1,), (0,)), precision=None):
    return lax.dot_general(
        a, b, (dims, ((), ())), precision=precision, preferred_element_type=F32
    )


def dot_nt(a, b):
    return dot(a, b, ((1,), (1,)))


def dot_tn(a, b):
    return dot(a, b, ((0,), (0,)))


def normal_cdf(v):
    return 0.5 * (1.0 + lax.erf(v * (1.0 / math.sqrt(2.0))))


def offset_table(buckets, rel):
    rows = lax.broadcasted_iota(jnp.int32, (NB, OFFSETS), 0)
    onehot = (rows == buckets).astype(F32)
    table = dot(rel, onehot, precision=lax.Precision.HIGHEST)
    return jnp.concatenate([table, jnp.zeros((rel.shape[0], 1), F32)], axis=1)


def toeplitz(row):
    wide = jnp.broadcast_to(row, (TILE, 2 * L))
    return pltpu.roll(wide, 2 * L - (TILE - 1), 1, stride=1, stride_axis=0)


def bounded(q, k, table, size, heads):
    rows = lax.broadcasted_iota(jnp.int32, (q.shape[1], W), 0) // size
    cols = lax.broadcasted_iota(jnp.int32, (q.shape[1], W), 1)
    pick = ((rows == cols) & (rows < heads)).astype(BF16)
    qf, kf = q.astype(F32), k.astype(F32)
    qn = jnp.max(dot((qf * qf).astype(BF16), pick), axis=0, keepdims=True)
    kn = jnp.max(dot((kf * kf).astype(BF16), pick), axis=0, keepdims=True)
    top = jnp.max(jnp.sqrt(qn) * jnp.sqrt(kn)) * 1.02
    return top + jnp.max(jnp.abs(table)) < LIMIT


def start_all(pairs, sems):
    copies = [pltpu.make_async_copy(src, dst, sems.at[n]) for n, (src, dst) in enumerate(pairs)]
    for copy in copies:
        copy.start()
    return copies


def backbone_kernel(
    lengths_ref, assign_ref, rel_hbm, bucket_hbm, x_hbm, gain1_hbm, wq_hbm, wk_hbm, wv_hbm, wo_hbm, gain2_hbm, w1_hbm,
    w2_hbm, wd_hbm,
    hidden_ref, taps_ref,
    rel, buckets, x_ref, gain1_ref, wq, wk, wv, wo, gain2_ref, w1, w2, wd, sems,
    normed, q_s, k_s, vx, ctx, table, stream, inner,
):
    pairs = (
        (x_hbm, x_ref), (gain1_hbm, gain1_ref.at[0]), (rel_hbm, rel), (bucket_hbm, buckets.at[0]),
        (wq_hbm, wq), (wk_hbm, wk), (wv_hbm, wv), (wo_hbm, wo), (gain2_hbm, gain2_ref.at[0]),
        (w1_hbm, w1), (w2_hbm, w2), (wd_hbm, wd),
    )
    copies = [pltpu.make_async_copy(src, dst, sems.at[n]) for n, (src, dst) in enumerate(pairs)]
    for n in (0, 1, 4):
        copies[n].start()
    length = lengths_ref[assign_ref[lax.axis_index("side")]]
    copies[0].wait()
    copies[1].wait()
    for n in (5, 6, 2, 3):
        copies[n].start()
    x = x_ref[...].astype(F32)
    scale = lax.rsqrt(jnp.mean(x * x, axis=1, keepdims=True) + EPS)
    normed[...] = (x * scale * gain1_ref[...]).astype(BF16)
    copies[4].wait()
    copies[7].start()
    q_s[...] = dot(normed[...], wq[...]).astype(BF16)
    copies[5].wait()
    k_s[...] = dot(normed[...], wk[...]).astype(BF16)
    copies[6].wait()
    for n in (8, 9, 10, 11):
        copies[n].start()
    live_row = lax.broadcasted_iota(jnp.int32, (L, 1), 0) < length
    value = dot(normed[...], wv[...])
    value = jnp.where(live_row, value, 0.0).astype(BF16)
    ones = jnp.where(live_row, 1.0, 0.0).astype(BF16)
    for pair in range(H // 2):
        vx[pair, :, :W] = value[:, pair * W : (pair + 1) * W]
        vx[pair, :, W:] = jnp.broadcast_to(ones, (L, W))
    low_half = lax.broadcasted_iota(jnp.int32, (L, W), 1) < HD
    low_row = lax.broadcasted_iota(jnp.int32, (TILE, W), 1) < HD
    live = lax.broadcasted_iota(jnp.int32, (1, L), 1) < length

    def attend(pair, stable):
        lanes = pl.ds(pl.multiple_of(pair * W, W), W)
        keys = k_s[:, lanes]
        tiles = [toeplitz(table[pl.ds(pair * 2 + half, 1)]) for half in range(2)]
        for block in range(L // TILE):
            rows = slice(block * TILE, (block + 1) * TILE)
            start = (L // TILE - 1 - block) * TILE
            query = q_s[rows, lanes]
            results = []
            for half in range(2):
                mine = low_row if half == 0 else jnp.logical_not(low_row)
                scores = dot_nt(jnp.where(mine, query, jnp.zeros_like(query)), keys)
                scores = scores + tiles[half][:, start : start + L]
                if stable:
                    scores = jnp.where(live, scores, MASKED)
                    scores = scores - jnp.max(scores, axis=1, keepdims=True)
                results.append(dot(jnp.exp(scores).astype(BF16), vx[pair]))
            top = jnp.where(low_row, results[0][:, :W], results[1][:, :W])
            total = jnp.where(low_row, results[0][:, W:], results[1][:, W:])
            ctx[rows, lanes] = (top / total).astype(BF16)

    copies[2].wait()
    copies[3].wait()
    table[...] = jnp.zeros_like(table)
    table[:H] = offset_table(buckets[...], rel[...])
    safe = bounded(q_s[...], k_s[...], table[...], HD, H)

    @pl.when(safe)
    def _():
        @pl.loop(0, H // 2, step=PAIRS)
        def _(first):
            for n in range(PAIRS):
                attend(first + n, False)

    @pl.when(jnp.logical_not(safe))
    def _():
        @pl.loop(0, H // 2)
        def _(pair):
            attend(pair, True)

    copies[7].wait()
    copies[8].wait()
    flow = x_ref[...].astype(F32) + dot(ctx[...], wo[...])
    stream[...] = flow
    scale = lax.rsqrt(jnp.mean(flow * flow, axis=1, keepdims=True) + EPS)
    normed[...] = (flow * scale * gain2_ref[...]).astype(BF16)
    copies[9].wait()
    copies[10].wait()
    for r in range(L // 256):
        part = slice(r * 256, (r + 1) * 256)
        for n in range(FF // 3072):
            cols = slice(n * 3072, (n + 1) * 3072)
            pre = dot(normed[part], w1[:, cols])
            inner[part, cols] = (pre * normal_cdf(pre)).astype(BF16)
        hidden_ref[part] = (stream[part] + dot(inner[part], w2[...])).astype(BF16)
    copies[11].wait()
    taps_ref[...] = dot_nt(wd[...], hidden_ref[...]).astype(BF16)


def backbone(*args):
    smem = pl.BlockSpec(memory_space=pltpu.SMEM)
    vmem = pl.BlockSpec(memory_space=pltpu.VMEM)
    hbm = pl.BlockSpec(memory_space=pl.ANY)
    fixed = pl.BlockSpec(memory_space=pltpu.HBM)
    return pl.pallas_call(
        backbone_kernel,
        out_shape=(
            pltpu.VMEM((L, D), BF16),
            pltpu.VMEM((DS, L), BF16),
        ),
        in_specs=[smem, smem] + [fixed] * 12,
        out_specs=(vmem, vmem),
        scratch_shapes=[
            pltpu.VMEM((H, NB), F32),
            pltpu.VMEM((1, OFFSETS), jnp.int32),
            pltpu.VMEM((L, D), BF16),
            pltpu.VMEM((1, D), F32),
            pltpu.VMEM((D, D), BF16),
            pltpu.VMEM((D, D), BF16),
            pltpu.VMEM((D, D), BF16),
            pltpu.VMEM((D, D), BF16),
            pltpu.VMEM((1, D), F32),
            pltpu.VMEM((D, FF), BF16),
            pltpu.VMEM((FF, D), BF16),
            pltpu.VMEM((DS, D), BF16),
            pltpu.SemaphoreType.DMA((12,)),
            pltpu.VMEM((L, D), BF16),
            pltpu.VMEM((L, D), BF16),
            pltpu.VMEM((L, D), BF16),
            pltpu.VMEM((H // 2, L, 2 * W), BF16),
            pltpu.VMEM((L, D), BF16),
            pltpu.VMEM((16, 2 * L), F32),
            pltpu.VMEM((L, D), F32),
            pltpu.VMEM((L, FF), BF16),
        ],
        compiler_params=pltpu.CompilerParams(vmem_limit_bytes=60 * 1024 * 1024),
        cost_estimate=pl.CostEstimate(
            flops=9_000_000_000, bytes_accessed=17_000_000, transcendentals=5_000_000
        ),
        name="backbone",
    )(*args)


DOWN0, QKV0, PROJ0, FFIN0, FFOUT0 = 0, 576, 864, 960, 1248
PACK = 1536
PART = PACK // 4


def place():
    index = lax.axis_index("dp")
    return lax.rem(index, 2), lax.rem(lax.div(index, 2), 2)


def column_norm(rows):
    return lax.rsqrt(jnp.mean(rows * rows, axis=0, keepdims=True) + EPS)


def norm_back(grad, unit, scale):
    return scale * (grad - unit * jnp.mean(grad * unit, axis=0, keepdims=True))


def head_sums(rows):
    return jnp.sum(rows.reshape(SH, SHD, L), axis=1)


def fill_heads(ref, rows, extra):
    for head in range(SH):
        mine = rows[head * SHD : (head + 1) * SHD]
        other = extra[head] if isinstance(extra, list) else extra
        ref[head] = jnp.concatenate([mine, other], axis=0).astype(BF16)


def side_kernel(count, lengths_ref, assign_ref, *rest):
    moved_hbm, rest = rest[:count], rest[count:]
    (
        taps_hbm, gate_hbm, gain1_hbm, gain2_hbm, wq_hbm, wk_hbm, wv_hbm, bucket_hbm, rel_hbm, wo_hbm, w1_hbm, w2_hbm,
        back_ref, tap_ref, rest_ref,
        taps, vectors, wq, wk, wv, buckets, rel, wo, w1, w2,
        moved, sems, table, probs, qt, kt, vt, dt, ctx, sums, dq, dk, dv, dall, diag, dtab,
    ) = rest
    rank = lax.axis_index("side")
    seq = assign_ref[rank]
    for step in range(count):

        @pl.when(lax.rem(rank + count - seq, count) == step)
        def _():
            pltpu.make_async_copy(moved_hbm[step], moved, sems.at[12]).start()

    pairs = (
        (taps_hbm, taps), (gate_hbm, vectors.at[0]), (gain1_hbm, vectors.at[1]), (gain2_hbm, vectors.at[2]),
        (wq_hbm, wq), (wk_hbm, wk), (wv_hbm, wv), (bucket_hbm, buckets.at[0]), (rel_hbm, rel), (wo_hbm, wo),
        (w1_hbm, w1), (w2_hbm, w2),
    )
    vectors[...] = jnp.zeros_like(vectors)
    copies = start_all(pairs, sems)
    length = lengths_ref[seq]
    row8 = lax.broadcasted_iota(jnp.int32, (SHD, L), 0)
    lane8 = lax.broadcasted_iota(jnp.int32, (SHD, L), 1)
    for copy in copies[:9]:
        copy.wait()
    table[...] = jnp.zeros_like(table)
    table[:SH] = offset_table(buckets[...], rel[...])
    eye = lax.broadcasted_iota(jnp.int32, (DS, DS), 0) == lax.broadcasted_iota(
        jnp.int32, (DS, DS), 1
    )
    columns = dot(eye.astype(F32), vectors[...], ((1,), (1,)), lax.Precision.HIGHEST)
    gate = jax.nn.sigmoid(columns[:, 0:1])
    gain1, gain2 = columns[:, 1:2], columns[:, 2:3]
    pltpu.make_async_copy(moved_hbm[0], moved, sems.at[12]).wait()
    tap = taps[...].astype(F32)
    old = moved[0].astype(F32)
    mixed = gate * tap + (1.0 - gate) * old
    scale1 = column_norm(mixed)
    unit1 = mixed * scale1
    normed1 = (unit1 * gain1).astype(BF16)
    query = dot_tn(wq[...], normed1).astype(BF16).astype(F32)
    key = dot_tn(wk[...], normed1).astype(BF16).astype(F32)
    value = dot_tn(wv[...], normed1)
    fill_heads(qt, query, jnp.where(row8 == 0, 1.0, 0.0))
    fill_heads(kt, key, jnp.where((row8 == 0) & (lane8 >= length), MASKED, 0.0))
    fill_heads(vt, value, jnp.where(row8 < 2, 1.0, 0.0))
    top = jnp.max(head_sums(query * query), axis=1) * jnp.max(head_sums(key * key), axis=1)
    safe = jnp.sqrt(jnp.max(top)) + jnp.max(jnp.abs(table[...])) < LIMIT
    blocks = [slice(b * TILE, (b + 1) * TILE) for b in range(L // TILE)]

    def rows8(head):
        return pl.ds(pl.multiple_of(head * SHD, SHD), SHD)

    def attend(head, stable):
        tile = toeplitz(table[pl.ds(head, 1)])
        for block, rows in enumerate(blocks):
            start = (L // TILE - 1 - block) * TILE
            scores = dot_tn(qt[head, :, rows], kt[head]) + tile[:, start : start + L]
            if stable:
                scores = scores - jnp.max(scores, axis=1, keepdims=True)
            probs[head, rows] = jnp.exp(scores).astype(BF16)
        both = dot_nt(vt[head], probs[head])
        ctx[rows8(head)] = both[:SHD]
        sums[rows8(head)] = jnp.broadcast_to(both[SHD : SHD + 1], (SHD, L))

    @pl.when(safe)
    def _():
        @pl.loop(0, SH, step=UNROLL)
        def _(first):
            for n in range(UNROLL):
                attend(first + n, False)

    @pl.when(jnp.logical_not(safe))
    def _():
        @pl.loop(0, SH)
        def _(head):
            attend(head, True)

    for copy in copies[9:12]:
        copy.wait()
    inverse = 1.0 / sums[...]
    context = ctx[...] * inverse
    context16 = context.astype(BF16)
    residual = mixed + dot_tn(wo[...], context16)
    scale2 = column_norm(residual)
    unit2 = residual * scale2
    normed2 = (unit2 * gain2).astype(BF16)
    pre = dot_tn(w1[...], normed2)
    cdf = normal_cdf(pre)
    inner = (pre * cdf).astype(BF16)
    back_ref[0] = (residual + dot(w2[...], inner)).astype(BF16)

    cotangent = moved[1]
    slope = cdf + pre * (jnp.exp(-0.5 * pre * pre) * (1.0 / math.sqrt(2.0 * math.pi)))
    d_pre = (dot_tn(w2[...], cotangent) * slope).astype(BF16)
    g_ffout = dot_nt(cotangent, inner)
    g_ffin = dot_nt(normed2, d_pre)
    for n in range(FS // W):
        for first, grad in ((FFIN0, g_ffin), (FFOUT0, g_ffout)):
            start = first - QKV0 + n * DS
            rest_ref[start : start + DS] = grad[:, n * W : (n + 1) * W].astype(BF16)
    dy = dot(w1[...], d_pre)
    g_gain2 = jnp.sum(dy * unit2, axis=1, keepdims=True)
    d_resid = cotangent.astype(F32) + norm_back(dy * gain2, unit2, scale2)
    d_attn = d_resid.astype(BF16)
    pad = jnp.zeros((W - DS, L), BF16)
    g_project = dot_nt(context16, jnp.concatenate([d_attn, pad], axis=0))
    d_context = dot(wo[...], d_attn).astype(BF16)
    d_scaled = (d_context.astype(F32) * inverse).astype(BF16).astype(F32)
    delta = head_sums(d_scaled * context)
    delta_hi = delta.astype(BF16).astype(F32)
    extra = []
    for head in range(SH):
        high, low = delta_hi[head : head + 1], (delta - delta_hi)[head : head + 1]
        extra.append(jnp.where(row8 == 0, -high, jnp.where(row8 == 1, -low, 0.0)))
    fill_heads(dt, d_scaled, extra)
    dtab[...] = jnp.zeros_like(dtab)

    def attend_back(head, spot):
        for block, rows in enumerate(blocks):
            grads = dot_tn(dt[head, :, rows], vt[head])
            dall[spot, rows] = (probs[head, rows].astype(F32) * grads).astype(BF16)
        dk[rows8(head)] = dot(qt[head], dall[spot])[:SHD]
        dv[rows8(head)] = dot(dt[head], probs[head])[:SHD]
        dq[rows8(head)] = dot_nt(kt[head], dall[spot])[:SHD]
        tiles = []
        for offset in range(2 * (L // TILE) - 1):
            total_tile = None
            for block, rows in enumerate(blocks):
                n = offset + block - (L // TILE - 1)
                if 0 <= n < L // TILE:
                    piece = dall[spot, rows, n * TILE : (n + 1) * TILE].astype(F32)
                    total_tile = piece if total_tile is None else total_tile + piece
            diag[spot, :, offset * TILE : (offset + 1) * TILE] = total_tile
        diag[spot, :, 2 * L - TILE :] = jnp.zeros((TILE, TILE), F32)
        back = 7 - lax.broadcasted_iota(jnp.int32, (8, 2 * L), 0)
        groups = [
            jnp.take_along_axis(diag[spot, g * 8 : g * 8 + 8], back, axis=0)
            for g in reversed(range(TILE // 8))
        ]
        rolled = pltpu.roll(jnp.concatenate(groups, axis=0), 0, 1, stride=1, stride_axis=0)
        dtab[pl.ds(head, 1)] = jnp.sum(rolled, axis=0, keepdims=True)

    @pl.loop(0, SH, step=UNROLL_BACK)
    def _(first):
        for n in range(UNROLL_BACK):
            attend_back(first + n, n)


    spots = lax.broadcasted_iota(jnp.int32, (W, OFFSETS), 0) - DS
    onehot = (spots == buckets[...]).astype(F32)
    g_rel = dot(dtab[:, :OFFSETS], onehot, ((1,), (1,)), lax.Precision.HIGHEST)
    grads = [ref[...].astype(BF16) for ref in (dq, dk, dv)]
    for n, grad in enumerate(grads):
        full = dot_nt(normed1, jnp.concatenate([grad, pad], axis=0))
        if n == 0:
            full = full + jnp.concatenate([g_rel, jnp.zeros((DS - 16, W), F32)], axis=0)
        rest_ref[n * DS : (n + 1) * DS] = full.astype(BF16)
    d_normed = dot(wq[...], grads[0]) + dot(wk[...], grads[1]) + dot(wv[...], grads[2])
    d_mixed = d_resid + norm_back(d_normed * gain1, unit1, scale1)
    back_ref[1] = ((1.0 - gate) * d_mixed).astype(BF16)
    tap_ref[...] = (gate * d_mixed).astype(BF16)
    g_gate = gate * (1.0 - gate) * jnp.sum(d_mixed * (tap - old), axis=1, keepdims=True)
    g_gain1 = jnp.sum(d_normed * unit1, axis=1, keepdims=True)
    lane = lax.broadcasted_iota(jnp.int32, (DS, W), 1)
    for n, grad in enumerate((g_gate, g_gain1, g_gain2)):
        g_project = jnp.where(lane == DS + n, grad, g_project)
    rest_ref[PROJ0 - QKV0 : PROJ0 - QKV0 + DS] = g_project.astype(BF16)


def pack_kernel(tap_ref, rest_ref, hidden_ref, keep_ref, send_ref, pack):
    down = dot(tap_ref[...], hidden_ref[...])
    for n in range(D // W):
        pack[n * DS : (n + 1) * DS] = down[:, n * W : (n + 1) * W].astype(BF16)
    pack[QKV0:] = rest_ref[...]
    core, across = place()
    for n in range(2):
        for ref, half in ((keep_ref, core), (send_ref, 1 - core)):
            start = (half * 2 + (across if n == 0 else 1 - across)) * PART
            ref[n] = pack[pl.ds(pl.multiple_of(start, PART), PART)]


def pack_grads(tap, rest, hidden):
    vmem = pl.BlockSpec(memory_space=pltpu.VMEM)
    return pl.pallas_call(
        pack_kernel,
        out_shape=(jax.ShapeDtypeStruct((2, PART, W), BF16),) * 2,
        in_specs=[vmem] * 3,
        out_specs=(vmem,) * 2,
        scratch_shapes=[pltpu.VMEM((PACK, W), BF16)],
        compiler_params=pltpu.CompilerParams(vmem_limit_bytes=8 * 1024 * 1024),
        cost_estimate=pl.CostEstimate(
            flops=80_000_000, bytes_accessed=2_000_000, transcendentals=0
        ),
        name="pack_grads",
    )(tap, rest, hidden)


def side_block(lengths, assign, moved, *args):
    smem = pl.BlockSpec(memory_space=pltpu.SMEM)
    vmem = pl.BlockSpec(memory_space=pltpu.VMEM)
    hbm = pl.BlockSpec(memory_space=pl.ANY)
    count = len(moved)
    return pl.pallas_call(
        functools.partial(side_kernel, count),
        out_shape=(
            jax.ShapeDtypeStruct((2, DS, L), BF16),
            jax.ShapeDtypeStruct((DS, L), BF16),
            jax.ShapeDtypeStruct((PACK - QKV0, W), BF16),
        ),
        in_specs=[smem, smem] + [hbm] * (count + len(args)),
        out_specs=(vmem,) * 3,
        scratch_shapes=[
            pltpu.VMEM((DS, L), BF16),
            pltpu.VMEM((8, DS), F32),
            pltpu.VMEM((DS, DS), BF16),
            pltpu.VMEM((DS, DS), BF16),
            pltpu.VMEM((DS, DS), BF16),
            pltpu.VMEM((1, OFFSETS), jnp.int32),
            pltpu.VMEM((SH, NB), F32),
            pltpu.VMEM((DS, DS), BF16),
            pltpu.VMEM((DS, FS), BF16),
            pltpu.VMEM((DS, FS), BF16),
            pltpu.VMEM((2, DS, L), BF16),
            pltpu.SemaphoreType.DMA((13,)),
            pltpu.VMEM((16, 2 * L), F32),
            pltpu.VMEM((SH, L, L), BF16),
            pltpu.VMEM((SH, 2 * SHD, L), BF16),
            pltpu.VMEM((SH, 2 * SHD, L), BF16),
            pltpu.VMEM((SH, 2 * SHD, L), BF16),
            pltpu.VMEM((SH, 2 * SHD, L), BF16),
            pltpu.VMEM((DS, L), F32),
            pltpu.VMEM((DS, L), F32),
            pltpu.VMEM((DS, L), F32),
            pltpu.VMEM((DS, L), F32),
            pltpu.VMEM((DS, L), F32),
            pltpu.VMEM((UNROLL_BACK, L, L), BF16),
            pltpu.VMEM((UNROLL_BACK, TILE, 2 * L), F32),
            pltpu.VMEM((16, 2 * L), F32),
        ],
        compiler_params=pltpu.CompilerParams(vmem_limit_bytes=VMEM_BYTES),
        cost_estimate=pl.CostEstimate(
            flops=9_000_000_000, bytes_accessed=4_000_000, transcendentals=5_000_000
        ),
        name="side_block",
    )(lengths, assign, *moved, *args)


def finish_kernel(count, assign_ref, *rest):
    quarters, rest = rest[:4], rest[4:]
    backs, results = rest[:count], rest[count : count + 13]
    part, out, *parts, sems = rest[count + 13 :]
    rank = lax.axis_index("side")
    core, across = place()
    spots = [
        2 * half + quarter for half in (core, 1 - core) for quarter in (across, 1 - across)
    ]
    masks = [0]
    for n in reversed(range(16)):
        if 1 << n < count:
            masks += [mask ^ (1 << n) for mask in masks]
    slot = jnp.int32(0)
    for n in range(count):
        slot = jnp.where(assign_ref[n] == rank, n, slot)
    gstate, down, gate, gain1, gq, gk, gv, go, rel, gain2, g1, g2 = parts
    for step in range(count):

        @pl.when((rank ^ slot) == masks[step])
        def _():
            out[...] = backs[step][0]
            gstate[...] = backs[step][1].astype(F32)

    targets = [out, *parts]
    pairs = [
        (ref.at[0] if ref.shape[0] == 1 else ref, result)
        for ref, result in zip(targets, results, strict=True)
    ]
    copies = [pltpu.make_async_copy(src, dst, sems.at[n]) for n, (src, dst) in enumerate(pairs)]
    copies[0].start()
    copies[1].start()
    for ref, spot in zip(quarters, spots, strict=True):
        part[spot] = ref[...]

    def take(start, stop):
        pieces = []
        for n in range(4):
            low, high = max(start, n * PART), min(stop, (n + 1) * PART)
            if low < high:
                pieces.append(part[n, low - n * PART : high - n * PART].astype(F32))
        return pieces[0] if len(pieces) == 1 else jnp.concatenate(pieces, axis=0)

    for n in range(D // W):
        down[:, n * W : (n + 1) * W] = take(DOWN0 + n * DS, DOWN0 + (n + 1) * DS)
    for n, ref in enumerate((gq, gk, gv)):
        ref[...] = take(QKV0 + n * DS, QKV0 + (n + 1) * DS)[:, :DS]
    rel[...] = take(QKV0, QKV0 + 16)[:SH, DS : DS + NB]
    project = take(PROJ0, PROJ0 + DS)
    go[...] = project[:, :DS]
    turned = project.T
    gate[...] = turned[DS : DS + 1]
    gain1[...] = turned[DS + 1 : DS + 2]
    gain2[...] = turned[DS + 2 : DS + 3]
    for n in range(FS // W):
        g1[:, n * W : (n + 1) * W] = take(FFIN0 + n * DS, FFIN0 + (n + 1) * DS)
        g2[:, n * W : (n + 1) * W] = take(FFOUT0 + n * DS, FFOUT0 + (n + 1) * DS)
    for copy in copies[2:]:
        copy.start()
    for copy in copies:
        copy.wait()


def finish(assign, quarters, backs):
    smem = pl.BlockSpec(memory_space=pltpu.SMEM)
    vmem = pl.BlockSpec(memory_space=pltpu.VMEM)
    hbm = pl.BlockSpec(memory_space=pl.ANY)
    fixed = pl.BlockSpec(memory_space=pltpu.HBM)
    count = len(backs)
    parts = [
        (DS, L), (DS, D), (1, DS), (1, DS), (DS, DS), (DS, DS), (DS, DS), (DS, DS), (SH, NB), (1, DS), (DS, FS), (DS, FS),
    ]
    shapes = [jax.ShapeDtypeStruct(p[1:] if p[0] == 1 else p, F32) for p in parts]
    return pl.pallas_call(
        functools.partial(finish_kernel, count),
        out_shape=(jax.ShapeDtypeStruct((DS, L), BF16), *shapes),
        in_specs=[smem] + [vmem] * (4 + count),
        out_specs=(hbm,) * 13,
        scratch_shapes=[
            pltpu.VMEM((4, PART, W), BF16),
            pltpu.VMEM((DS, L), BF16),
            *[pltpu.VMEM(p, F32) for p in parts],
            pltpu.SemaphoreType.DMA((13,)),
        ],
        compiler_params=pltpu.CompilerParams(vmem_limit_bytes=16 * 1024 * 1024),
        name="finish",
    )(assign, *quarters, *backs)


def swap(value, axis, bit):
    size = lax.axis_size(axis)
    return lax.ppermute(value, axis, [(i, i ^ bit) for i in range(size)])


def rotations(value):
    size = lax.axis_size("side")
    return [value] + [
        lax.ppermute(value, "side", [(i, (i + k) % size) for i in range(size)])
        for k in range(1, size)
    ]


def add(one, two):
    return (one.astype(F32) + two.astype(F32)).astype(BF16)


def bits(axis, first=0):
    return [1 << n for n in range(first, 16) if 1 << n < lax.axis_size(axis)]


def spread(blocks, bit):
    return blocks + [swap(block, "side", bit) for block in blocks]


def settle_kernel(_, out_ref):
    del out_ref


def settle(block):
    hbm = pl.BlockSpec(memory_space=pl.ANY)
    return pl.pallas_call(
        settle_kernel,
        out_shape=jax.ShapeDtypeStruct(block.shape, block.dtype),
        in_specs=[hbm],
        out_specs=hbm,
        input_output_aliases={0: 0},
        cost_estimate=pl.CostEstimate(flops=1000000000, bytes_accessed=0, transcendentals=0),
        compiler_params=pltpu.CompilerParams(vmem_limit_bytes=1024 * 1024),
        name="settle",
    )(block)


def total(keep, send, back):
    levels = bits("side")[::-1]
    backs = spread([back], levels[0])
    got = swap(send, "dp", 1)
    mine = add(keep[0], got[0])
    across = swap(add(keep[1], got[1]), "dp", 2)
    mine = add(mine, across)
    mine = add(mine, swap(mine, "side", 1))
    mine, backs[1] = lax.optimization_barrier((mine, settle(backs[1])))
    for bit in levels[1:]:
        backs = spread(backs, bit)
    for bit in bits("dp", 2):
        mine = add(mine, swap(mine, "dp", bit))
    for bit in bits("side", 1):
        mine = add(mine, swap(mine, "side", bit))
    across = swap(mine, "dp", 2)
    return (mine, across, swap(mine, "dp", 1), swap(across, "dp", 1)), backs


def shards(
    hidden_in, side_state, lengths, assign, buckets,
    backbone_gain_attn, backbone_query, backbone_key, backbone_value, backbone_project, backbone_rel,
    backbone_gain_ff, backbone_ff_in, backbone_ff_out, down_weight, gate_logit,
    side_gain_attn, side_query, side_key, side_value, side_project, side_rel,
    side_gain_ff, side_ff_in, side_ff_out, cotangent,
):
    moved = rotations(jnp.stack([side_state[0].T, cotangent[0].T]))
    hidden, taps = backbone(
        lengths, assign, backbone_rel.T, buckets, hidden_in[0], backbone_gain_attn,
        backbone_query, backbone_key, backbone_value, backbone_project, backbone_gain_ff,
        backbone_ff_in, backbone_ff_out, down_weight.T,
    )
    back, tap, rest = side_block(
        lengths, assign, moved, taps, gate_logit, side_gain_attn, side_gain_ff,
        side_query, side_key, side_value, buckets, side_rel.T, side_project, side_ff_in, side_ff_out.T,
    )
    keep, send = pack_grads(tap, rest, hidden)
    quarters, backs = total(keep, send, back)
    res = finish(assign, quarters, backs)
    out, gstate, down, gate, gain1, gq, gk, gv, go, rel, gain2, g1, g2 = res
    return (
        out.T[None], gstate.T[None], down.T, gate, gain1, gq, gk, gv, go, rel.T, gain2, g1, g2.T,
    )


def solution(mesh):
    rows = P(("dp", "side"), None, None)
    return jax.shard_map(
        shards,
        mesh=mesh,
        in_specs=(rows, rows, P("dp"), P("dp")) + (P(),) * 21 + (rows,),
        out_specs=(rows, rows) + (P(),) * 11,
        check_vma=False,
    )
```

```python
import functools
import math

import jax
import jax.numpy as jnp
from jax import lax
from jax.experimental import pallas as pl
from jax.experimental.pallas import tpu as pltpu
from jax.sharding import PartitionSpec as P

D = 768
H = 12
HD = 64
FF = 3072
NB = 32
DS = 96
SH = 12
SHD = 8
FS = 384
L = 512
W = 128
OFFSETS = 2 * L - 1
TILE = 128

EPS = 1e-06
MASKED = -1e9
LIMIT = 60.0
F32 = jnp.float32
BF16 = jnp.bfloat16
VMEM_BYTES = 44 * 1024 * 1024
UNROLL = 12
UNROLL_BACK = 12
PAIRS = 6


def dot(a, b, dims=((1,), (0,)), precision=None):
    return lax.dot_general(
        a, b, (dims, ((), ())), precision=precision, preferred_element_type=F32
    )


def dot_nt(a, b):
    return dot(a, b, ((1,), (1,)))


def dot_tn(a, b):
    return dot(a, b, ((0,), (0,)))


def normal_cdf(v):
    return 0.5 * (1.0 + lax.erf(v * (1.0 / math.sqrt(2.0))))


def offset_table(buckets, rel):
    rows = lax.broadcasted_iota(jnp.int32, (NB, OFFSETS), 0)
    onehot = (rows == buckets).astype(F32)
    table = dot(rel, onehot, precision=lax.Precision.HIGHEST)
    return jnp.concatenate([table, jnp.zeros((rel.shape[0], 1), F32)], axis=1)


def toeplitz(row):
    wide = jnp.broadcast_to(row, (TILE, 2 * L))
    return pltpu.roll(wide, 2 * L - (TILE - 1), 1, stride=1, stride_axis=0)


def bounded(q, k, table, size, heads):
    rows = lax.broadcasted_iota(jnp.int32, (q.shape[1], W), 0) // size
    cols = lax.broadcasted_iota(jnp.int32, (q.shape[1], W), 1)
    pick = ((rows == cols) & (rows < heads)).astype(BF16)
    qf, kf = q.astype(F32), k.astype(F32)
    qn = jnp.max(dot((qf * qf).astype(BF16), pick), axis=0, keepdims=True)
    kn = jnp.max(dot((kf * kf).astype(BF16), pick), axis=0, keepdims=True)
    top = jnp.max(jnp.sqrt(qn) * jnp.sqrt(kn)) * 1.02
    return top + jnp.max(jnp.abs(table)) < LIMIT


def start_all(pairs, sems):
    copies = [pltpu.make_async_copy(src, dst, sems.at[n]) for n, (src, dst) in enumerate(pairs)]
    for copy in copies:
        copy.start()
    return copies


def backbone_kernel(
    lengths_ref, assign_ref, rel_hbm, bucket_hbm, x_hbm, gain1_hbm, wq_hbm, wk_hbm, wv_hbm, wo_hbm, gain2_hbm, w1_hbm,
    w2_hbm, wd_hbm,
    hidden_ref, taps_ref,
    rel, buckets, x_ref, gain1_ref, wq, wk, wv, wo, gain2_ref, w1, w2, wd, sems,
    normed, q_s, k_s, vx, ctx, table, stream, inner,
):
    pairs = (
        (x_hbm, x_ref), (gain1_hbm, gain1_ref.at[0]), (rel_hbm, rel), (bucket_hbm, buckets.at[0]),
        (wq_hbm, wq), (wk_hbm, wk), (wv_hbm, wv), (wo_hbm, wo), (gain2_hbm, gain2_ref.at[0]),
        (w1_hbm, w1), (w2_hbm, w2), (wd_hbm, wd),
    )
    copies = [pltpu.make_async_copy(src, dst, sems.at[n]) for n, (src, dst) in enumerate(pairs)]
    for n in (2, 3, 0, 1, 4):
        copies[n].start()
    length = lengths_ref[assign_ref[lax.axis_index("side")]]
    copies[2].wait()
    copies[3].wait()
    table[...] = jnp.zeros_like(table)
    table[:H] = offset_table(buckets[...], rel[...])
    copies[0].wait()
    copies[1].wait()
    for n in (5, 6):
        copies[n].start()
    x = x_ref[...].astype(F32)
    scale = lax.rsqrt(jnp.mean(x * x, axis=1, keepdims=True) + EPS)
    normed[...] = (x * scale * gain1_ref[...]).astype(BF16)
    copies[4].wait()
    copies[7].start()
    q_s[...] = dot(normed[...], wq[...]).astype(BF16)
    copies[5].wait()
    k_s[...] = dot(normed[...], wk[...]).astype(BF16)
    copies[6].wait()
    for n in (8, 9, 10, 11):
        copies[n].start()
    live_row = lax.broadcasted_iota(jnp.int32, (L, 1), 0) < length
    value = dot(normed[...], wv[...])
    value = jnp.where(live_row, value, 0.0).astype(BF16)
    ones = jnp.where(live_row, 1.0, 0.0).astype(BF16)
    for pair in range(H // 2):
        vx[pair, :, :W] = value[:, pair * W : (pair + 1) * W]
        vx[pair, :, W:] = jnp.broadcast_to(ones, (L, W))
    low_half = lax.broadcasted_iota(jnp.int32, (L, W), 1) < HD
    low_row = lax.broadcasted_iota(jnp.int32, (TILE, W), 1) < HD
    live = lax.broadcasted_iota(jnp.int32, (1, L), 1) < length

    def attend(pair, stable):
        lanes = pl.ds(pl.multiple_of(pair * W, W), W)
        keys = k_s[:, lanes]
        tiles = [toeplitz(table[pl.ds(pair * 2 + half, 1)]) for half in range(2)]
        for block in range(L // TILE):
            rows = slice(block * TILE, (block + 1) * TILE)
            start = (L // TILE - 1 - block) * TILE
            query = q_s[rows, lanes]
            results = []
            for half in range(2):
                mine = low_row if half == 0 else jnp.logical_not(low_row)
                scores = dot_nt(jnp.where(mine, query, jnp.zeros_like(query)), keys)
                scores = scores + tiles[half][:, start : start + L]
                if stable:
                    scores = jnp.where(live, scores, MASKED)
                    scores = scores - jnp.max(scores, axis=1, keepdims=True)
                results.append(dot(jnp.exp(scores).astype(BF16), vx[pair]))
            top = jnp.where(low_row, results[0][:, :W], results[1][:, :W])
            total = jnp.where(low_row, results[0][:, W:], results[1][:, W:])
            ctx[rows, lanes] = (top / total).astype(BF16)

    safe = bounded(q_s[...], k_s[...], table[...], HD, H)

    @pl.when(safe)
    def _():
        @pl.loop(0, H // 2, step=PAIRS)
        def _(first):
            for n in range(PAIRS):
                attend(first + n, False)

    @pl.when(jnp.logical_not(safe))
    def _():
        @pl.loop(0, H // 2)
        def _(pair):
            attend(pair, True)

    copies[7].wait()
    copies[8].wait()
    flow = x_ref[...].astype(F32) + dot(ctx[...], wo[...])
    stream[...] = flow
    scale = lax.rsqrt(jnp.mean(flow * flow, axis=1, keepdims=True) + EPS)
    normed[...] = (flow * scale * gain2_ref[...]).astype(BF16)
    copies[9].wait()
    copies[10].wait()
    for r in range(L // 256):
        part = slice(r * 256, (r + 1) * 256)
        for n in range(FF // 3072):
            cols = slice(n * 3072, (n + 1) * 3072)
            pre = dot(normed[part], w1[:, cols])
            inner[part, cols] = (pre * normal_cdf(pre)).astype(BF16)
        hidden_ref[part] = (stream[part] + dot(inner[part], w2[...])).astype(BF16)
    copies[11].wait()
    taps_ref[...] = dot_nt(wd[...], hidden_ref[...]).astype(BF16)


def backbone(*args):
    smem = pl.BlockSpec(memory_space=pltpu.SMEM)
    vmem = pl.BlockSpec(memory_space=pltpu.VMEM)
    hbm = pl.BlockSpec(memory_space=pl.ANY)
    fixed = pl.BlockSpec(memory_space=pltpu.HBM)
    return pl.pallas_call(
        backbone_kernel,
        out_shape=(
            pltpu.VMEM((L, D), BF16),
            pltpu.VMEM((DS, L), BF16),
        ),
        in_specs=[smem, smem] + [fixed] * 12,
        out_specs=(vmem, vmem),
        scratch_shapes=[
            pltpu.VMEM((H, NB), F32),
            pltpu.VMEM((1, OFFSETS), jnp.int32),
            pltpu.VMEM((L, D), BF16),
            pltpu.VMEM((1, D), F32),
            pltpu.VMEM((D, D), BF16),
            pltpu.VMEM((D, D), BF16),
            pltpu.VMEM((D, D), BF16),
            pltpu.VMEM((D, D), BF16),
            pltpu.VMEM((1, D), F32),
            pltpu.VMEM((D, FF), BF16),
            pltpu.VMEM((FF, D), BF16),
            pltpu.VMEM((DS, D), BF16),
            pltpu.SemaphoreType.DMA((12,)),
            pltpu.VMEM((L, D), BF16),
            pltpu.VMEM((L, D), BF16),
            pltpu.VMEM((L, D), BF16),
            pltpu.VMEM((H // 2, L, 2 * W), BF16),
            pltpu.VMEM((L, D), BF16),
            pltpu.VMEM((16, 2 * L), F32),
            pltpu.VMEM((L, D), F32),
            pltpu.VMEM((L, FF), BF16),
        ],
        compiler_params=pltpu.CompilerParams(vmem_limit_bytes=60 * 1024 * 1024),
        cost_estimate=pl.CostEstimate(
            flops=9_000_000_000, bytes_accessed=17_000_000, transcendentals=5_000_000
        ),
        name="backbone",
    )(*args)


DOWN0, QKV0, PROJ0, FFIN0, FFOUT0 = 0, 576, 864, 960, 1248
PACK = 1536
PART = PACK // 4


def place():
    index = lax.axis_index("dp")
    return lax.rem(index, 2), lax.rem(lax.div(index, 2), 2)


def column_norm(rows):
    return lax.rsqrt(jnp.mean(rows * rows, axis=0, keepdims=True) + EPS)


def norm_back(grad, unit, scale):
    return scale * (grad - unit * jnp.mean(grad * unit, axis=0, keepdims=True))


def head_sums(rows):
    return jnp.sum(rows.reshape(SH, SHD, L), axis=1)


def fill_heads(ref, rows, extra):
    for head in range(SH):
        mine = rows[head * SHD : (head + 1) * SHD]
        other = extra[head] if isinstance(extra, list) else extra
        ref[head] = jnp.concatenate([mine, other], axis=0).astype(BF16)


def side_kernel(count, lengths_ref, assign_ref, *rest):
    moved_refs, rest = rest[:count], rest[count:]
    (
        taps, gate_hbm, gain1_hbm, gain2_hbm, wq, wk, wv, bucket_hbm, rel, wo, w1, w2,
        back_ref, tap_ref, rest_ref,
        vectors, buckets, moved, sems, table, probs, qt, kt, vt, dt, ctx, sums, dq, dk, dv, dall, diag, dtab,
    ) = rest
    rank = lax.axis_index("side")
    seq = assign_ref[rank]
    pairs = (
        (bucket_hbm, buckets.at[0]), (gate_hbm, vectors.at[0]), (gain1_hbm, vectors.at[1]),
        (gain2_hbm, vectors.at[2]),
    )
    vectors[...] = jnp.zeros_like(vectors)
    copies = start_all(pairs, sems)
    for step in range(count):

        @pl.when(lax.rem(rank + count - seq, count) == step)
        def _():
            moved[...] = moved_refs[step][...]

    length = lengths_ref[seq]
    row8 = lax.broadcasted_iota(jnp.int32, (SHD, L), 0)
    lane8 = lax.broadcasted_iota(jnp.int32, (SHD, L), 1)
    for copy in copies:
        copy.wait()
    table[...] = jnp.zeros_like(table)
    table[:SH] = offset_table(buckets[...], rel[...])
    eye = lax.broadcasted_iota(jnp.int32, (DS, DS), 0) == lax.broadcasted_iota(
        jnp.int32, (DS, DS), 1
    )
    columns = dot(eye.astype(F32), vectors[...], ((1,), (1,)), lax.Precision.HIGHEST)
    gate = jax.nn.sigmoid(columns[:, 0:1])
    gain1, gain2 = columns[:, 1:2], columns[:, 2:3]
    tap = taps[...].astype(F32)
    old = moved[0].astype(F32)
    mixed = gate * tap + (1.0 - gate) * old
    scale1 = column_norm(mixed)
    unit1 = mixed * scale1
    normed1 = (unit1 * gain1).astype(BF16)
    query = dot_tn(wq[...], normed1).astype(BF16).astype(F32)
    key = dot_tn(wk[...], normed1).astype(BF16).astype(F32)
    value = dot_tn(wv[...], normed1)
    fill_heads(qt, query, jnp.where(row8 == 0, 1.0, 0.0))
    fill_heads(kt, key, jnp.where((row8 == 0) & (lane8 >= length), MASKED, 0.0))
    fill_heads(vt, value, jnp.where(row8 < 2, 1.0, 0.0))
    top = jnp.max(head_sums(query * query), axis=1) * jnp.max(head_sums(key * key), axis=1)
    safe = jnp.sqrt(jnp.max(top)) + jnp.max(jnp.abs(table[...])) < LIMIT
    blocks = [slice(b * TILE, (b + 1) * TILE) for b in range(L // TILE)]

    def rows8(head):
        return pl.ds(pl.multiple_of(head * SHD, SHD), SHD)

    def attend(head, stable):
        tile = toeplitz(table[pl.ds(head, 1)])
        for block, rows in enumerate(blocks):
            start = (L // TILE - 1 - block) * TILE
            scores = dot_tn(qt[head, :, rows], kt[head]) + tile[:, start : start + L]
            if stable:
                scores = scores - jnp.max(scores, axis=1, keepdims=True)
            probs[head, rows] = jnp.exp(scores).astype(BF16)
        both = dot_nt(vt[head], probs[head])
        ctx[rows8(head)] = both[:SHD]
        sums[rows8(head)] = jnp.broadcast_to(both[SHD : SHD + 1], (SHD, L))

    @pl.when(safe)
    def _():
        @pl.loop(0, SH, step=UNROLL)
        def _(first):
            for n in range(UNROLL):
                attend(first + n, False)

    @pl.when(jnp.logical_not(safe))
    def _():
        @pl.loop(0, SH)
        def _(head):
            attend(head, True)

    inverse = 1.0 / sums[...]
    context = ctx[...] * inverse
    context16 = context.astype(BF16)
    residual = mixed + dot_tn(wo[...], context16)
    scale2 = column_norm(residual)
    unit2 = residual * scale2
    normed2 = (unit2 * gain2).astype(BF16)
    pre = dot_tn(w1[...], normed2)
    cdf = normal_cdf(pre)
    inner = (pre * cdf).astype(BF16)
    back_ref[0] = (residual + dot(w2[...], inner)).astype(BF16)

    cotangent = moved[1]
    slope = cdf + pre * (jnp.exp(-0.5 * pre * pre) * (1.0 / math.sqrt(2.0 * math.pi)))
    d_pre = (dot_tn(w2[...], cotangent) * slope).astype(BF16)
    g_ffout = dot_nt(cotangent, inner)
    g_ffin = dot_nt(normed2, d_pre)
    for n in range(FS // W):
        for first, grad in ((FFIN0, g_ffin), (FFOUT0, g_ffout)):
            start = first - QKV0 + n * DS
            rest_ref[start : start + DS] = grad[:, n * W : (n + 1) * W].astype(BF16)
    dy = dot(w1[...], d_pre)
    g_gain2 = jnp.sum(dy * unit2, axis=1, keepdims=True)
    d_resid = cotangent.astype(F32) + norm_back(dy * gain2, unit2, scale2)
    d_attn = d_resid.astype(BF16)
    pad = jnp.zeros((W - DS, L), BF16)
    g_project = dot_nt(context16, jnp.concatenate([d_attn, pad], axis=0))
    d_context = dot(wo[...], d_attn).astype(BF16)
    d_scaled = (d_context.astype(F32) * inverse).astype(BF16).astype(F32)
    delta = head_sums(d_scaled * context)
    delta_hi = delta.astype(BF16).astype(F32)
    extra = []
    for head in range(SH):
        high, low = delta_hi[head : head + 1], (delta - delta_hi)[head : head + 1]
        extra.append(jnp.where(row8 == 0, -high, jnp.where(row8 == 1, -low, 0.0)))
    fill_heads(dt, d_scaled, extra)
    dtab[...] = jnp.zeros_like(dtab)

    def attend_back(head, spot):
        for block, rows in enumerate(blocks):
            grads = dot_tn(dt[head, :, rows], vt[head])
            dall[spot, rows] = (probs[head, rows].astype(F32) * grads).astype(BF16)
        dk[rows8(head)] = dot(qt[head], dall[spot])[:SHD]
        dv[rows8(head)] = dot(dt[head], probs[head])[:SHD]
        dq[rows8(head)] = dot_nt(kt[head], dall[spot])[:SHD]
        tiles = []
        for offset in range(2 * (L // TILE) - 1):
            total_tile = None
            for block, rows in enumerate(blocks):
                n = offset + block - (L // TILE - 1)
                if 0 <= n < L // TILE:
                    piece = dall[spot, rows, n * TILE : (n + 1) * TILE].astype(F32)
                    total_tile = piece if total_tile is None else total_tile + piece
            diag[spot, :, offset * TILE : (offset + 1) * TILE] = total_tile
        diag[spot, :, 2 * L - TILE :] = jnp.zeros((TILE, TILE), F32)
        back = 7 - lax.broadcasted_iota(jnp.int32, (8, 2 * L), 0)
        groups = [
            jnp.take_along_axis(diag[spot, g * 8 : g * 8 + 8], back, axis=0)
            for g in reversed(range(TILE // 8))
        ]
        rolled = pltpu.roll(jnp.concatenate(groups, axis=0), 0, 1, stride=1, stride_axis=0)
        dtab[pl.ds(head, 1)] = jnp.sum(rolled, axis=0, keepdims=True)

    @pl.loop(0, SH, step=UNROLL_BACK)
    def _(first):
        for n in range(UNROLL_BACK):
            attend_back(first + n, n)


    spots = lax.broadcasted_iota(jnp.int32, (W, OFFSETS), 0) - DS
    onehot = (spots == buckets[...]).astype(F32)
    g_rel = dot(dtab[:, :OFFSETS], onehot, ((1,), (1,)), lax.Precision.HIGHEST)
    grads = [ref[...].astype(BF16) for ref in (dq, dk, dv)]
    for n, grad in enumerate(grads):
        full = dot_nt(normed1, jnp.concatenate([grad, pad], axis=0))
        if n == 0:
            full = full + jnp.concatenate([g_rel, jnp.zeros((DS - 16, W), F32)], axis=0)
        rest_ref[n * DS : (n + 1) * DS] = full.astype(BF16)
    d_normed = dot(wq[...], grads[0]) + dot(wk[...], grads[1]) + dot(wv[...], grads[2])
    d_mixed = d_resid + norm_back(d_normed * gain1, unit1, scale1)
    back_ref[1] = ((1.0 - gate) * d_mixed).astype(BF16)
    tap_ref[...] = (gate * d_mixed).astype(BF16)
    g_gate = gate * (1.0 - gate) * jnp.sum(d_mixed * (tap - old), axis=1, keepdims=True)
    g_gain1 = jnp.sum(d_normed * unit1, axis=1, keepdims=True)
    lane = lax.broadcasted_iota(jnp.int32, (DS, W), 1)
    for n, grad in enumerate((g_gate, g_gain1, g_gain2)):
        g_project = jnp.where(lane == DS + n, grad, g_project)
    rest_ref[PROJ0 - QKV0 : PROJ0 - QKV0 + DS] = g_project.astype(BF16)


def pack_kernel(tap_ref, rest_ref, hidden_ref, keep_ref, send_ref, pack):
    down = dot(tap_ref[...], hidden_ref[...])
    for n in range(D // W):
        pack[n * DS : (n + 1) * DS] = down[:, n * W : (n + 1) * W].astype(BF16)
    pack[QKV0:] = rest_ref[...]
    core, across = place()
    for n in range(2):
        for ref, half in ((keep_ref, core), (send_ref, 1 - core)):
            start = (half * 2 + (across if n == 0 else 1 - across)) * PART
            ref[n] = pack[pl.ds(pl.multiple_of(start, PART), PART)]


def pack_grads(tap, rest, hidden):
    vmem = pl.BlockSpec(memory_space=pltpu.VMEM)
    return pl.pallas_call(
        pack_kernel,
        out_shape=(jax.ShapeDtypeStruct((2, PART, W), BF16),) * 2,
        in_specs=[vmem] * 3,
        out_specs=(vmem,) * 2,
        scratch_shapes=[pltpu.VMEM((PACK, W), BF16)],
        compiler_params=pltpu.CompilerParams(vmem_limit_bytes=8 * 1024 * 1024),
        cost_estimate=pl.CostEstimate(
            flops=80_000_000, bytes_accessed=2_000_000, transcendentals=0
        ),
        name="pack_grads",
    )(tap, rest, hidden)


def side_block(lengths, assign, moved, *args):
    smem = pl.BlockSpec(memory_space=pltpu.SMEM)
    vmem = pl.BlockSpec(memory_space=pltpu.VMEM)
    hbm = pl.BlockSpec(memory_space=pl.ANY)
    count = len(moved)
    return pl.pallas_call(
        functools.partial(side_kernel, count),
        out_shape=(
            jax.ShapeDtypeStruct((2, DS, L), BF16),
            jax.ShapeDtypeStruct((DS, L), BF16),
            jax.ShapeDtypeStruct((PACK - QKV0, W), BF16),
        ),
        in_specs=[smem, smem] + [vmem] * count + [hbm if a.ndim == 1 else vmem for a in args],
        out_specs=(vmem,) * 3,
        scratch_shapes=[
            pltpu.VMEM((8, DS), F32),
            pltpu.VMEM((1, OFFSETS), jnp.int32),
            pltpu.VMEM((2, DS, L), BF16),
            pltpu.SemaphoreType.DMA((4,)),
            pltpu.VMEM((16, 2 * L), F32),
            pltpu.VMEM((SH, L, L), BF16),
            pltpu.VMEM((SH, 2 * SHD, L), BF16),
            pltpu.VMEM((SH, 2 * SHD, L), BF16),
            pltpu.VMEM((SH, 2 * SHD, L), BF16),
            pltpu.VMEM((SH, 2 * SHD, L), BF16),
            pltpu.VMEM((DS, L), F32),
            pltpu.VMEM((DS, L), F32),
            pltpu.VMEM((DS, L), F32),
            pltpu.VMEM((DS, L), F32),
            pltpu.VMEM((DS, L), F32),
            pltpu.VMEM((UNROLL_BACK, L, L), BF16),
            pltpu.VMEM((UNROLL_BACK, TILE, 2 * L), F32),
            pltpu.VMEM((16, 2 * L), F32),
        ],
        compiler_params=pltpu.CompilerParams(vmem_limit_bytes=VMEM_BYTES),
        cost_estimate=pl.CostEstimate(
            flops=9_000_000_000, bytes_accessed=4_000_000, transcendentals=5_000_000
        ),
        name="side_block",
    )(lengths, assign, *moved, *args)


def finish_kernel(count, assign_ref, *rest):
    quarters, rest = rest[:4], rest[4:]
    backs, results = rest[:count], rest[count : count + 13]
    part, out, *parts, sems = rest[count + 13 :]
    rank = lax.axis_index("side")
    core, across = place()
    spots = [
        2 * half + quarter for half in (core, 1 - core) for quarter in (across, 1 - across)
    ]
    masks = [0]
    for n in reversed(range(16)):
        if 1 << n < count:
            masks += [mask ^ (1 << n) for mask in masks]
    slot = jnp.int32(0)
    for n in range(count):
        slot = jnp.where(assign_ref[n] == rank, n, slot)
    gstate, down, gate, gain1, gq, gk, gv, go, rel, gain2, g1, g2 = parts
    for step in range(count):

        @pl.when((rank ^ slot) == masks[step])
        def _():
            out[...] = backs[step][0]
            gstate[...] = backs[step][1].astype(F32)

    targets = [out, *parts]
    pairs = [
        (ref.at[0] if ref.shape[0] == 1 else ref, result)
        for ref, result in zip(targets, results, strict=True)
    ]
    copies = [pltpu.make_async_copy(src, dst, sems.at[n]) for n, (src, dst) in enumerate(pairs)]
    copies[0].start()
    copies[1].start()
    for ref, spot in zip(quarters, spots, strict=True):
        part[spot] = ref[...]

    def take(start, stop):
        pieces = []
        for n in range(4):
            low, high = max(start, n * PART), min(stop, (n + 1) * PART)
            if low < high:
                pieces.append(part[n, low - n * PART : high - n * PART].astype(F32))
        return pieces[0] if len(pieces) == 1 else jnp.concatenate(pieces, axis=0)

    for n in range(D // W):
        down[:, n * W : (n + 1) * W] = take(DOWN0 + n * DS, DOWN0 + (n + 1) * DS)
    for n, ref in enumerate((gq, gk, gv)):
        ref[...] = take(QKV0 + n * DS, QKV0 + (n + 1) * DS)[:, :DS]
    rel[...] = take(QKV0, QKV0 + 16)[:SH, DS : DS + NB]
    project = take(PROJ0, PROJ0 + DS)
    go[...] = project[:, :DS]
    turned = project.T
    gate[...] = turned[DS : DS + 1]
    gain1[...] = turned[DS + 1 : DS + 2]
    gain2[...] = turned[DS + 2 : DS + 3]
    for n in range(FS // W):
        g1[:, n * W : (n + 1) * W] = take(FFIN0 + n * DS, FFIN0 + (n + 1) * DS)
        g2[:, n * W : (n + 1) * W] = take(FFOUT0 + n * DS, FFOUT0 + (n + 1) * DS)
    for copy in copies[2:]:
        copy.start()
    for copy in copies:
        copy.wait()


def finish(assign, quarters, backs):
    smem = pl.BlockSpec(memory_space=pltpu.SMEM)
    vmem = pl.BlockSpec(memory_space=pltpu.VMEM)
    hbm = pl.BlockSpec(memory_space=pl.ANY)
    fixed = pl.BlockSpec(memory_space=pltpu.HBM)
    count = len(backs)
    parts = [
        (DS, L), (DS, D), (1, DS), (1, DS), (DS, DS), (DS, DS), (DS, DS), (DS, DS), (SH, NB), (1, DS), (DS, FS), (DS, FS),
    ]
    shapes = [jax.ShapeDtypeStruct(p[1:] if p[0] == 1 else p, F32) for p in parts]
    return pl.pallas_call(
        functools.partial(finish_kernel, count),
        out_shape=(jax.ShapeDtypeStruct((DS, L), BF16), *shapes),
        in_specs=[smem] + [vmem] * (4 + count),
        out_specs=(hbm,) * 13,
        scratch_shapes=[
            pltpu.VMEM((4, PART, W), BF16),
            pltpu.VMEM((DS, L), BF16),
            *[pltpu.VMEM(p, F32) for p in parts],
            pltpu.SemaphoreType.DMA((13,)),
        ],
        compiler_params=pltpu.CompilerParams(vmem_limit_bytes=16 * 1024 * 1024),
        name="finish",
    )(assign, *quarters, *backs)


def swap(value, axis, bit):
    size = lax.axis_size(axis)
    return lax.ppermute(value, axis, [(i, i ^ bit) for i in range(size)])


def rotations(value):
    size = lax.axis_size("side")
    return [value] + [
        lax.ppermute(value, "side", [(i, (i + k) % size) for i in range(size)])
        for k in range(1, size)
    ]


def add(one, two):
    return (one.astype(F32) + two.astype(F32)).astype(BF16)


def bits(axis, first=0):
    return [1 << n for n in range(first, 16) if 1 << n < lax.axis_size(axis)]


def spread(blocks, bit):
    return blocks + [swap(block, "side", bit) for block in blocks]


def settle_kernel(_, out_ref):
    del out_ref


def settle(block):
    hbm = pl.BlockSpec(memory_space=pl.ANY)
    return pl.pallas_call(
        settle_kernel,
        out_shape=jax.ShapeDtypeStruct(block.shape, block.dtype),
        in_specs=[hbm],
        out_specs=hbm,
        input_output_aliases={0: 0},
        cost_estimate=pl.CostEstimate(flops=1000000000, bytes_accessed=0, transcendentals=0),
        compiler_params=pltpu.CompilerParams(vmem_limit_bytes=1024 * 1024),
        name="settle",
    )(block)


def total(keep, send, back):
    levels = bits("side")[::-1]
    backs = spread([back], levels[0])
    got = swap(send, "dp", 1)
    mine = add(keep[0], got[0])
    across = swap(add(keep[1], got[1]), "dp", 2)
    mine = add(mine, across)
    mine = add(mine, swap(mine, "side", 1))
    mine, backs[1] = lax.optimization_barrier((mine, settle(backs[1])))
    for bit in levels[1:]:
        backs = spread(backs, bit)
    for bit in bits("dp", 2):
        mine = add(mine, swap(mine, "dp", bit))
    for bit in bits("side", 1):
        mine = add(mine, swap(mine, "side", bit))
    if len(levels) > 1:
        own = len(backs) // 2
        mine, backs[own] = lax.optimization_barrier((mine, settle(backs[own])))
    across = swap(mine, "dp", 2)
    return (mine, across, swap(mine, "dp", 1), swap(across, "dp", 1)), backs


def shards(
    hidden_in, side_state, lengths, assign, buckets,
    backbone_gain_attn, backbone_query, backbone_key, backbone_value, backbone_project, backbone_rel,
    backbone_gain_ff, backbone_ff_in, backbone_ff_out, down_weight, gate_logit,
    side_gain_attn, side_query, side_key, side_value, side_project, side_rel,
    side_gain_ff, side_ff_in, side_ff_out, cotangent,
):
    moved = rotations(jnp.stack([side_state[0].T, cotangent[0].T]))
    hidden, taps = backbone(
        lengths, assign, backbone_rel.T, buckets, hidden_in[0], backbone_gain_attn,
        backbone_query, backbone_key, backbone_value, backbone_project, backbone_gain_ff,
        backbone_ff_in, backbone_ff_out, down_weight.T,
    )
    back, tap, rest = side_block(
        lengths, assign, moved, taps, gate_logit, side_gain_attn, side_gain_ff,
        side_query, side_key, side_value, buckets, side_rel.T, side_project, side_ff_in, side_ff_out.T,
    )
    keep, send = pack_grads(tap, rest, hidden)
    quarters, backs = total(keep, send, back)
    res = finish(assign, quarters, backs)
    out, gstate, down, gate, gain1, gq, gk, gv, go, rel, gain2, g1, g2 = res
    return (
        out.T[None], gstate.T[None], down.T, gate, gain1, gq, gk, gv, go, rel.T, gain2, g1, g2.T,
    )


def solution(mesh):
    rows = P(("dp", "side"), None, None)
    return jax.shard_map(
        shards,
        mesh=mesh,
        in_specs=(rows, rows, P("dp"), P("dp")) + (P(),) * 21 + (rows,),
        out_specs=(rows, rows) + (P(),) * 11,
        check_vma=False,
    )
```

```python
import functools
import math

import jax
import jax.numpy as jnp
from jax import lax
from jax.experimental import pallas as pl
from jax.experimental.pallas import tpu as pltpu
from jax.sharding import PartitionSpec as P

D = 768
H = 12
HD = 64
FF = 3072
NB = 32
DS = 96
SH = 12
SHD = 8
FS = 384
L = 512
W = 128
OFFSETS = 2 * L - 1
TILE = 128

EPS = 1e-06
MASKED = -1e9
LIMIT = 60.0
F32 = jnp.float32
BF16 = jnp.bfloat16
VMEM_BYTES = 44 * 1024 * 1024
UNROLL = 12
UNROLL_BACK = 12
PAIRS = 6


def dot(a, b, dims=((1,), (0,)), precision=None):
    return lax.dot_general(
        a, b, (dims, ((), ())), precision=precision, preferred_element_type=F32
    )


def dot_nt(a, b):
    return dot(a, b, ((1,), (1,)))


def dot_tn(a, b):
    return dot(a, b, ((0,), (0,)))


def normal_cdf(v):
    return 0.5 * (1.0 + lax.erf(v * (1.0 / math.sqrt(2.0))))


def offset_table(buckets, rel):
    rows = lax.broadcasted_iota(jnp.int32, (NB, OFFSETS), 0)
    onehot = (rows == buckets).astype(F32)
    table = dot(rel, onehot, precision=lax.Precision.HIGHEST)
    return jnp.concatenate([table, jnp.zeros((rel.shape[0], 1), F32)], axis=1)


def toeplitz(row):
    wide = jnp.broadcast_to(row, (TILE, 2 * L))
    return pltpu.roll(wide, 2 * L - (TILE - 1), 1, stride=1, stride_axis=0)


def bounded(q, k, table, size, heads):
    rows = lax.broadcasted_iota(jnp.int32, (q.shape[1], W), 0) // size
    cols = lax.broadcasted_iota(jnp.int32, (q.shape[1], W), 1)
    pick = ((rows == cols) & (rows < heads)).astype(BF16)
    qn = jnp.max(dot(q * q, pick), axis=0, keepdims=True)
    kn = jnp.max(dot(k * k, pick), axis=0, keepdims=True)
    top = jnp.max(jnp.sqrt(qn) * jnp.sqrt(kn)) * 1.02
    return top + jnp.max(jnp.abs(table)) < LIMIT


def start_all(pairs, sems):
    copies = [pltpu.make_async_copy(src, dst, sems.at[n]) for n, (src, dst) in enumerate(pairs)]
    for copy in copies:
        copy.start()
    return copies


def backbone_kernel(
    lengths_ref, assign_ref, rel_hbm, bucket_hbm, x_hbm, gain1_hbm, wq_hbm, wk_hbm, wv_hbm, wo_hbm, gain2_hbm, w1_hbm,
    w2_hbm, wd_hbm,
    hidden_ref, taps_ref,
    rel, buckets, x_ref, gain1_ref, wq, wk, wv, wo, gain2_ref, w1, w2, wd, sems,
    normed, q_s, k_s, vx, ctx, table, stream, inner,
):
    pairs = (
        (x_hbm, x_ref), (gain1_hbm, gain1_ref.at[0]), (rel_hbm, rel), (bucket_hbm, buckets.at[0]),
        (wq_hbm, wq), (wk_hbm, wk), (wv_hbm, wv), (wo_hbm, wo), (gain2_hbm, gain2_ref.at[0]),
        (w1_hbm, w1), (w2_hbm, w2), (wd_hbm, wd),
    )
    copies = [pltpu.make_async_copy(src, dst, sems.at[n]) for n, (src, dst) in enumerate(pairs)]
    for n in (2, 3, 0, 1, 4):
        copies[n].start()
    length = lengths_ref[assign_ref[lax.axis_index("side")]]
    copies[2].wait()
    copies[3].wait()
    table[...] = jnp.zeros_like(table)
    table[:H] = offset_table(buckets[...], rel[...])
    copies[0].wait()
    copies[1].wait()
    for n in (5, 6):
        copies[n].start()
    x = x_ref[...].astype(F32)
    scale = lax.rsqrt(jnp.mean(x * x, axis=1, keepdims=True) + EPS)
    normed[...] = (x * scale * gain1_ref[...]).astype(BF16)
    copies[4].wait()
    copies[7].start()
    q_s[...] = dot(normed[...], wq[...]).astype(BF16)
    copies[5].wait()
    k_s[...] = dot(normed[...], wk[...]).astype(BF16)
    copies[6].wait()
    for n in (8, 9, 10, 11):
        copies[n].start()
    live_row = lax.broadcasted_iota(jnp.int32, (L, 1), 0) < length
    value = dot(normed[...], wv[...])
    value = jnp.where(live_row, value, 0.0).astype(BF16)
    ones = jnp.where(live_row, 1.0, 0.0).astype(BF16)
    for pair in range(H // 2):
        vx[pair, :, :W] = value[:, pair * W : (pair + 1) * W]
        vx[pair, :, W:] = jnp.broadcast_to(ones, (L, W))
    low_half = lax.broadcasted_iota(jnp.int32, (L, W), 1) < HD
    low_row = lax.broadcasted_iota(jnp.int32, (TILE, W), 1) < HD
    live = lax.broadcasted_iota(jnp.int32, (1, L), 1) < length

    def attend(pair, stable):
        lanes = pl.ds(pl.multiple_of(pair * W, W), W)
        keys = k_s[:, lanes]
        tiles = [toeplitz(table[pl.ds(pair * 2 + half, 1)]) for half in range(2)]
        for block in range(L // TILE):
            rows = slice(block * TILE, (block + 1) * TILE)
            start = (L // TILE - 1 - block) * TILE
            query = q_s[rows, lanes]
            results = []
            for half in range(2):
                mine = low_row if half == 0 else jnp.logical_not(low_row)
                scores = dot_nt(jnp.where(mine, query, jnp.zeros_like(query)), keys)
                scores = scores + tiles[half][:, start : start + L]
                if stable:
                    scores = jnp.where(live, scores, MASKED)
                    scores = scores - jnp.max(scores, axis=1, keepdims=True)
                results.append(dot(jnp.exp(scores).astype(BF16), vx[pair]))
            top = jnp.where(low_row, results[0][:, :W], results[1][:, :W])
            total = jnp.where(low_row, results[0][:, W:], results[1][:, W:])
            ctx[rows, lanes] = (top / total).astype(BF16)

    safe = bounded(q_s[...], k_s[...], table[...], HD, H)

    @pl.when(safe)
    def _():
        @pl.loop(0, H // 2, step=PAIRS)
        def _(first):
            for n in range(PAIRS):
                attend(first + n, False)

    @pl.when(jnp.logical_not(safe))
    def _():
        @pl.loop(0, H // 2)
        def _(pair):
            attend(pair, True)

    copies[7].wait()
    copies[8].wait()
    flow = x_ref[...].astype(F32) + dot(ctx[...], wo[...])
    stream[...] = flow
    scale = lax.rsqrt(jnp.mean(flow * flow, axis=1, keepdims=True) + EPS)
    normed[...] = (flow * scale * gain2_ref[...]).astype(BF16)
    copies[9].wait()
    copies[10].wait()
    for r in range(L // 256):
        part = slice(r * 256, (r + 1) * 256)
        for n in range(FF // 3072):
            cols = slice(n * 3072, (n + 1) * 3072)
            pre = dot(normed[part], w1[:, cols])
            inner[part, cols] = (pre * normal_cdf(pre)).astype(BF16)
        hidden_ref[part] = (stream[part] + dot(inner[part], w2[...])).astype(BF16)
    copies[11].wait()
    taps_ref[...] = dot_nt(wd[...], hidden_ref[...]).astype(BF16)


def backbone(*args):
    smem = pl.BlockSpec(memory_space=pltpu.SMEM)
    vmem = pl.BlockSpec(memory_space=pltpu.VMEM)
    hbm = pl.BlockSpec(memory_space=pl.ANY)
    fixed = pl.BlockSpec(memory_space=pltpu.HBM)
    return pl.pallas_call(
        backbone_kernel,
        out_shape=(
            pltpu.VMEM((L, D), BF16),
            pltpu.VMEM((DS, L), BF16),
        ),
        in_specs=[smem, smem] + [fixed] * 12,
        out_specs=(vmem, vmem),
        scratch_shapes=[
            pltpu.VMEM((H, NB), F32),
            pltpu.VMEM((1, OFFSETS), jnp.int32),
            pltpu.VMEM((L, D), BF16),
            pltpu.VMEM((1, D), F32),
            pltpu.VMEM((D, D), BF16),
            pltpu.VMEM((D, D), BF16),
            pltpu.VMEM((D, D), BF16),
            pltpu.VMEM((D, D), BF16),
            pltpu.VMEM((1, D), F32),
            pltpu.VMEM((D, FF), BF16),
            pltpu.VMEM((FF, D), BF16),
            pltpu.VMEM((DS, D), BF16),
            pltpu.SemaphoreType.DMA((12,)),
            pltpu.VMEM((L, D), BF16),
            pltpu.VMEM((L, D), BF16),
            pltpu.VMEM((L, D), BF16),
            pltpu.VMEM((H // 2, L, 2 * W), BF16),
            pltpu.VMEM((L, D), BF16),
            pltpu.VMEM((16, 2 * L), F32),
            pltpu.VMEM((L, D), F32),
            pltpu.VMEM((L, FF), BF16),
        ],
        compiler_params=pltpu.CompilerParams(vmem_limit_bytes=60 * 1024 * 1024),
        cost_estimate=pl.CostEstimate(
            flops=9_000_000_000, bytes_accessed=17_000_000, transcendentals=5_000_000
        ),
        name="backbone",
    )(*args)


DOWN0, QKV0, PROJ0, FFIN0, FFOUT0 = 0, 576, 864, 960, 1248
PACK = 1536
PART = PACK // 4


def place():
    index = lax.axis_index("dp")
    return lax.rem(index, 2), lax.rem(lax.div(index, 2), 2)


def column_norm(rows):
    return lax.rsqrt(jnp.mean(rows * rows, axis=0, keepdims=True) + EPS)


def norm_back(grad, unit, scale):
    return scale * (grad - unit * jnp.mean(grad * unit, axis=0, keepdims=True))


def head_sums(rows):
    return jnp.sum(rows.reshape(SH, SHD, L), axis=1)


def fill_heads(ref, rows, extra):
    for head in range(SH):
        mine = rows[head * SHD : (head + 1) * SHD]
        other = extra[head] if isinstance(extra, list) else extra
        ref[head] = jnp.concatenate([mine, other], axis=0).astype(BF16)


def side_kernel(count, lengths_ref, assign_ref, *rest):
    moved_refs, rest = rest[:count], rest[count:]
    (
        taps, gate_hbm, gain1_hbm, gain2_hbm, wq, wk, wv, bucket_hbm, rel, wo, w1, w2,
        out_ref, gstate_ref, tap_ref, rest_ref,
        vectors, buckets, moved, sems, table, probs, qt, kt, vt, dt, ctx, sums, dq, dk, dv, dall, diag, dtab,
    ) = rest
    rank = lax.axis_index("side")
    seq = assign_ref[rank]
    pairs = (
        (bucket_hbm, buckets.at[0]), (gate_hbm, vectors.at[0]), (gain1_hbm, vectors.at[1]),
        (gain2_hbm, vectors.at[2]),
    )
    vectors[...] = jnp.zeros_like(vectors)
    copies = start_all(pairs, sems)
    for step in range(count):

        @pl.when(lax.rem(rank + count - seq, count) == step)
        def _():
            moved[...] = moved_refs[step][...]

    length = lengths_ref[seq]
    row8 = lax.broadcasted_iota(jnp.int32, (SHD, L), 0)
    lane8 = lax.broadcasted_iota(jnp.int32, (SHD, L), 1)
    for copy in copies:
        copy.wait()
    table[...] = jnp.zeros_like(table)
    table[:SH] = offset_table(buckets[...], rel[...])
    eye = lax.broadcasted_iota(jnp.int32, (DS, DS), 0) == lax.broadcasted_iota(
        jnp.int32, (DS, DS), 1
    )
    columns = dot(eye.astype(F32), vectors[...], ((1,), (1,)), lax.Precision.HIGHEST)
    gate = jax.nn.sigmoid(columns[:, 0:1])
    gain1, gain2 = columns[:, 1:2], columns[:, 2:3]
    tap = taps[...].astype(F32)
    old = moved[0].astype(F32)
    mixed = gate * tap + (1.0 - gate) * old
    scale1 = column_norm(mixed)
    unit1 = mixed * scale1
    normed1 = (unit1 * gain1).astype(BF16)
    query = dot_tn(wq[...], normed1).astype(BF16).astype(F32)
    key = dot_tn(wk[...], normed1).astype(BF16).astype(F32)
    value = dot_tn(wv[...], normed1)
    fill_heads(qt, query, jnp.where(row8 == 0, 1.0, 0.0))
    fill_heads(kt, key, jnp.where((row8 == 0) & (lane8 >= length), MASKED, 0.0))
    fill_heads(vt, value, jnp.where(row8 < 2, 1.0, 0.0))
    top = jnp.max(head_sums(query * query), axis=1) * jnp.max(head_sums(key * key), axis=1)
    safe = jnp.sqrt(jnp.max(top)) + jnp.max(jnp.abs(table[...])) < LIMIT
    blocks = [slice(b * TILE, (b + 1) * TILE) for b in range(L // TILE)]

    def rows8(head):
        return pl.ds(pl.multiple_of(head * SHD, SHD), SHD)

    def attend(head, stable):
        tile = toeplitz(table[pl.ds(head, 1)])
        for block, rows in enumerate(blocks):
            start = (L // TILE - 1 - block) * TILE
            scores = dot_tn(qt[head, :, rows], kt[head]) + tile[:, start : start + L]
            if stable:
                scores = scores - jnp.max(scores, axis=1, keepdims=True)
            probs[head, rows] = jnp.exp(scores).astype(BF16)
        both = dot_nt(vt[head], probs[head])
        ctx[rows8(head)] = both[:SHD]
        sums[rows8(head)] = jnp.broadcast_to(both[SHD : SHD + 1], (SHD, L))

    @pl.when(safe)
    def _():
        @pl.loop(0, SH, step=UNROLL)
        def _(first):
            for n in range(UNROLL):
                attend(first + n, False)

    @pl.when(jnp.logical_not(safe))
    def _():
        @pl.loop(0, SH)
        def _(head):
            attend(head, True)

    inverse = 1.0 / sums[...]
    context = ctx[...] * inverse
    context16 = context.astype(BF16)
    residual = mixed + dot_tn(wo[...], context16)
    scale2 = column_norm(residual)
    unit2 = residual * scale2
    normed2 = (unit2 * gain2).astype(BF16)
    pre = dot_tn(w1[...], normed2)
    cdf = normal_cdf(pre)
    inner = (pre * cdf).astype(BF16)
    out_ref[...] = (residual + dot(w2[...], inner)).astype(BF16)

    cotangent = moved[1]
    slope = cdf + pre * (jnp.exp(-0.5 * pre * pre) * (1.0 / math.sqrt(2.0 * math.pi)))
    d_pre = (dot_tn(w2[...], cotangent) * slope).astype(BF16)
    g_ffout = dot_nt(cotangent, inner)
    g_ffin = dot_nt(normed2, d_pre)
    for n in range(FS // W):
        for first, grad in ((FFIN0, g_ffin), (FFOUT0, g_ffout)):
            start = first - QKV0 + n * DS
            rest_ref[start : start + DS] = grad[:, n * W : (n + 1) * W].astype(BF16)
    dy = dot(w1[...], d_pre)
    g_gain2 = jnp.sum(dy * unit2, axis=1, keepdims=True)
    d_resid = cotangent.astype(F32) + norm_back(dy * gain2, unit2, scale2)
    d_attn = d_resid.astype(BF16)
    pad = jnp.zeros((W - DS, L), BF16)
    g_project = dot_nt(context16, jnp.concatenate([d_attn, pad], axis=0))
    d_context = dot(wo[...], d_attn).astype(BF16)
    d_scaled = (d_context.astype(F32) * inverse).astype(BF16).astype(F32)
    delta = head_sums(d_scaled * context)
    delta_hi = delta.astype(BF16).astype(F32)
    extra = []
    for head in range(SH):
        high, low = delta_hi[head : head + 1], (delta - delta_hi)[head : head + 1]
        extra.append(jnp.where(row8 == 0, -high, jnp.where(row8 == 1, -low, 0.0)))
    fill_heads(dt, d_scaled, extra)
    dtab[...] = jnp.zeros_like(dtab)

    def attend_back(head, spot):
        for block, rows in enumerate(blocks):
            grads = dot_tn(dt[head, :, rows], vt[head])
            dall[spot, rows] = (probs[head, rows].astype(F32) * grads).astype(BF16)
        dk[rows8(head)] = dot(qt[head], dall[spot])[:SHD]
        dv[rows8(head)] = dot(dt[head], probs[head])[:SHD]
        dq[rows8(head)] = dot_nt(kt[head], dall[spot])[:SHD]
        tiles = []
        for offset in range(2 * (L // TILE) - 1):
            total_tile = None
            for block, rows in enumerate(blocks):
                n = offset + block - (L // TILE - 1)
                if 0 <= n < L // TILE:
                    piece = dall[spot, rows, n * TILE : (n + 1) * TILE].astype(F32)
                    total_tile = piece if total_tile is None else total_tile + piece
            diag[spot, :, offset * TILE : (offset + 1) * TILE] = total_tile
        diag[spot, :, 2 * L - TILE :] = jnp.zeros((TILE, TILE), F32)
        back = 7 - lax.broadcasted_iota(jnp.int32, (8, 2 * L), 0)
        groups = [
            jnp.take_along_axis(diag[spot, g * 8 : g * 8 + 8], back, axis=0)
            for g in reversed(range(TILE // 8))
        ]
        rolled = pltpu.roll(jnp.concatenate(groups, axis=0), 0, 1, stride=1, stride_axis=0)
        dtab[pl.ds(head, 1)] = jnp.sum(rolled, axis=0, keepdims=True)

    @pl.loop(0, SH, step=UNROLL_BACK)
    def _(first):
        for n in range(UNROLL_BACK):
            attend_back(first + n, n)


    spots = lax.broadcasted_iota(jnp.int32, (W, OFFSETS), 0) - DS
    onehot = (spots == buckets[...]).astype(F32)
    g_rel = dot(dtab[:, :OFFSETS], onehot, ((1,), (1,)), lax.Precision.HIGHEST)
    grads = [ref[...].astype(BF16) for ref in (dq, dk, dv)]
    for n, grad in enumerate(grads):
        full = dot_nt(normed1, jnp.concatenate([grad, pad], axis=0))
        if n == 0:
            full = full + jnp.concatenate([g_rel, jnp.zeros((DS - 16, W), F32)], axis=0)
        rest_ref[n * DS : (n + 1) * DS] = full.astype(BF16)
    d_normed = dot(wq[...], grads[0]) + dot(wk[...], grads[1]) + dot(wv[...], grads[2])
    d_mixed = d_resid + norm_back(d_normed * gain1, unit1, scale1)
    gstate_ref[...] = ((1.0 - gate) * d_mixed).astype(BF16)
    tap_ref[...] = (gate * d_mixed).astype(BF16)
    g_gate = gate * (1.0 - gate) * jnp.sum(d_mixed * (tap - old), axis=1, keepdims=True)
    g_gain1 = jnp.sum(d_normed * unit1, axis=1, keepdims=True)
    lane = lax.broadcasted_iota(jnp.int32, (DS, W), 1)
    for n, grad in enumerate((g_gate, g_gain1, g_gain2)):
        g_project = jnp.where(lane == DS + n, grad, g_project)
    rest_ref[PROJ0 - QKV0 : PROJ0 - QKV0 + DS] = g_project.astype(BF16)


def pack_kernel(tap_ref, rest_ref, hidden_ref, keep_ref, send_ref, pack):
    down = dot(tap_ref[...], hidden_ref[...])
    for n in range(D // W):
        pack[n * DS : (n + 1) * DS] = down[:, n * W : (n + 1) * W].astype(BF16)
    pack[QKV0:] = rest_ref[...]
    core, across = place()
    for n in range(2):
        for ref, half in ((keep_ref, core), (send_ref, 1 - core)):
            start = (half * 2 + (across if n == 0 else 1 - across)) * PART
            ref[n] = pack[pl.ds(pl.multiple_of(start, PART), PART)]


def pack_grads(tap, rest, hidden):
    vmem = pl.BlockSpec(memory_space=pltpu.VMEM)
    return pl.pallas_call(
        pack_kernel,
        out_shape=(jax.ShapeDtypeStruct((2, PART, W), BF16),) * 2,
        in_specs=[vmem] * 3,
        out_specs=(vmem,) * 2,
        scratch_shapes=[pltpu.VMEM((PACK, W), BF16)],
        compiler_params=pltpu.CompilerParams(vmem_limit_bytes=8 * 1024 * 1024),
        cost_estimate=pl.CostEstimate(
            flops=80_000_000, bytes_accessed=2_000_000, transcendentals=0
        ),
        name="pack_grads",
    )(tap, rest, hidden)


def side_block(lengths, assign, moved, *args):
    smem = pl.BlockSpec(memory_space=pltpu.SMEM)
    vmem = pl.BlockSpec(memory_space=pltpu.VMEM)
    hbm = pl.BlockSpec(memory_space=pl.ANY)
    count = len(moved)
    return pl.pallas_call(
        functools.partial(side_kernel, count),
        out_shape=(
            pltpu.VMEM((DS, L), BF16),
            pltpu.VMEM((DS, L), BF16),
            pltpu.VMEM((DS, L), BF16),
            pltpu.VMEM((PACK - QKV0, W), BF16),
        ),
        in_specs=[smem, smem] + [vmem] * count + [hbm if a.ndim == 1 else vmem for a in args],
        out_specs=(vmem,) * 4,
        scratch_shapes=[
            pltpu.VMEM((8, DS), F32),
            pltpu.VMEM((1, OFFSETS), jnp.int32),
            pltpu.VMEM((2, DS, L), BF16),
            pltpu.SemaphoreType.DMA((4,)),
            pltpu.VMEM((16, 2 * L), F32),
            pltpu.VMEM((SH, L, L), BF16),
            pltpu.VMEM((SH, 2 * SHD, L), BF16),
            pltpu.VMEM((SH, 2 * SHD, L), BF16),
            pltpu.VMEM((SH, 2 * SHD, L), BF16),
            pltpu.VMEM((SH, 2 * SHD, L), BF16),
            pltpu.VMEM((DS, L), F32),
            pltpu.VMEM((DS, L), F32),
            pltpu.VMEM((DS, L), F32),
            pltpu.VMEM((DS, L), F32),
            pltpu.VMEM((DS, L), F32),
            pltpu.VMEM((UNROLL_BACK, L, L), BF16),
            pltpu.VMEM((UNROLL_BACK, TILE, 2 * L), F32),
            pltpu.VMEM((16, 2 * L), F32),
        ],
        compiler_params=pltpu.CompilerParams(vmem_limit_bytes=VMEM_BYTES),
        cost_estimate=pl.CostEstimate(
            flops=9_000_000_000, bytes_accessed=4_000_000, transcendentals=5_000_000
        ),
        name="side_block",
    )(lengths, assign, *moved, *args)


def finish_kernel(count, assign_ref, *rest):
    quarters, rest = rest[:4], rest[4:]
    outs, gstates, results = rest[:count], rest[count : 2 * count], rest[2 * count : 2 * count + 13]
    part, out, *parts, sems = rest[2 * count + 13 :]
    rank = lax.axis_index("side")
    core, across = place()
    spots = [
        2 * half + quarter for half in (core, 1 - core) for quarter in (across, 1 - across)
    ]
    masks = [0]
    for n in reversed(range(16)):
        if 1 << n < count:
            masks += [mask ^ (1 << n) for mask in masks]
    slot = jnp.int32(0)
    for n in range(count):
        slot = jnp.where(assign_ref[n] == rank, n, slot)
    gstate, down, gate, gain1, gq, gk, gv, go, rel, gain2, g1, g2 = parts
    for step in range(count):

        @pl.when((rank ^ slot) == masks[step])
        def _():
            out[...] = outs[step][...]
            gstate[...] = gstates[step][...].astype(F32)

    targets = [out, *parts]
    pairs = [
        (ref.at[0] if ref.shape[0] == 1 else ref, result)
        for ref, result in zip(targets, results, strict=True)
    ]
    copies = [pltpu.make_async_copy(src, dst, sems.at[n]) for n, (src, dst) in enumerate(pairs)]
    copies[0].start()
    copies[1].start()
    for ref, spot in zip(quarters, spots, strict=True):
        part[spot] = ref[...]

    def take(start, stop):
        pieces = []
        for n in range(4):
            low, high = max(start, n * PART), min(stop, (n + 1) * PART)
            if low < high:
                pieces.append(part[n, low - n * PART : high - n * PART].astype(F32))
        return pieces[0] if len(pieces) == 1 else jnp.concatenate(pieces, axis=0)

    for n in range(D // W):
        down[:, n * W : (n + 1) * W] = take(DOWN0 + n * DS, DOWN0 + (n + 1) * DS)
    copies[2].start()
    for n in range(FS // W):
        g1[:, n * W : (n + 1) * W] = take(FFIN0 + n * DS, FFIN0 + (n + 1) * DS)
        g2[:, n * W : (n + 1) * W] = take(FFOUT0 + n * DS, FFOUT0 + (n + 1) * DS)
    copies[11].start()
    copies[12].start()
    for n, ref in enumerate((gq, gk, gv)):
        ref[...] = take(QKV0 + n * DS, QKV0 + (n + 1) * DS)[:, :DS]
        copies[5 + n].start()
    rel[...] = take(QKV0, QKV0 + 16)[:SH, DS : DS + NB]
    project = take(PROJ0, PROJ0 + DS)
    go[...] = project[:, :DS]
    copies[8].start()
    copies[9].start()
    turned = project.T
    gate[...] = turned[DS : DS + 1]
    gain1[...] = turned[DS + 1 : DS + 2]
    gain2[...] = turned[DS + 2 : DS + 3]
    for n in (3, 4, 10):
        copies[n].start()
    for copy in copies:
        copy.wait()


def finish(assign, quarters, outs, gstates):
    smem = pl.BlockSpec(memory_space=pltpu.SMEM)
    vmem = pl.BlockSpec(memory_space=pltpu.VMEM)
    hbm = pl.BlockSpec(memory_space=pl.ANY)
    fixed = pl.BlockSpec(memory_space=pltpu.HBM)
    count = len(outs)
    parts = [
        (DS, L), (DS, D), (1, DS), (1, DS), (DS, DS), (DS, DS), (DS, DS), (DS, DS), (SH, NB), (1, DS), (DS, FS), (DS, FS),
    ]
    shapes = [jax.ShapeDtypeStruct(p[1:] if p[0] == 1 else p, F32) for p in parts]
    return pl.pallas_call(
        functools.partial(finish_kernel, count),
        out_shape=(jax.ShapeDtypeStruct((DS, L), BF16), *shapes),
        in_specs=[smem] + [vmem] * (4 + 2 * count),
        out_specs=(hbm,) * 13,
        scratch_shapes=[
            pltpu.VMEM((4, PART, W), BF16),
            pltpu.VMEM((DS, L), BF16),
            *[pltpu.VMEM(p, F32) for p in parts],
            pltpu.SemaphoreType.DMA((13,)),
        ],
        compiler_params=pltpu.CompilerParams(vmem_limit_bytes=16 * 1024 * 1024),
        name="finish",
    )(assign, *quarters, *outs, *gstates)


def swap(value, axis, bit):
    size = lax.axis_size(axis)
    return lax.ppermute(value, axis, [(i, i ^ bit) for i in range(size)])


def rotations(value):
    size = lax.axis_size("side")
    return [value] + [
        lax.ppermute(value, "side", [(i, (i + k) % size) for i in range(size)])
        for k in range(1, size)
    ]


def add(one, two):
    return (one.astype(F32) + two.astype(F32)).astype(BF16)


def bits(axis, first=0):
    return [1 << n for n in range(first, 16) if 1 << n < lax.axis_size(axis)]


def spread(blocks, bit):
    return blocks + [swap(block, "side", bit) for block in blocks]


def settle_kernel(_, out_ref):
    del out_ref


def settle(block):
    hbm = pl.BlockSpec(memory_space=pl.ANY)
    return pl.pallas_call(
        settle_kernel,
        out_shape=jax.ShapeDtypeStruct(block.shape, block.dtype),
        in_specs=[hbm],
        out_specs=hbm,
        input_output_aliases={0: 0},
        cost_estimate=pl.CostEstimate(flops=1000000000, bytes_accessed=0, transcendentals=0),
        compiler_params=pltpu.CompilerParams(vmem_limit_bytes=1024 * 1024),
        name="settle",
    )(block)


def hold(value, blocks):
    return lax.optimization_barrier((value, [settle(block) for block in blocks]))


def total(keep, send, out, gstate):
    levels = bits("side")[::-1]
    outs, gstates = spread([out], levels[0]), spread([gstate], levels[0])
    got = swap(send, "dp", 1)
    mine = add(keep[0], got[0])
    across = swap(add(keep[1], got[1]), "dp", 2)
    mine = add(mine, across)
    mine = add(mine, swap(mine, "side", 1))
    mine, outs[1:] = hold(mine, outs[1:])
    for bit in bits("dp", 2):
        mine = add(mine, swap(mine, "dp", bit))
    mine, gstates[1:] = hold(mine, gstates[1:])
    for bit in levels[1:]:
        outs, gstates = spread(outs, bit), spread(gstates, bit)
    for bit in bits("side", 1):
        mine = add(mine, swap(mine, "side", bit))
    if len(levels) > 1:
        own = len(outs) // 2
        mine, outs[own:] = hold(mine, outs[own:])
    across = swap(mine, "dp", 2)
    return (mine, across, swap(mine, "dp", 1), swap(across, "dp", 1)), outs, gstates


def shards(
    hidden_in, side_state, lengths, assign, buckets,
    backbone_gain_attn, backbone_query, backbone_key, backbone_value, backbone_project, backbone_rel,
    backbone_gain_ff, backbone_ff_in, backbone_ff_out, down_weight, gate_logit,
    side_gain_attn, side_query, side_key, side_value, side_project, side_rel,
    side_gain_ff, side_ff_in, side_ff_out, cotangent,
):
    moved = rotations(jnp.stack([side_state[0].T, cotangent[0].T]))
    hidden, taps = backbone(
        lengths, assign, backbone_rel.T, buckets, hidden_in[0], backbone_gain_attn,
        backbone_query, backbone_key, backbone_value, backbone_project, backbone_gain_ff,
        backbone_ff_in, backbone_ff_out, down_weight.T,
    )
    out, gstate, tap, rest = side_block(
        lengths, assign, moved, taps, gate_logit, side_gain_attn, side_gain_ff,
        side_query, side_key, side_value, buckets, side_rel.T, side_project, side_ff_in, side_ff_out.T,
    )
    keep, send = pack_grads(tap, rest, hidden)
    quarters, outs, gstates = total(keep, send, out, gstate)
    res = finish(assign, quarters, outs, gstates)
    out, gstate, down, gate, gain1, gq, gk, gv, go, rel, gain2, g1, g2 = res
    return (
        out.T[None], gstate.T[None], down.T, gate, gain1, gq, gk, gv, go, rel.T, gain2, g1, g2.T,
    )


def solution(mesh):
    rows = P(("dp", "side"), None, None)
    return jax.shard_map(
        shards,
        mesh=mesh,
        in_specs=(rows, rows, P("dp"), P("dp")) + (P(),) * 21 + (rows,),
        out_specs=(rows, rows) + (P(),) * 11,
        check_vma=False,
    )
```

```python
import functools
import math

import jax
import jax.numpy as jnp
from jax import lax
from jax.experimental import pallas as pl
from jax.experimental.pallas import tpu as pltpu
from jax.sharding import PartitionSpec as P

D = 768
H = 12
HD = 64
FF = 3072
NB = 32
DS = 96
SH = 12
SHD = 8
FS = 384
L = 512
W = 128
OFFSETS = 2 * L - 1
TILE = 128

EPS = 1e-06
MASKED = -1e9
LIMIT = 60.0
F32 = jnp.float32
BF16 = jnp.bfloat16
VMEM_BYTES = 44 * 1024 * 1024
UNROLL = 12
UNROLL_BACK = 12
PAIRS = 6


def dot(a, b, dims=((1,), (0,)), precision=None):
    return lax.dot_general(
        a, b, (dims, ((), ())), precision=precision, preferred_element_type=F32
    )


def dot_nt(a, b):
    return dot(a, b, ((1,), (1,)))


def dot_tn(a, b):
    return dot(a, b, ((0,), (0,)))


def normal_cdf(v):
    return 0.5 * (1.0 + lax.erf(v * (1.0 / math.sqrt(2.0))))


def offset_table(buckets, rel):
    rows = lax.broadcasted_iota(jnp.int32, (NB, OFFSETS), 0)
    onehot = (rows == buckets).astype(F32)
    table = dot(rel, onehot, precision=lax.Precision.HIGHEST)
    return jnp.concatenate([table, jnp.zeros((rel.shape[0], 1), F32)], axis=1)


def toeplitz(row):
    wide = jnp.broadcast_to(row, (TILE, 2 * L))
    return pltpu.roll(wide, 2 * L - (TILE - 1), 1, stride=1, stride_axis=0)


def bounded(q, k, table, size, heads):
    rows = lax.broadcasted_iota(jnp.int32, (q.shape[1], W), 0) // size
    cols = lax.broadcasted_iota(jnp.int32, (q.shape[1], W), 1)
    pick = ((rows == cols) & (rows < heads)).astype(BF16)
    qn = jnp.max(dot(q * q, pick), axis=0, keepdims=True)
    kn = jnp.max(dot(k * k, pick), axis=0, keepdims=True)
    top = jnp.max(jnp.sqrt(qn) * jnp.sqrt(kn)) * 1.02
    return top + jnp.max(jnp.abs(table)) < LIMIT


def start_all(pairs, sems):
    copies = [pltpu.make_async_copy(src, dst, sems.at[n]) for n, (src, dst) in enumerate(pairs)]
    for copy in copies:
        copy.start()
    return copies


def backbone_kernel(
    lengths_ref, assign_ref, rel_hbm, bucket_hbm, x_hbm, gain1_hbm, wq_hbm, wk_hbm, wv_hbm, wo_hbm, gain2_hbm, w1_hbm,
    w2_hbm, wd_hbm,
    hidden_ref, taps_ref,
    rel, buckets, x_ref, gain1_ref, wq, wk, wv, wo, gain2_ref, w1, w2, wd, sems,
    normed, q_s, k_s, vx, ctx, table, stream, inner,
):
    pairs = (
        (x_hbm, x_ref), (gain1_hbm, gain1_ref.at[0]), (rel_hbm, rel), (bucket_hbm, buckets.at[0]),
        (wq_hbm, wq), (wk_hbm, wk), (wv_hbm, wv), (wo_hbm, wo), (gain2_hbm, gain2_ref.at[0]),
        (w1_hbm, w1), (w2_hbm, w2), (wd_hbm, wd),
    )
    copies = [pltpu.make_async_copy(src, dst, sems.at[n]) for n, (src, dst) in enumerate(pairs)]
    for n in (2, 3, 0, 1, 4):
        copies[n].start()
    length = lengths_ref[assign_ref[lax.axis_index("side")]]
    copies[2].wait()
    copies[3].wait()
    table[...] = jnp.zeros_like(table)
    table[:H] = offset_table(buckets[...], rel[...])
    copies[0].wait()
    copies[1].wait()
    for n in (5, 6):
        copies[n].start()
    x = x_ref[...].astype(F32)
    scale = lax.rsqrt(jnp.mean(x * x, axis=1, keepdims=True) + EPS)
    normed[...] = (x * scale * gain1_ref[...]).astype(BF16)
    copies[4].wait()
    copies[7].start()
    q_s[...] = dot(normed[...], wq[...]).astype(BF16)
    copies[5].wait()
    k_s[...] = dot(normed[...], wk[...]).astype(BF16)
    copies[6].wait()
    for n in (8, 9, 10, 11):
        copies[n].start()
    live_row = lax.broadcasted_iota(jnp.int32, (L, 1), 0) < length
    value = dot(normed[...], wv[...])
    value = jnp.where(live_row, value, 0.0).astype(BF16)
    ones = jnp.where(live_row, 1.0, 0.0).astype(BF16)
    for pair in range(H // 2):
        vx[pair, :, :W] = value[:, pair * W : (pair + 1) * W]
        vx[pair, :, W:] = jnp.broadcast_to(ones, (L, W))
    low_half = lax.broadcasted_iota(jnp.int32, (L, W), 1) < HD
    low_row = lax.broadcasted_iota(jnp.int32, (TILE, W), 1) < HD
    live = lax.broadcasted_iota(jnp.int32, (1, L), 1) < length

    def attend(pair, stable):
        lanes = pl.ds(pl.multiple_of(pair * W, W), W)
        keys = k_s[:, lanes]
        tiles = [toeplitz(table[pl.ds(pair * 2 + half, 1)]) for half in range(2)]
        for block in range(L // TILE):
            rows = slice(block * TILE, (block + 1) * TILE)
            start = (L // TILE - 1 - block) * TILE
            query = q_s[rows, lanes]
            results = []
            for half in range(2):
                mine = low_row if half == 0 else jnp.logical_not(low_row)
                scores = dot_nt(jnp.where(mine, query, jnp.zeros_like(query)), keys)
                scores = scores + tiles[half][:, start : start + L]
                if stable:
                    scores = jnp.where(live, scores, MASKED)
                    scores = scores - jnp.max(scores, axis=1, keepdims=True)
                results.append(dot(jnp.exp(scores).astype(BF16), vx[pair]))
            top = jnp.where(low_row, results[0][:, :W], results[1][:, :W])
            total = jnp.where(low_row, results[0][:, W:], results[1][:, W:])
            ctx[rows, lanes] = (top / total).astype(BF16)

    safe = bounded(q_s[...], k_s[...], table[...], HD, H)

    @pl.when(safe)
    def _():
        @pl.loop(0, H // 2, step=PAIRS)
        def _(first):
            for n in range(PAIRS):
                attend(first + n, False)

    @pl.when(jnp.logical_not(safe))
    def _():
        @pl.loop(0, H // 2)
        def _(pair):
            attend(pair, True)

    copies[7].wait()
    copies[8].wait()
    flow = x_ref[...].astype(F32) + dot(ctx[...], wo[...])
    stream[...] = flow
    scale = lax.rsqrt(jnp.mean(flow * flow, axis=1, keepdims=True) + EPS)
    normed[...] = (flow * scale * gain2_ref[...]).astype(BF16)
    copies[9].wait()
    copies[10].wait()
    for r in range(L // 256):
        part = slice(r * 256, (r + 1) * 256)
        for n in range(FF // 3072):
            cols = slice(n * 3072, (n + 1) * 3072)
            pre = dot(normed[part], w1[:, cols])
            inner[part, cols] = (pre * normal_cdf(pre)).astype(BF16)
        hidden_ref[part] = (stream[part] + dot(inner[part], w2[...])).astype(BF16)
    copies[11].wait()
    taps_ref[...] = dot_nt(wd[...], hidden_ref[...]).astype(BF16)


def backbone(*args):
    smem = pl.BlockSpec(memory_space=pltpu.SMEM)
    vmem = pl.BlockSpec(memory_space=pltpu.VMEM)
    hbm = pl.BlockSpec(memory_space=pl.ANY)
    fixed = pl.BlockSpec(memory_space=pltpu.HBM)
    return pl.pallas_call(
        backbone_kernel,
        out_shape=(
            pltpu.VMEM((L, D), BF16),
            pltpu.VMEM((DS, L), BF16),
        ),
        in_specs=[smem, smem] + [fixed] * 12,
        out_specs=(vmem, vmem),
        scratch_shapes=[
            pltpu.VMEM((H, NB), F32),
            pltpu.VMEM((1, OFFSETS), jnp.int32),
            pltpu.VMEM((L, D), BF16),
            pltpu.VMEM((1, D), F32),
            pltpu.VMEM((D, D), BF16),
            pltpu.VMEM((D, D), BF16),
            pltpu.VMEM((D, D), BF16),
            pltpu.VMEM((D, D), BF16),
            pltpu.VMEM((1, D), F32),
            pltpu.VMEM((D, FF), BF16),
            pltpu.VMEM((FF, D), BF16),
            pltpu.VMEM((DS, D), BF16),
            pltpu.SemaphoreType.DMA((12,)),
            pltpu.VMEM((L, D), BF16),
            pltpu.VMEM((L, D), BF16),
            pltpu.VMEM((L, D), BF16),
            pltpu.VMEM((H // 2, L, 2 * W), BF16),
            pltpu.VMEM((L, D), BF16),
            pltpu.VMEM((16, 2 * L), F32),
            pltpu.VMEM((L, D), F32),
            pltpu.VMEM((L, FF), BF16),
        ],
        compiler_params=pltpu.CompilerParams(vmem_limit_bytes=60 * 1024 * 1024),
        cost_estimate=pl.CostEstimate(
            flops=9_000_000_000, bytes_accessed=17_000_000, transcendentals=5_000_000
        ),
        name="backbone",
    )(*args)


DOWN0, QKV0, PROJ0, FFIN0, FFOUT0 = 0, 576, 864, 960, 1248
PACK = 1536
PART = PACK // 4


def place():
    index = lax.axis_index("dp")
    return lax.rem(index, 2), lax.rem(lax.div(index, 2), 2)


def column_norm(rows):
    return lax.rsqrt(jnp.mean(rows * rows, axis=0, keepdims=True) + EPS)


def norm_back(grad, unit, scale):
    return scale * (grad - unit * jnp.mean(grad * unit, axis=0, keepdims=True))


def head_sums(rows):
    return jnp.sum(rows.reshape(SH, SHD, L), axis=1)


def fill_heads(ref, rows, extra):
    for head in range(SH):
        mine = rows[head * SHD : (head + 1) * SHD]
        other = extra[head] if isinstance(extra, list) else extra
        ref[head] = jnp.concatenate([mine, other], axis=0).astype(BF16)


def side_kernel(count, lengths_ref, assign_ref, *rest):
    moved_refs, rest = rest[:count], rest[count:]
    (
        taps, gate_hbm, gain1_hbm, gain2_hbm, wq, wk, wv, bucket_hbm, rel, wo, w1, w2,
        out_ref, gstate_ref, tap_ref, rest_ref,
        vectors, buckets, moved, sems, table, probs, qt, kt, vt, dt, ctx, sums, dq, dk, dv, dall, diag, dtab,
    ) = rest
    rank = lax.axis_index("side")
    seq = assign_ref[rank]
    pairs = (
        (bucket_hbm, buckets.at[0]), (gate_hbm, vectors.at[0]), (gain1_hbm, vectors.at[1]),
        (gain2_hbm, vectors.at[2]),
    )
    vectors[...] = jnp.zeros_like(vectors)
    copies = start_all(pairs, sems)
    for step in range(count):

        @pl.when(lax.rem(rank + count - seq, count) == step)
        def _():
            moved[...] = moved_refs[step][...]

    length = lengths_ref[seq]
    row8 = lax.broadcasted_iota(jnp.int32, (SHD, L), 0)
    lane8 = lax.broadcasted_iota(jnp.int32, (SHD, L), 1)
    for copy in copies:
        copy.wait()
    table[...] = jnp.zeros_like(table)
    table[:SH] = offset_table(buckets[...], rel[...])
    eye = lax.broadcasted_iota(jnp.int32, (DS, DS), 0) == lax.broadcasted_iota(
        jnp.int32, (DS, DS), 1
    )
    columns = dot(eye.astype(F32), vectors[...], ((1,), (1,)), lax.Precision.HIGHEST)
    gate = jax.nn.sigmoid(columns[:, 0:1])
    gain1, gain2 = columns[:, 1:2], columns[:, 2:3]
    tap = taps[...].astype(F32)
    old = moved[0].astype(F32)
    mixed = gate * tap + (1.0 - gate) * old
    scale1 = column_norm(mixed)
    unit1 = mixed * scale1
    normed1 = (unit1 * gain1).astype(BF16)
    query = dot_tn(wq[...], normed1).astype(BF16).astype(F32)
    key = dot_tn(wk[...], normed1).astype(BF16).astype(F32)
    value = dot_tn(wv[...], normed1)
    fill_heads(qt, query, jnp.where(row8 == 0, 1.0, 0.0))
    fill_heads(kt, key, jnp.where((row8 == 0) & (lane8 >= length), MASKED, 0.0))
    fill_heads(vt, value, jnp.where(row8 < 2, 1.0, 0.0))
    top = jnp.max(head_sums(query * query), axis=1) * jnp.max(head_sums(key * key), axis=1)
    safe = jnp.sqrt(jnp.max(top)) + jnp.max(jnp.abs(table[...])) < LIMIT
    blocks = [slice(b * TILE, (b + 1) * TILE) for b in range(L // TILE)]

    def rows8(head):
        return pl.ds(pl.multiple_of(head * SHD, SHD), SHD)

    def attend(head, stable):
        tile = toeplitz(table[pl.ds(head, 1)])
        for block, rows in enumerate(blocks):
            start = (L // TILE - 1 - block) * TILE
            scores = dot_tn(qt[head, :, rows], kt[head]) + tile[:, start : start + L]
            if stable:
                scores = scores - jnp.max(scores, axis=1, keepdims=True)
            probs[head, rows] = jnp.exp(scores).astype(BF16)
        both = dot_nt(vt[head], probs[head])
        ctx[rows8(head)] = both[:SHD]
        sums[rows8(head)] = jnp.broadcast_to(both[SHD : SHD + 1], (SHD, L))

    @pl.when(safe)
    def _():
        @pl.loop(0, SH, step=UNROLL)
        def _(first):
            for n in range(UNROLL):
                attend(first + n, False)

    @pl.when(jnp.logical_not(safe))
    def _():
        @pl.loop(0, SH)
        def _(head):
            attend(head, True)

    inverse = 1.0 / sums[...]
    context = ctx[...] * inverse
    context16 = context.astype(BF16)
    residual = mixed + dot_tn(wo[...], context16)
    scale2 = column_norm(residual)
    unit2 = residual * scale2
    normed2 = (unit2 * gain2).astype(BF16)
    pre = dot_tn(w1[...], normed2)
    cdf = normal_cdf(pre)
    inner = (pre * cdf).astype(BF16)
    out_ref[...] = (residual + dot(w2[...], inner)).astype(BF16)

    cotangent = moved[1]
    slope = cdf + pre * (jnp.exp(-0.5 * pre * pre) * (1.0 / math.sqrt(2.0 * math.pi)))
    d_pre = (dot_tn(w2[...], cotangent) * slope).astype(BF16)
    g_ffout = dot_nt(cotangent, inner)
    g_ffin = dot_nt(normed2, d_pre)
    for n in range(FS // W):
        for first, grad in ((FFIN0, g_ffin), (FFOUT0, g_ffout)):
            start = first - QKV0 + n * DS
            rest_ref[start : start + DS] = grad[:, n * W : (n + 1) * W].astype(BF16)
    dy = dot(w1[...], d_pre)
    g_gain2 = jnp.sum(dy * unit2, axis=1, keepdims=True)
    d_resid = cotangent.astype(F32) + norm_back(dy * gain2, unit2, scale2)
    d_attn = d_resid.astype(BF16)
    pad = jnp.zeros((W - DS, L), BF16)
    g_project = dot_nt(context16, jnp.concatenate([d_attn, pad], axis=0))
    d_context = dot(wo[...], d_attn).astype(BF16)
    d_scaled = (d_context.astype(F32) * inverse).astype(BF16).astype(F32)
    delta = head_sums(d_scaled * context)
    delta_hi = delta.astype(BF16).astype(F32)
    extra = []
    for head in range(SH):
        high, low = delta_hi[head : head + 1], (delta - delta_hi)[head : head + 1]
        extra.append(jnp.where(row8 == 0, -high, jnp.where(row8 == 1, -low, 0.0)))
    fill_heads(dt, d_scaled, extra)
    dtab[...] = jnp.zeros_like(dtab)

    def attend_back(head, spot):
        for block, rows in enumerate(blocks):
            grads = dot_tn(dt[head, :, rows], vt[head])
            dall[spot, rows] = (probs[head, rows].astype(F32) * grads).astype(BF16)
        dk[rows8(head)] = dot(qt[head], dall[spot])[:SHD]
        dv[rows8(head)] = dot(dt[head], probs[head])[:SHD]
        dq[rows8(head)] = dot_nt(kt[head], dall[spot])[:SHD]
        tiles = []
        for offset in range(2 * (L // TILE) - 1):
            total_tile = None
            for block, rows in enumerate(blocks):
                n = offset + block - (L // TILE - 1)
                if 0 <= n < L // TILE:
                    piece = dall[spot, rows, n * TILE : (n + 1) * TILE].astype(F32)
                    total_tile = piece if total_tile is None else total_tile + piece
            diag[spot, :, offset * TILE : (offset + 1) * TILE] = total_tile
        diag[spot, :, 2 * L - TILE :] = jnp.zeros((TILE, TILE), F32)
        back = 7 - lax.broadcasted_iota(jnp.int32, (8, 2 * L), 0)
        groups = [
            jnp.take_along_axis(diag[spot, g * 8 : g * 8 + 8], back, axis=0)
            for g in reversed(range(TILE // 8))
        ]
        rolled = pltpu.roll(jnp.concatenate(groups, axis=0), 0, 1, stride=1, stride_axis=0)
        dtab[pl.ds(head, 1)] = jnp.sum(rolled, axis=0, keepdims=True)

    @pl.loop(0, SH, step=UNROLL_BACK)
    def _(first):
        for n in range(UNROLL_BACK):
            attend_back(first + n, n)


    spots = lax.broadcasted_iota(jnp.int32, (W, OFFSETS), 0) - DS
    onehot = (spots == buckets[...]).astype(F32)
    g_rel = dot(dtab[:, :OFFSETS], onehot, ((1,), (1,)), lax.Precision.HIGHEST)
    grads = [ref[...].astype(BF16) for ref in (dq, dk, dv)]
    for n, grad in enumerate(grads):
        full = dot_nt(normed1, jnp.concatenate([grad, pad], axis=0))
        if n == 0:
            full = full + jnp.concatenate([g_rel, jnp.zeros((DS - 16, W), F32)], axis=0)
        rest_ref[n * DS : (n + 1) * DS] = full.astype(BF16)
    d_normed = dot(wq[...], grads[0]) + dot(wk[...], grads[1]) + dot(wv[...], grads[2])
    d_mixed = d_resid + norm_back(d_normed * gain1, unit1, scale1)
    gstate_ref[...] = ((1.0 - gate) * d_mixed).astype(BF16)
    tap_ref[...] = (gate * d_mixed).astype(BF16)
    g_gate = gate * (1.0 - gate) * jnp.sum(d_mixed * (tap - old), axis=1, keepdims=True)
    g_gain1 = jnp.sum(d_normed * unit1, axis=1, keepdims=True)
    lane = lax.broadcasted_iota(jnp.int32, (DS, W), 1)
    for n, grad in enumerate((g_gate, g_gain1, g_gain2)):
        g_project = jnp.where(lane == DS + n, grad, g_project)
    rest_ref[PROJ0 - QKV0 : PROJ0 - QKV0 + DS] = g_project.astype(BF16)


def pack_kernel(tap_ref, rest_ref, hidden_ref, keep_ref, send_ref, pack):
    down = dot(tap_ref[...], hidden_ref[...])
    for n in range(D // W):
        pack[n * DS : (n + 1) * DS] = down[:, n * W : (n + 1) * W].astype(BF16)
    pack[QKV0:] = rest_ref[...]
    core, across = place()
    for n in range(2):
        for ref, half in ((keep_ref, core), (send_ref, 1 - core)):
            start = (half * 2 + (across if n == 0 else 1 - across)) * PART
            ref[n] = pack[pl.ds(pl.multiple_of(start, PART), PART)]


def pack_grads(tap, rest, hidden):
    vmem = pl.BlockSpec(memory_space=pltpu.VMEM)
    return pl.pallas_call(
        pack_kernel,
        out_shape=(jax.ShapeDtypeStruct((2, PART, W), BF16),) * 2,
        in_specs=[vmem] * 3,
        out_specs=(vmem,) * 2,
        scratch_shapes=[pltpu.VMEM((PACK, W), BF16)],
        compiler_params=pltpu.CompilerParams(vmem_limit_bytes=8 * 1024 * 1024),
        cost_estimate=pl.CostEstimate(
            flops=80_000_000, bytes_accessed=2_000_000, transcendentals=0
        ),
        name="pack_grads",
    )(tap, rest, hidden)


def side_block(lengths, assign, moved, *args):
    smem = pl.BlockSpec(memory_space=pltpu.SMEM)
    vmem = pl.BlockSpec(memory_space=pltpu.VMEM)
    hbm = pl.BlockSpec(memory_space=pl.ANY)
    count = len(moved)
    return pl.pallas_call(
        functools.partial(side_kernel, count),
        out_shape=(
            pltpu.VMEM((DS, L), BF16),
            pltpu.VMEM((DS, L), BF16),
            pltpu.VMEM((DS, L), BF16),
            pltpu.VMEM((PACK - QKV0, W), BF16),
        ),
        in_specs=[smem, smem] + [vmem] * count + [hbm if a.ndim == 1 else vmem for a in args],
        out_specs=(vmem,) * 4,
        scratch_shapes=[
            pltpu.VMEM((8, DS), F32),
            pltpu.VMEM((1, OFFSETS), jnp.int32),
            pltpu.VMEM((2, DS, L), BF16),
            pltpu.SemaphoreType.DMA((4,)),
            pltpu.VMEM((16, 2 * L), F32),
            pltpu.VMEM((SH, L, L), BF16),
            pltpu.VMEM((SH, 2 * SHD, L), BF16),
            pltpu.VMEM((SH, 2 * SHD, L), BF16),
            pltpu.VMEM((SH, 2 * SHD, L), BF16),
            pltpu.VMEM((SH, 2 * SHD, L), BF16),
            pltpu.VMEM((DS, L), F32),
            pltpu.VMEM((DS, L), F32),
            pltpu.VMEM((DS, L), F32),
            pltpu.VMEM((DS, L), F32),
            pltpu.VMEM((DS, L), F32),
            pltpu.VMEM((UNROLL_BACK, L, L), BF16),
            pltpu.VMEM((UNROLL_BACK, TILE, 2 * L), F32),
            pltpu.VMEM((16, 2 * L), F32),
        ],
        compiler_params=pltpu.CompilerParams(vmem_limit_bytes=VMEM_BYTES),
        cost_estimate=pl.CostEstimate(
            flops=9_000_000_000, bytes_accessed=4_000_000, transcendentals=5_000_000
        ),
        name="side_block",
    )(lengths, assign, *moved, *args)


def finish_kernel(count, assign_ref, *rest):
    quarters, rest = rest[:4], rest[4:]
    outs, gstates, results = rest[:count], rest[count : 2 * count], rest[2 * count : 2 * count + 13]
    part, out, *parts, sems = rest[2 * count + 13 :]
    rank = lax.axis_index("side")
    core, across = place()
    spots = [
        2 * half + quarter for half in (core, 1 - core) for quarter in (across, 1 - across)
    ]
    masks = [0]
    for n in reversed(range(16)):
        if 1 << n < count:
            masks += [mask ^ (1 << n) for mask in masks]
    slot = jnp.int32(0)
    for n in range(count):
        slot = jnp.where(assign_ref[n] == rank, n, slot)
    gstate, down, gate, gain1, gq, gk, gv, go, rel, gain2, g1, g2 = parts
    for step in range(count):

        @pl.when((rank ^ slot) == masks[step])
        def _():
            out[...] = outs[step][...]
            gstate[...] = gstates[step][...].astype(F32)

    targets = [out, *parts]
    pairs = [
        (ref.at[0] if ref.shape[0] == 1 else ref, result)
        for ref, result in zip(targets, results, strict=True)
    ]
    copies = [pltpu.make_async_copy(src, dst, sems.at[n]) for n, (src, dst) in enumerate(pairs)]
    copies[0].start()
    copies[1].start()
    for ref, spot in zip(quarters, spots, strict=True):
        part[spot] = ref[...]

    def take(start, stop):
        pieces = []
        for n in range(4):
            low, high = max(start, n * PART), min(stop, (n + 1) * PART)
            if low < high:
                pieces.append(part[n, low - n * PART : high - n * PART].astype(F32))
        return pieces[0] if len(pieces) == 1 else jnp.concatenate(pieces, axis=0)

    for n in range(D // W):
        down[:, n * W : (n + 1) * W] = take(DOWN0 + n * DS, DOWN0 + (n + 1) * DS)
    copies[2].start()
    for n in range(FS // W):
        g1[:, n * W : (n + 1) * W] = take(FFIN0 + n * DS, FFIN0 + (n + 1) * DS)
        g2[:, n * W : (n + 1) * W] = take(FFOUT0 + n * DS, FFOUT0 + (n + 1) * DS)
    copies[11].start()
    copies[12].start()
    for n, ref in enumerate((gq, gk, gv)):
        ref[...] = take(QKV0 + n * DS, QKV0 + (n + 1) * DS)[:, :DS]
        copies[5 + n].start()
    rel[...] = take(QKV0, QKV0 + 16)[:SH, DS : DS + NB]
    project = take(PROJ0, PROJ0 + DS)
    go[...] = project[:, :DS]
    copies[8].start()
    copies[9].start()
    turned = project.T
    gate[...] = turned[DS : DS + 1]
    gain1[...] = turned[DS + 1 : DS + 2]
    gain2[...] = turned[DS + 2 : DS + 3]
    for n in (3, 4, 10):
        copies[n].start()
    for copy in copies:
        copy.wait()


def finish(assign, quarters, outs, gstates):
    smem = pl.BlockSpec(memory_space=pltpu.SMEM)
    vmem = pl.BlockSpec(memory_space=pltpu.VMEM)
    hbm = pl.BlockSpec(memory_space=pl.ANY)
    fixed = pl.BlockSpec(memory_space=pltpu.HBM)
    count = len(outs)
    parts = [
        (DS, L), (DS, D), (1, DS), (1, DS), (DS, DS), (DS, DS), (DS, DS), (DS, DS), (SH, NB), (1, DS), (DS, FS), (DS, FS),
    ]
    shapes = [jax.ShapeDtypeStruct(p[1:] if p[0] == 1 else p, F32) for p in parts]
    return pl.pallas_call(
        functools.partial(finish_kernel, count),
        out_shape=(jax.ShapeDtypeStruct((DS, L), BF16), *shapes),
        in_specs=[smem] + [vmem] * (4 + 2 * count),
        out_specs=(hbm,) * 13,
        scratch_shapes=[
            pltpu.VMEM((4, PART, W), BF16),
            pltpu.VMEM((DS, L), BF16),
            *[pltpu.VMEM(p, F32) for p in parts],
            pltpu.SemaphoreType.DMA((13,)),
        ],
        compiler_params=pltpu.CompilerParams(vmem_limit_bytes=16 * 1024 * 1024),
        name="finish",
    )(assign, *quarters, *outs, *gstates)


def swap(value, axis, bit):
    size = lax.axis_size(axis)
    return lax.ppermute(value, axis, [(i, i ^ bit) for i in range(size)])


def rotations(value):
    size = lax.axis_size("side")
    return [value] + [
        lax.ppermute(value, "side", [(i, (i + k) % size) for i in range(size)])
        for k in range(1, size)
    ]


def add(one, two):
    return (one.astype(F32) + two.astype(F32)).astype(BF16)


def bits(axis, first=0):
    return [1 << n for n in range(first, 16) if 1 << n < lax.axis_size(axis)]


def spread(blocks, bit):
    return blocks + [swap(block, "side", bit) for block in blocks]


def settle_kernel(_, out_ref):
    del out_ref


def settle(block):
    hbm = pl.BlockSpec(memory_space=pl.ANY)
    return pl.pallas_call(
        settle_kernel,
        out_shape=jax.ShapeDtypeStruct(block.shape, block.dtype),
        in_specs=[hbm],
        out_specs=hbm,
        input_output_aliases={0: 0},
        cost_estimate=pl.CostEstimate(flops=1000000000, bytes_accessed=0, transcendentals=0),
        compiler_params=pltpu.CompilerParams(vmem_limit_bytes=1024 * 1024),
        name="settle",
    )(block)


def hold(value, blocks):
    return lax.optimization_barrier((value, [settle(block) for block in blocks]))


def total(keep, send, out, gstate):
    levels = bits("side")[::-1]
    outs, gstates = spread([out], levels[0]), spread([gstate], levels[0])
    got = swap(send, "dp", 1)
    mine = add(keep[0], got[0])
    across = swap(add(keep[1], got[1]), "dp", 2)
    mine = add(mine, across)
    mine = add(mine, swap(mine, "side", 1))
    mine, outs[1:] = hold(mine, outs[1:])
    for bit in bits("dp", 2):
        mine = add(mine, swap(mine, "dp", bit))
    mine, gstates[1:] = hold(mine, gstates[1:])
    for bit in levels[1:]:
        outs, gstates = spread(outs, bit), spread(gstates, bit)
    for bit in bits("side", 1):
        mine = add(mine, swap(mine, "side", bit))
    if len(levels) > 1:
        own = len(outs) // 2
        mine, outs[own:], gstates[own : own + 1] = lax.optimization_barrier(
            (mine, [settle(b) for b in outs[own:]], [settle(gstates[own])])
        )
    across = swap(mine, "dp", 2)
    return (mine, across, swap(mine, "dp", 1), swap(across, "dp", 1)), outs, gstates


def shards(
    hidden_in, side_state, lengths, assign, buckets,
    backbone_gain_attn, backbone_query, backbone_key, backbone_value, backbone_project, backbone_rel,
    backbone_gain_ff, backbone_ff_in, backbone_ff_out, down_weight, gate_logit,
    side_gain_attn, side_query, side_key, side_value, side_project, side_rel,
    side_gain_ff, side_ff_in, side_ff_out, cotangent,
):
    moved = rotations(jnp.stack([side_state[0].T, cotangent[0].T]))
    hidden, taps = backbone(
        lengths, assign, backbone_rel.T, buckets, hidden_in[0], backbone_gain_attn,
        backbone_query, backbone_key, backbone_value, backbone_project, backbone_gain_ff,
        backbone_ff_in, backbone_ff_out, down_weight.T,
    )
    out, gstate, tap, rest = side_block(
        lengths, assign, moved, taps, gate_logit, side_gain_attn, side_gain_ff,
        side_query, side_key, side_value, buckets, side_rel.T, side_project, side_ff_in, side_ff_out.T,
    )
    keep, send = pack_grads(tap, rest, hidden)
    quarters, outs, gstates = total(keep, send, out, gstate)
    res = finish(assign, quarters, outs, gstates)
    out, gstate, down, gate, gain1, gq, gk, gv, go, rel, gain2, g1, g2 = res
    return (
        out.T[None], gstate.T[None], down.T, gate, gain1, gq, gk, gv, go, rel.T, gain2, g1, g2.T,
    )


def solution(mesh):
    rows = P(("dp", "side"), None, None)
    return jax.shard_map(
        shards,
        mesh=mesh,
        in_specs=(rows, rows, P("dp"), P("dp")) + (P(),) * 21 + (rows,),
        out_specs=(rows, rows) + (P(),) * 11,
        check_vma=False,
    )
```
